32 devices in a mesh: dp: 2 (over core), seq: 8 (over z, x), chan: 2 (over y).
Axes of the slice: x: 2, y: 2, z: 4, core: 2. Of those that a mesh axis runs over, the one named last changes fastest.
Arguments:
- inputs: float32 [16, 1024, 1024], P('dp', 'seq', 'chan'), may hold values from -6 to 6
- cotangent: float32 [16, 1024, 1024], P('dp', 'seq', 'chan'), may hold values from -6 to 6
- norm1_gain: float32 [1024], P('chan'), may hold values from 0.1 to 1.9
- norm1_bias: float32 [1024], P('chan'), may hold values from -3 to 3
- log_step: float32 [1024], P('chan'), may hold values from -6.9 to -2.3
- decay_log: float32 [1024, 32], P('chan'), may hold values from -4.6 to 0
- freq: float32 [1024, 32], P('chan'), may hold values from 0 to 8
- out_coef: float32 [2, 1024, 32], P(None, 'chan'), may hold values from -2 to 2
- skip: float32 [1024], P('chan'), may hold values from -4 to 4
- glu_weight: float32 [1024, 2, 1024], P(None, None, 'chan'), may hold values from -0.1875 to 0.1875
- glu_bias: float32 [2, 1024], P(None, 'chan'), may hold values from -3 to 3
- norm2_gain: float32 [1024], P('chan'), may hold values from 0.1 to 1.9
- norm2_bias: float32 [1024], P('chan'), may hold values from -3 to 3
- ffn_in: float32 [1024, 4096], P(None, 'chan'), may hold values from -0.1875 to 0.1875
- ffn_in_bias: float32 [4096], P('chan'), may hold values from -3 to 3
- ffn_out: float32 [4096, 1024], P('chan'), may hold values from -0.09375 to 0.09375
- ffn_out_bias: float32 [1024], P('chan'), may hold values from -3 to 3
Outputs:
- output: float32 [16, 1024, 1024], P('dp', 'seq', 'chan')
- grad_inputs: float32 [16, 1024, 1024], P('dp', 'seq', 'chan')
- grad_norm1_gain: float32 [1024], P('chan')
- grad_norm1_bias: float32 [1024], P('chan')
- grad_log_step: float32 [1024], P('chan')
- grad_decay_log: float32 [1024, 32], P('chan')
- grad_freq: float32 [1024, 32], P('chan')
- grad_out_coef: float32 [2, 1024, 32], P(None, 'chan')
- grad_skip: float32 [1024], P('chan')
- grad_glu_weight: float32 [1024, 2, 1024], P(('dp', 'seq'), None, 'chan')
- grad_glu_bias: float32 [2, 1024], P(None, 'chan')
- grad_norm2_gain: float32 [1024], P('chan')
- grad_norm2_bias: float32 [1024], P('chan')
- grad_ffn_in: float32 [1024, 4096], P(('dp', 'seq'), 'chan')
- grad_ffn_in_bias: float32 [4096], P('chan')
- grad_ffn_out: float32 [4096, 1024], P('chan', ('dp', 'seq'))
- grad_ffn_out_bias: float32 [1024], P('chan')
The draws below stay inside these ranges and needn't reach their ends.
All inputs are finite; a program needn't handle non-finite values.
Results may differ from the reference program's by a relative error of at most 0.0003.
Values sent between devices are 32-bit elements; how exact they have to be, the bound alone decides.
No kernel may reach another device: no remote copies, remote signals or barrier semaphores. Data moves between devices by JAX's collectives and lax.ppermute only.
A program may use at most 256 MiB of HBM per device.

```python
import jax
import jax.numpy as jnp
from jax import lax

D = 1024
FF = 4096
MODES = 32
ROWS = 128
LEN = 1024
CONTEXTS = 16


def shard_levels(own_key, dims, shards, low, high):
    level, own = 1.0, jax.random.fold_in(own_key, 6)
    for dim, blocks in shards:
        steps = jnp.exp(jax.random.uniform(jax.random.fold_in(own, dim), (blocks,), jnp.float32, low / len(shards), high / len(shards)))
        level = level * jnp.repeat(steps, dims[dim] // blocks).reshape([-1 if axis == dim else 1 for axis in range(len(dims))])
    return level


def scatter_about(rng, shape, spread, most, pieces=(), kind=jnp.bfloat16):
    loudness = shard_levels(rng, shape, pieces, -0.22, 0.18) if pieces else 1.0
    entries = jax.random.normal(rng, shape, jnp.float32) * spread * loudness
    return jnp.minimum(jnp.maximum(entries, -most), most).astype(kind)


def setup_inputs(seed: int = 0) -> dict:
    keys = jax.random.split(jax.random.key(seed), 18)
    inputs = scatter_about(keys[0], (CONTEXTS, LEN, D), 1.0, 6.0, ((0, 2), (1, 8), (2, 2)), jnp.float32)
    cotangent = scatter_about(keys[1], (CONTEXTS, LEN, D), 1.0, 6.0, ((0, 2), (1, 8), (2, 2)), jnp.float32)
    norm1_gain = jnp.clip(1.0 + 0.18 * jax.random.normal(keys[2], (D,), jnp.float32), 0.1, 1.9)
    norm1_bias = scatter_about(keys[3], (D,), 0.5, 3.0, ((0, 2),), jnp.float32)
    log_step = jnp.clip(-6.9 + 4.6000001430511475 * jax.random.uniform(keys[4], (D,), jnp.float32) ** shard_levels(keys[4], (D,), ((0, 2),), -0.2, 0.2), -6.9, -2.3)
    decay_log = jnp.clip(-4.6 + 4.6 * jax.random.uniform(keys[5], (D, MODES), jnp.float32) ** shard_levels(keys[5], (D, MODES), ((0, 2),), -0.2, 0.2), -4.6, 0.0)
    freq = jnp.clip(8.0 * jax.random.uniform(keys[6], (D, MODES), jnp.float32) ** shard_levels(keys[6], (D, MODES), ((0, 2),), -0.2, 0.2), 0.0, 8.0)
    out_coef = scatter_about(keys[7], (2, D, MODES), 0.3, 2.0, ((1, 2),), jnp.float32)
    skip = scatter_about(keys[8], (D,), 1.0, 4.0, ((0, 2),), jnp.float32)
    glu_weight = scatter_about(keys[9], (D, 2, D), D ** -0.5, 0.1875, ((2, 2),), jnp.float32)
    glu_bias = scatter_about(keys[10], (2, D), 0.5, 3.0, ((1, 2),), jnp.float32)
    norm2_gain = jnp.clip(1.0 + 0.18 * jax.random.normal(keys[11], (D,), jnp.float32), 0.1, 1.9)
    norm2_bias = scatter_about(keys[12], (D,), 0.5, 3.0, ((0, 2),), jnp.float32)
    ffn_in = scatter_about(keys[13], (D, FF), D ** -0.5, 0.1875, ((1, 2),), jnp.float32)
    ffn_in_bias = scatter_about(keys[14], (FF,), 0.5, 3.0, ((0, 2),), jnp.float32)
    ffn_out = scatter_about(keys[15], (FF, D), FF ** -0.5, 0.09375, ((0, 2),), jnp.float32)
    ffn_out_bias = scatter_about(keys[16], (D,), 0.5, 3.0, ((0, 2),), jnp.float32)
    return {"inputs": inputs, "cotangent": cotangent, "norm1_gain": norm1_gain, "norm1_bias": norm1_bias, "log_step": log_step, "decay_log": decay_log, "freq": freq, "out_coef": out_coef, "skip": skip, "glu_weight": glu_weight, "glu_bias": glu_bias, "norm2_gain": norm2_gain, "norm2_bias": norm2_bias, "ffn_in": ffn_in, "ffn_in_bias": ffn_in_bias, "ffn_out": ffn_out, "ffn_out_bias": ffn_out_bias}


epsilon = 1e-05
highest = lax.Precision.HIGHEST

@jax.custom_vjp
def low(v):
    return lax.optimization_barrier(v.astype(jnp.bfloat16)).astype(jnp.float32)

@jax.custom_vjp
def low_back(v):
    return v

def low_keep(v):
    return (low(v), None)

def low_pass(kept, grad):
    return (grad,)

def back_keep(v):
    return (v, None)

def back_low(kept, grad):
    return (low(grad),)
low.defvjp(low_keep, low_pass)
low_back.defvjp(back_keep, back_low)

def product(left, right):
    return jnp.dot(left, right, precision=highest, preferred_element_type=jnp.float32)

def kernel_rows(positions, log_step, decay_log, freq, out_coef):
    step = jnp.exp(log_step)[:, None]
    real_rate = -jnp.exp(decay_log)
    scaled_real = step * real_rate
    scaled_imag = step * freq
    minus_real = jnp.expm1(scaled_real) * jnp.cos(scaled_imag) - 2.0 * jnp.sin(0.5 * scaled_imag) ** 2
    minus_imag = jnp.exp(scaled_real) * jnp.sin(scaled_imag)
    modulus = real_rate * real_rate + freq * freq
    ratio_real = (minus_real * real_rate + minus_imag * freq) / modulus
    ratio_imag = (minus_imag * real_rate - minus_real * freq) / modulus
    weight_real = out_coef[0] * ratio_real - out_coef[1] * ratio_imag
    weight_imag = out_coef[0] * ratio_imag + out_coef[1] * ratio_real
    where = positions[:, None, None]
    magnitude = jnp.exp(where * scaled_real)
    angle = where * scaled_imag
    return 2.0 * lax.optimization_barrier(jnp.sum(weight_real * magnitude * jnp.cos(angle) - weight_imag * magnitude * jnp.sin(angle), axis=2))

def layer_norm(values, gain, bias):
    mean = lax.optimization_barrier(jnp.mean(values, axis=-1, keepdims=True))
    centered = values - mean
    variance = lax.optimization_barrier(jnp.mean(centered * centered, axis=-1, keepdims=True))
    return centered * lax.rsqrt(variance + epsilon) * gain + bias

def forward(inputs, norm1_gain, norm1_bias, log_step, decay_log, freq, out_coef, skip, glu_weight, glu_bias, norm2_gain, norm2_bias, ffn_in, ffn_in_bias, ffn_out, ffn_out_bias):
    positions = jnp.arange(LEN).astype(jnp.float32).reshape(LEN // ROWS, ROWS)
    kernel = lax.map(jax.checkpoint(lambda block: kernel_rows(block, log_step, decay_log, freq, out_coef)), positions).reshape(LEN, D)
    length = 2 * LEN
    kernel_freq = jnp.fft.rfft(kernel, n=length, axis=0)

    def context(values):
        normed = layer_norm(values, norm1_gain, norm1_bias)
        conv = jnp.fft.irfft(jnp.fft.rfft(normed, n=length, axis=0) * kernel_freq, n=length, axis=0)[:LEN]
        mixed = jax.nn.gelu(conv + skip * normed, approximate=False)
        value = product(mixed, glu_weight[:, 0, :]) + glu_bias[0]
        gate = product(mixed, glu_weight[:, 1, :]) + glu_bias[1]
        resid = values + value * jax.nn.sigmoid(gate)
        normed2 = layer_norm(resid, norm2_gain, norm2_bias)
        hidden = jax.nn.gelu(product(normed2, ffn_in) + ffn_in_bias, approximate=False)
        return resid + product(hidden, ffn_out) + ffn_out_bias
    return lax.map(jax.checkpoint(context), inputs)

def reference(inputs, cotangent, norm1_gain, norm1_bias, log_step, decay_log, freq, out_coef, skip, glu_weight, glu_bias, norm2_gain, norm2_bias, ffn_in, ffn_in_bias, ffn_out, ffn_out_bias):
    output, pullback = jax.vjp(forward, inputs, norm1_gain, norm1_bias, log_step, decay_log, freq, out_coef, skip, glu_weight, glu_bias, norm2_gain, norm2_bias, ffn_in, ffn_in_bias, ffn_out, ffn_out_bias)
    grads = pullback(cotangent)
    return (output, grads[0], grads[1], grads[2], grads[3], grads[4], grads[5], grads[6], grads[7], grads[8], grads[9], grads[10], grads[11], grads[12], grads[13], grads[14], grads[15])
```

```python
from functools import partial

import jax
import jax.numpy as jnp
from jax import lax
from jax.experimental import pallas as pl
from jax.experimental.pallas import tpu as pltpu
from jax.sharding import PartitionSpec as P

epsilon = 1e-05
high = lax.Precision.HIGH
highest = lax.Precision.HIGHEST
swap = [(0, 1), (1, 0)]


def contract(left, right, left_dim, right_dim):
    return lax.dot_general(
        left,
        right,
        (((left_dim,), (right_dim,)), ((), ())),
        precision=high,
        preferred_element_type=jnp.float32,
    )


def state_modes(log_step, decay_log, freq, out_coef):
    step = jnp.exp(log_step)[:, None]
    real_rate = -jnp.exp(decay_log)
    scaled_real = step * real_rate
    scaled_imag = step * freq
    minus_real = (
        jnp.expm1(scaled_real) * jnp.cos(scaled_imag) - 2.0 * jnp.sin(0.5 * scaled_imag) ** 2
    )
    minus_imag = jnp.exp(scaled_real) * jnp.sin(scaled_imag)
    modulus = real_rate * real_rate + freq * freq
    ratio_real = (minus_real * real_rate + minus_imag * freq) / modulus
    ratio_imag = (minus_imag * real_rate - minus_real * freq) / modulus
    weight_real = out_coef[0] * ratio_real - out_coef[1] * ratio_imag
    weight_imag = out_coef[0] * ratio_imag + out_coef[1] * ratio_real
    return (weight_real, weight_imag, scaled_real, scaled_imag)


def powers(positions, scaled_real, scaled_imag):
    where = positions[None, None, :]
    magnitude = jnp.exp(where * scaled_real[:, :, None])
    angle = where * scaled_imag[:, :, None]
    return (magnitude * jnp.cos(angle), magnitude * jnp.sin(angle))


def toeplitz_pair(kernel_ref, channel, lag, before, keep):
    rows = kernel_ref.shape[2]
    out = []
    for step in range(2):
        line = kernel_ref[channel, pl.ds(lag + step, 1), :]
        now = pltpu.roll(jnp.broadcast_to(line, (rows, rows)), 0, 1, stride=1, stride_axis=0)
        out.append(jnp.where(keep, now, before))
        before = now
    return (jnp.concatenate(out, axis=1), before)


def conv_kernel(unit_ref, kernel_ref, table_ref, mixed_ref, slope_ref):
    groups, block, sequences, rows = unit_ref.shape
    count = groups * sequences
    row_at = lax.broadcasted_iota(jnp.int32, (rows, rows), 0)
    lane_at = lax.broadcasted_iota(jnp.int32, (rows, rows), 1)
    keep = lane_at >= row_at

    def one(channel, carry):
        unit = unit_ref[:, channel].reshape(count, rows)
        gain = table_ref[channel, 0:1, :]
        bias = table_ref[channel, 1:2, :]
        skip = table_ref[channel, 2:3, :]
        normed = unit * gain + bias
        before = jnp.zeros((rows, rows), jnp.float32)
        sums = [None] * groups
        for lag in range(0, groups, 2):
            table, before = toeplitz_pair(kernel_ref, channel, lag, before, keep)
            part = jnp.dot(
                normed, table, precision=high, preferred_element_type=jnp.float32
            )
            for step in range(2):
                for group in range(groups - lag - step):
                    piece = part[
                        group * sequences : (group + 1) * sequences,
                        step * rows : (step + 1) * rows,
                    ]
                    at = group + lag + step
                    sums[at] = piece if sums[at] is None else sums[at] + piece
        inner = jnp.concatenate(sums, axis=0) + skip * normed
        below = 0.5 * (1.0 + lax.erf(inner * 0.7071067811865476))
        density = 0.3989422804014327 * jnp.exp(-0.5 * inner * inner)
        mixed_ref[:, channel] = (inner * below).reshape(groups, sequences, rows)
        slope_ref[:, channel] = (below + inner * density).reshape(groups, sequences, rows)
        return carry

    lax.fori_loop(0, block, one, 0)


def conv_back_kernel(
    unit_ref, slope_ref, grad_ref, kernel_ref, table_ref, back_ref, lags_ref, sums_ref
):
    groups, block, sequences, rows = unit_ref.shape
    count = groups * sequences
    row_at = lax.broadcasted_iota(jnp.int32, (rows, rows), 0)
    lane_at = lax.broadcasted_iota(jnp.int32, (rows, rows), 1)
    keep = lane_at >= row_at
    line_at = lane_at[:8]
    tile_row = row_at[:8]

    def tiles(cross):
        out = [cross[:8]]
        for tile in range(1, rows // 8):
            out.append(pltpu.roll(cross[8 * tile : 8 * tile + 8], rows - 8 * tile, 1))
        return out

    def merge(first, second):
        out = first[0]
        for tile in range(1, rows // 8):
            out = out + jnp.where(line_at < rows - 8 * tile, first[tile], second[tile])
        for bit in (1, 2, 4):
            out = jnp.where(tile_row & bit != 0, pltpu.roll(out, rows - bit, 1), out)
        return out

    def one(channel, carry):
        unit = unit_ref[:, channel].reshape(count, rows)
        gain = table_ref[channel, 0:1, :]
        bias = table_ref[channel, 1:2, :]
        skip = table_ref[channel, 2:3, :]
        normed = unit * gain + bias
        grad = (grad_ref[:, channel] * slope_ref[:, channel]).reshape(count, rows)
        normed_t = normed.T
        before = jnp.zeros((rows, rows), jnp.float32)
        total = skip * grad
        held = None
        lines = []
        for lag in range(0, groups, 2):
            table, before = toeplitz_pair(kernel_ref, channel, lag, before, keep)
            for step in range(2):
                at = lag + step
                shift = at * sequences
                moved = grad[shift:]
                if at:
                    moved = jnp.concatenate(
                        [moved, jnp.zeros((shift, rows), jnp.float32)], axis=0
                    )
                total = total + lax.dot_general(
                    moved,
                    table[:, step * rows : (step + 1) * rows],
                    (((1,), (1,)), ((), ())),
                    precision=high,
                    preferred_element_type=jnp.float32,
                )
                cross = tiles(
                    jnp.dot(normed_t, moved, precision=high, preferred_element_type=jnp.float32)
                )
                if at:
                    lines.append(merge(held, cross))
                held = cross
        nothing = jnp.zeros((8, rows), jnp.float32)
        lines.append(merge(held, [nothing] * (rows // 8)))
        lines.append(nothing)
        for at in range(groups):
            line = jnp.where(line_at + tile_row < rows, lines[at], lines[at + 1])
            lags_ref[channel, at : at + 1, :] = jnp.sum(line, axis=0, keepdims=True)
        back_ref[:, channel] = (total * gain).reshape(groups, sequences, rows)
        sums_ref[channel, 0:1, :] = jnp.sum(total * unit, axis=0, keepdims=True)
        sums_ref[channel, 1:2, :] = jnp.sum(total, axis=0, keepdims=True)
        sums_ref[channel, 2:3, :] = jnp.sum(grad * normed, axis=0, keepdims=True)
        sums_ref[channel, 3:8, :] = jnp.zeros((5, rows), jnp.float32)
        return carry

    lax.fori_loop(0, block, one, 0)


def channel_blocks(part):
    return 8 if part % 8 == 0 else part


def long_conv(unit, kernel, table):
    groups, part, sequences, rows = unit.shape
    block = channel_blocks(part)
    wide = pl.BlockSpec((groups, block, sequences, rows), lambda i: (0, i, 0, 0))
    return pl.pallas_call(
        conv_kernel,
        grid=(part // block,),
        in_specs=[
            wide,
            pl.BlockSpec((block, groups, rows), lambda i: (i, 0, 0)),
            pl.BlockSpec((block, 8, rows), lambda i: (i, 0, 0)),
        ],
        out_specs=[wide, wide],
        out_shape=[jax.ShapeDtypeStruct(unit.shape, jnp.float32)] * 2,
        compiler_params=pltpu.CompilerParams(vmem_limit_bytes=48 * 1024 * 1024),
        name="conv_forward",
    )(unit, kernel, table)


def long_conv_back(unit, slope, grad, kernel, table):
    groups, part, sequences, rows = unit.shape
    block = channel_blocks(part)
    wide = pl.BlockSpec((groups, block, sequences, rows), lambda i: (0, i, 0, 0))
    lags = pl.BlockSpec((block, groups, rows), lambda i: (i, 0, 0))
    few = pl.BlockSpec((block, 8, rows), lambda i: (i, 0, 0))
    return pl.pallas_call(
        conv_back_kernel,
        grid=(part // block,),
        in_specs=[wide, wide, wide, lags, few],
        out_specs=[wide, lags, few],
        out_shape=[
            jax.ShapeDtypeStruct(unit.shape, jnp.float32),
            jax.ShapeDtypeStruct(kernel.shape, jnp.float32),
            jax.ShapeDtypeStruct((part, 8, rows), jnp.float32),
        ],
        compiler_params=pltpu.CompilerParams(vmem_limit_bytes=48 * 1024 * 1024),
        name="conv_backward",
    )(unit, slope, grad, kernel, table)


def body(
    inputs,
    cotangent,
    norm1_gain,
    norm1_bias,
    log_step,
    decay_log,
    freq,
    out_coef,
    skip,
    glu_weight,
    glu_bias,
    norm2_gain,
    norm2_bias,
    ffn_in,
    ffn_in_bias,
    ffn_out,
    ffn_out_bias,
):
    sequences, rows, channels = inputs.shape
    groups = lax.axis_size("seq")
    seq_index = lax.axis_index("seq")
    chan_index = lax.axis_index("chan")
    dp_index = lax.axis_index("dp")
    width = channels * lax.axis_size("chan")
    count = sequences * rows
    part = channels // groups
    hidden_count = ffn_in.shape[1]

    def to_chan(values):
        return lax.ppermute(values, "chan", swap)

    def spread(values):
        return lax.all_to_all(values, "seq", 0, 0, tiled=True)

    def own_part(values, dim):
        return lax.dynamic_slice_in_dim(values, seq_index * part, part, dim)

    own_at = chan_index * channels
    other_at = channels - own_at

    own_coef = own_part(out_coef, 1)
    modes, modes_back = jax.vjp(
        state_modes, own_part(log_step, 0), own_part(decay_log, 0), own_part(freq, 0), own_coef
    )
    weight_real, weight_imag, scaled_real, scaled_imag = modes
    fine_at = jnp.arange(rows, dtype=jnp.int32).astype(jnp.float32)
    coarse_at = (jnp.arange(groups, dtype=jnp.int32) * rows).astype(jnp.float32)
    fine_real, fine_imag = powers(fine_at, scaled_real, scaled_imag)
    coarse_real, coarse_imag = powers(coarse_at, scaled_real, scaled_imag)
    fine = jnp.concatenate([fine_real, fine_imag], axis=1)
    start_real = weight_real[:, :, None] * coarse_real - weight_imag[:, :, None] * coarse_imag
    start_imag = weight_real[:, :, None] * coarse_imag + weight_imag[:, :, None] * coarse_real
    kernel = 2.0 * jnp.einsum(
        "hnd,hnb->hdb",
        jnp.concatenate([start_real, -start_imag], axis=1),
        fine,
        precision=highest,
        preferred_element_type=jnp.float32,
    )
    table = jnp.stack(
        [own_part(norm1_gain, 0), own_part(norm1_bias, 0), own_part(skip, 0)]
        + [jnp.zeros((part,), jnp.float32)] * 5,
        axis=1,
    )
    table = jnp.broadcast_to(table[:, :, None], (part, 8, rows))

    flat = inputs.reshape(count, channels)
    grad_out = cotangent.reshape(count, channels)
    grad_out_other = to_chan(grad_out)
    total, squares = lax.psum(
        (jnp.sum(flat, axis=1, keepdims=True), jnp.sum(flat * flat, axis=1, keepdims=True)), "chan"
    )
    mean = total / width
    scale1 = lax.rsqrt(squares / width - mean * mean + epsilon)
    unit1 = (flat - mean) * scale1
    unit_parts = spread(unit1.T.reshape(groups, part, sequences, rows))
    mixed_parts, slope_parts = long_conv(unit_parts, kernel, table)
    mixed_t = spread(mixed_parts).reshape(channels, count)
    mixed_t_other = to_chan(mixed_t)

    glu_flat = glu_weight.reshape(width, 2 * channels)
    glu_own = lax.dynamic_slice_in_dim(glu_flat, own_at, channels, 0)
    glu_other = lax.dynamic_slice_in_dim(glu_flat, other_at, channels, 0)
    both = (
        contract(mixed_t, glu_own, 0, 0)
        + contract(mixed_t_other, glu_other, 0, 0)
        + glu_bias.reshape(1, 2 * channels)
    )
    value = both[:, :channels]
    gate = jax.nn.sigmoid(both[:, channels:])
    resid = flat + value * gate
    resid_other = to_chan(resid)

    gain2_other, bias2_other = to_chan((norm2_gain, norm2_bias))
    total = jnp.sum(resid, axis=1, keepdims=True) + jnp.sum(resid_other, axis=1, keepdims=True)
    squares = jnp.sum(resid * resid, axis=1, keepdims=True) + jnp.sum(
        resid_other * resid_other, axis=1, keepdims=True
    )
    mean = total / width
    scale2 = lax.rsqrt(squares / width - mean * mean + epsilon)
    unit2 = (resid - mean) * scale2
    normed2 = unit2 * norm2_gain + norm2_bias
    normed2_other = (resid_other - mean) * scale2 * gain2_other + bias2_other

    in_own = lax.dynamic_slice_in_dim(ffn_in, own_at, channels, 0)
    in_other = lax.dynamic_slice_in_dim(ffn_in, other_at, channels, 0)
    out_own = lax.dynamic_slice_in_dim(ffn_out, own_at, channels, 1)
    out_other = lax.dynamic_slice_in_dim(ffn_out, other_at, channels, 1)
    grad_hidden = contract(grad_out, out_own, 1, 1) + contract(grad_out_other, out_other, 1, 1)
    pre = contract(normed2, in_own, 1, 0) + contract(normed2_other, in_other, 1, 0) + ffn_in_bias
    below = 0.5 * (1.0 + lax.erf(pre * 0.7071067811865476))
    hidden = pre * below
    grad_pre = grad_hidden * (below + pre * (0.3989422804014327 * jnp.exp(-0.5 * pre * pre)))
    grad_normed2 = to_chan(contract(grad_pre, in_other, 1, 1)) + contract(grad_pre, in_own, 1, 1)
    output = (
        to_chan(contract(hidden, out_other, 1, 0))
        + contract(hidden, out_own, 1, 0)
        + resid
        + ffn_out_bias
    )

    scaled = grad_normed2 * norm2_gain
    total, along = lax.psum(
        (
            jnp.sum(scaled, axis=1, keepdims=True),
            jnp.sum(scaled * unit2, axis=1, keepdims=True),
        ),
        "chan",
    )
    grad_resid = grad_out + scale2 * (scaled - total / width - unit2 * (along / width))
    grad_value = grad_resid * gate
    grad_both = jnp.concatenate([grad_value, grad_value * value * (1.0 - gate)], axis=1)
    grad_mixed_t = to_chan(contract(glu_other, grad_both, 1, 1)) + contract(
        glu_own, grad_both, 1, 1
    )
    grad_parts = spread(grad_mixed_t.reshape(groups, part, sequences, rows))
    back_parts, grad_kernel, conv_sums = long_conv_back(
        unit_parts, slope_parts, grad_parts, kernel, table
    )
    scaled = spread(back_parts).reshape(channels, count).T
    total, along = lax.psum(
        (
            jnp.sum(scaled, axis=1, keepdims=True),
            jnp.sum(scaled * unit1, axis=1, keepdims=True),
        ),
        "chan",
    )
    grad_inputs = grad_resid + scale1 * (scaled - total / width - unit1 * (along / width))

    pulled = jnp.einsum(
        "hdb,hnb->hnd",
        jnp.concatenate([grad_kernel, grad_kernel * fine_at], axis=1),
        fine,
        precision=highest,
        preferred_element_type=jnp.float32,
    )
    modes_count = freq.shape[1]
    flat_real, flat_imag = pulled[:, :modes_count, :groups], pulled[:, modes_count:, :groups]
    slant_real = pulled[:, :modes_count, groups:] + coarse_at * flat_real
    slant_imag = pulled[:, modes_count:, groups:] + coarse_at * flat_imag
    zero_real = jnp.sum(coarse_real * flat_real - coarse_imag * flat_imag, axis=2)
    zero_imag = jnp.sum(coarse_real * flat_imag + coarse_imag * flat_real, axis=2)
    one_real = jnp.sum(coarse_real * slant_real - coarse_imag * slant_imag, axis=2)
    one_imag = jnp.sum(coarse_real * slant_imag + coarse_imag * slant_real, axis=2)
    grad_step, grad_decay, grad_freq, grad_coef = modes_back(
        (
            2.0 * zero_real,
            -2.0 * zero_imag,
            2.0 * (weight_real * one_real - weight_imag * one_imag),
            -2.0 * (weight_real * one_imag + weight_imag * one_real),
        )
    )
    sums = jnp.sum(conv_sums, axis=2)
    states = lax.psum(
        jnp.concatenate(
            [grad_decay, grad_freq, grad_coef[0], grad_coef[1], sums[:, :3], grad_step[:, None]],
            axis=1,
        ),
        "dp",
    )
    states = lax.all_gather(states, "seq", axis=0, tiled=True)

    same = chan_index == dp_index

    def halves(own, other):
        return (jnp.where(same, own, other), jnp.where(same, other, own))

    def summed(keep, send, right, left_dim):
        sent = lax.ppermute(contract(send, right, left_dim, 0), "dp", swap)
        return lax.psum_scatter(
            contract(keep, right, left_dim, 0) + sent, "seq", scatter_dimension=0, tiled=True
        )

    grad_ffn_out = summed(*halves(grad_out, grad_out_other), hidden, 0).T
    grad_ffn_in = summed(*halves(normed2, normed2_other), grad_pre, 0)
    grad_glu = summed(*halves(mixed_t, mixed_t_other), grad_both, 1)
    locals_flat = jnp.concatenate(
        [
            jnp.sum(grad_both, axis=0),
            jnp.sum(grad_normed2 * unit2, axis=0),
            jnp.sum(grad_normed2, axis=0),
            jnp.sum(grad_out, axis=0),
            jnp.sum(grad_pre, axis=0),
        ]
    )
    locals_flat = lax.psum(locals_flat, ("dp", "seq"))
    c = channels
    return (
        output.reshape(sequences, rows, channels),
        grad_inputs.reshape(sequences, rows, channels),
        states[:, 4 * modes_count],
        states[:, 4 * modes_count + 1],
        states[:, 4 * modes_count + 3],
        states[:, :modes_count],
        states[:, modes_count : 2 * modes_count],
        jnp.stack(
            [
                states[:, 2 * modes_count : 3 * modes_count],
                states[:, 3 * modes_count : 4 * modes_count],
            ]
        ),
        states[:, 4 * modes_count + 2],
        grad_glu.reshape(-1, 2, channels),
        locals_flat[: 2 * c].reshape(2, c),
        locals_flat[2 * c : 3 * c],
        locals_flat[3 * c : 4 * c],
        grad_ffn_in,
        locals_flat[5 * c :],
        grad_ffn_out,
        locals_flat[4 * c : 5 * c],
    )


def solution(mesh):
    placed = (
        P("dp", "seq", "chan"),
        P("dp", "seq", "chan"),
        P("chan"),
        P("chan"),
        P("chan"),
        P("chan", None),
        P("chan", None),
        P(None, "chan", None),
        P("chan"),
        P(None, None, "chan"),
        P(None, "chan"),
        P("chan"),
        P("chan"),
        P(None, "chan"),
        P("chan"),
        P("chan", None),
        P("chan"),
    )
    return jax.shard_map(
        body,
        mesh=mesh,
        in_specs=placed,
        out_specs=(
            P("dp", "seq", "chan"),
            P("dp", "seq", "chan"),
            P("chan"),
            P("chan"),
            P("chan"),
            P("chan", None),
            P("chan", None),
            P(None, "chan", None),
            P("chan"),
            P(("dp", "seq"), None, "chan"),
            P(None, "chan"),
            P("chan"),
            P("chan"),
            P(("dp", "seq"), "chan"),
            P("chan"),
            P("chan", ("dp", "seq")),
            P("chan"),
        ),
        check_vma=False,
    )
```

```python
from functools import partial

import jax
import jax.numpy as jnp
from jax import lax
from jax.experimental import pallas as pl
from jax.experimental.pallas import tpu as pltpu
from jax.sharding import PartitionSpec as P

epsilon = 1e-05
high = lax.Precision.HIGH
highest = lax.Precision.HIGHEST
swap = [(0, 1), (1, 0)]
anywhere = pl.BlockSpec(memory_space=pl.ANY)
window = 30


def tie(values, *earlier):
    def kernel(*refs):
        pass

    return pl.pallas_call(
        kernel,
        in_specs=[anywhere] * (1 + len(earlier)),
        out_specs=anywhere,
        out_shape=jax.ShapeDtypeStruct(values.shape, values.dtype),
        input_output_aliases={0: 0},
        name="tie",
    )(values, *earlier)


def split(values):
    first = values.astype(jnp.bfloat16)
    return (first, (values - first.astype(jnp.float32)).astype(jnp.bfloat16))


def dot(left, right):
    return jnp.dot(left, right, preferred_element_type=jnp.float32)


def contract(left, right, left_dim, right_dim):
    return lax.dot_general(
        left,
        right,
        (((left_dim,), (right_dim,)), ((), ())),
        precision=high,
        preferred_element_type=jnp.float32,
    )


def state_modes(log_step, decay_log, freq, out_coef):
    step = jnp.exp(log_step)[:, None]
    real_rate = -jnp.exp(decay_log)
    scaled_real = step * real_rate
    scaled_imag = step * freq
    minus_real = (
        jnp.expm1(scaled_real) * jnp.cos(scaled_imag) - 2.0 * jnp.sin(0.5 * scaled_imag) ** 2
    )
    minus_imag = jnp.exp(scaled_real) * jnp.sin(scaled_imag)
    modulus = real_rate * real_rate + freq * freq
    ratio_real = (minus_real * real_rate + minus_imag * freq) / modulus
    ratio_imag = (minus_imag * real_rate - minus_real * freq) / modulus
    weight_real = out_coef[0] * ratio_real - out_coef[1] * ratio_imag
    weight_imag = out_coef[0] * ratio_imag + out_coef[1] * ratio_real
    return (weight_real, weight_imag, scaled_real, scaled_imag)


def powers(positions, scaled_real, scaled_imag):
    where = positions[None, None, :]
    magnitude = jnp.exp(where * scaled_real[:, :, None])
    angle = where * scaled_imag[:, :, None]
    return (magnitude * jnp.cos(angle), magnitude * jnp.sin(angle))


def split(values):
    first = values.astype(jnp.bfloat16)
    return (first, (values - first.astype(jnp.float32)).astype(jnp.bfloat16))

def dot(left, right):
    return jnp.dot(left, right, preferred_element_type=jnp.float32)

def toeplitz_pair(line_ref, channel, lag, before, keep, turn):
    size, rows = keep.shape
    out = []
    for step in range(2):
        line = line_ref[channel, pl.ds(lag + step, 1), :]
        now = pltpu.roll(jnp.broadcast_to(line, (size, rows)), turn, 1, stride=1, stride_axis=0)
        out.append(jnp.where(keep, now, before))
        before = now
    high, low = split(jnp.concatenate(out, axis=1))
    return (jnp.concatenate([high, high, low, jnp.zeros_like(low)], axis=0), before)


def half_blocks(values, left):
    size = values.shape[1] // 2
    high = values.astype(jnp.bfloat16).astype(jnp.float32)
    low = values - high
    high_turned, low_turned = pltpu.roll(high, size, 1), pltpu.roll(low, size, 1)
    first = jnp.concatenate([jnp.where(left, high, low_turned), high], axis=1)
    second = jnp.concatenate([jnp.where(left, high_turned, low), high_turned], axis=1)
    return jnp.concatenate([first, second], axis=0).astype(jnp.bfloat16)


def conv_kernel(unit_ref, kernel_ref, table_ref, *rest):
    mixed_ref, slope_ref = rest[-2:]
    groups, block, sequences, rows = unit_ref.shape
    count, half = groups * sequences, rows // 2
    keep = lax.broadcasted_iota(jnp.int32, (half, rows), 1) >= lax.broadcasted_iota(
        jnp.int32, (half, rows), 0
    )
    left = lax.broadcasted_iota(jnp.int32, (count, rows), 1) < half

    def one(channel, carry):
        unit = unit_ref[:, channel].reshape(count, rows)
        gain = table_ref[channel, 0:1, :]
        bias = table_ref[channel, 1:2, :]
        skip = table_ref[channel, 2:3, :]
        normed = unit * gain + bias
        signal = half_blocks(normed, left)
        before = jnp.zeros((half, rows), jnp.float32)
        even, odd = [0.0] * groups, [0.0] * groups
        for lag in range(0, groups, 2):
            table, before = toeplitz_pair(kernel_ref, channel, lag, before, keep, 0)
            part = dot(signal, table)
            for step in range(2):
                lanes = slice(step * rows, (step + 1) * rows)
                for group in range(groups - lag - step):
                    at, to = group * sequences, group + lag + step
                    even[to] += part[at : at + sequences, lanes]
                    odd[to] += part[count + at : count + at + sequences, lanes]
        turned = pltpu.roll(jnp.concatenate(odd, axis=0), half, 1)
        late = jnp.concatenate(
            [jnp.zeros((sequences, rows), jnp.float32), turned[: count - sequences]], axis=0
        )
        inner = (
            jnp.concatenate(even, axis=0) + jnp.where(left, late, turned) + skip * normed
        )
        below = 0.5 + 0.5 * lax.erf(inner * 0.7071067811865476)
        density = 0.3989422804014327 * jnp.exp(-0.5 * inner * inner)
        mixed_ref[:, channel] = (inner * below).reshape(groups, sequences, rows)
        slope_ref[:, channel] = (below + inner * density).reshape(groups, sequences, rows)
        return carry

    lax.fori_loop(0, block, one, 0, unroll=block)


def conv_back_kernel(unit_ref, slope_ref, grad_ref, kernel_ref, table_ref, *rest):
    back_ref, lags_ref, sums_ref, cross_ref = rest[-4:]
    groups, block, sequences, rows = unit_ref.shape
    count, half = groups * sequences, rows // 2
    keep = (
        lax.broadcasted_iota(jnp.int32, (half, rows), 1)
        <= lax.broadcasted_iota(jnp.int32, (half, rows), 0) + half
    )
    left = lax.broadcasted_iota(jnp.int32, (count, rows), 1) < half
    line_at = lax.broadcasted_iota(jnp.int32, (8, rows), 1)
    tile_row = lax.broadcasted_iota(jnp.int32, (8, rows), 0)

    def diagonals(channel, carry):
        lines = [None] * groups
        for tile in range(half // 8):
            turned = []
            for lag in range(groups):
                now = cross_ref[
                    channel,
                    lag // 2,
                    8 * tile : 8 * tile + 8,
                    (lag % 2) * rows : (lag % 2 + 1) * rows,
                ]
                turned.append(pltpu.roll(now, rows - 8 * tile, 1) if tile else now)
            turned.append(jnp.zeros((8, rows), jnp.float32))
            for lag in range(groups):
                now = turned[lag]
                if tile:
                    now = jnp.where(line_at < rows - 8 * tile, now, turned[lag + 1])
                lines[lag] = now if lines[lag] is None else lines[lag] + now
        lines.append(jnp.zeros((8, rows), jnp.float32))
        for lag in range(groups):
            line = lines[lag]
            for bit in (1, 2, 4):
                line = jnp.where(tile_row & bit != 0, pltpu.roll(line, rows - bit, 1), line)
            lines[lag] = line
        for lag in range(groups):
            line = jnp.where(line_at + tile_row < rows, lines[lag], lines[lag + 1])
            lags_ref[channel, lag : lag + 1, :] = jnp.sum(line, axis=0, keepdims=True)
        return carry

    def one(channel, carry):
        unit = unit_ref[:, channel].reshape(count, rows)
        gain = table_ref[channel, 0:1, :]
        bias = table_ref[channel, 1:2, :]
        skip = table_ref[channel, 2:3, :]
        normed = unit * gain + bias
        grad = (grad_ref[:, channel] * slope_ref[:, channel]).reshape(count, rows)
        nothing = jnp.zeros((sequences, rows), jnp.float32)
        signal = half_blocks(grad, left)
        turned = pltpu.roll(grad, half, 1)
        between = jnp.where(
            left, turned, jnp.concatenate([turned[sequences:], nothing], axis=0)
        )
        sides = jnp.concatenate([normed, pltpu.roll(normed, half, 1)], axis=0)
        sides, sides_low = split(sides.T[:half])
        sides = jnp.concatenate([sides, sides_low, sides], axis=1)
        before = jnp.zeros((half, rows), jnp.float32)
        even, odd = [0.0] * groups, [0.0] * groups
        for lag in range(0, groups, 2):
            table, before = toeplitz_pair(kernel_ref, channel, lag, before, keep, half)
            part = dot(signal, table)
            moved = []
            for step in range(2):
                lanes = slice(step * rows, (step + 1) * rows)
                shift = (lag + step) * sequences
                for group in range(groups - lag - step):
                    at = group * sequences + shift
                    even[group] += part[at : at + sequences, lanes]
                    odd[group] += part[count + at : count + at + sequences, lanes]
                pad = [jnp.zeros((shift, rows), jnp.float32)] if shift else []
                moved.append(
                    jnp.concatenate([grad[shift:], *pad, between[shift:], *pad], axis=0)
                )
            right, right_low = split(jnp.concatenate(moved, axis=1))
            cross_ref[channel, lag // 2] = dot(
                sides, jnp.concatenate([right, right, right_low], axis=0)
            )
        turned = pltpu.roll(jnp.concatenate(even, axis=0), half, 1)
        early = jnp.concatenate([turned[sequences:], nothing], axis=0)
        total = jnp.concatenate(odd, axis=0) + jnp.where(left, turned, early) + skip * grad
        back_ref[:, channel] = (total * gain).reshape(groups, sequences, rows)
        sums_ref[channel, 0:1, :] = jnp.sum(total * unit, axis=0, keepdims=True)
        sums_ref[channel, 1:2, :] = jnp.sum(total, axis=0, keepdims=True)
        sums_ref[channel, 2:3, :] = jnp.sum(grad * normed, axis=0, keepdims=True)
        sums_ref[channel, 3:8, :] = jnp.zeros((5, rows), jnp.float32)
        return carry

    lax.fori_loop(0, block, one, 0, unroll=min(4, block))
    lax.fori_loop(0, block, diagonals, 0, unroll=min(2, block))


def channel_blocks(groups, part):
    block = max(1, 64 // groups)
    return block if part % block == 0 else 1


def long_conv(unit, kernel, table, tokens):
    groups, part, sequences, rows = unit.shape
    block = channel_blocks(groups, part)
    wide = pl.BlockSpec((groups, block, sequences, rows), lambda i: (0, i, 0, 0))
    return pl.pallas_call(
        conv_kernel,
        grid=(part // block,),
        in_specs=[
            wide,
            pl.BlockSpec((block, groups, rows), lambda i: (i, 0, 0)),
            pl.BlockSpec((block, 8, rows), lambda i: (i, 0, 0)),
        ]
        + [anywhere] * len(tokens),
        out_specs=[wide, wide],
        out_shape=[jax.ShapeDtypeStruct(unit.shape, jnp.float32)] * 2,
        compiler_params=pltpu.CompilerParams(vmem_limit_bytes=48 * 1024 * 1024),
        cost_estimate=pl.CostEstimate(
            flops=part * groups * groups * sequences * rows * rows * 6 * window,
            bytes_accessed=12 * unit.size,
            transcendentals=2 * unit.size,
        ),
        name="conv_forward",
    )(unit, kernel, table, *tokens)

def long_conv_back(unit, slope, grad, kernel, table, tokens):
    groups, part, sequences, rows = unit.shape
    block = channel_blocks(groups, part)
    wide = pl.BlockSpec((groups, block, sequences, rows), lambda i: (0, i, 0, 0))
    lags = pl.BlockSpec((block, groups, rows), lambda i: (i, 0, 0))
    few = pl.BlockSpec((block, 8, rows), lambda i: (i, 0, 0))
    return pl.pallas_call(
        conv_back_kernel,
        grid=(part // block,),
        in_specs=[wide, wide, wide, lags, few] + [anywhere] * len(tokens),
        out_specs=[wide, lags, few],
        out_shape=[
            jax.ShapeDtypeStruct(unit.shape, jnp.float32),
            jax.ShapeDtypeStruct(kernel.shape, jnp.float32),
            jax.ShapeDtypeStruct((part, 8, rows), jnp.float32),
        ],
        scratch_shapes=[pltpu.VMEM((block, groups // 2, rows // 2, 2 * rows), jnp.float32)],
        compiler_params=pltpu.CompilerParams(vmem_limit_bytes=48 * 1024 * 1024),
        cost_estimate=pl.CostEstimate(
            flops=part * groups * groups * sequences * rows * rows * 12 * window,
            bytes_accessed=16 * unit.size,
            transcendentals=0,
        ),
        name="conv_backward",
    )(unit, slope, grad, kernel, table, *tokens)


def turned_dot(left, right):
    return lax.dot_general(
        left, right, (((1,), (1,)), ((), ())), preferred_element_type=jnp.float32
    )


def feed_forward_kernel(
    index_ref, resid_ref, other_ref, norm_ref, weight_ref, line_ref, back_ref, *rest
):
    (
        hidden_ref,
        grad_ref,
        keep_ref,
        send_ref,
        unit_ref,
        kept_ref,
        sums_ref,
        bias_ref,
        sent_ref,
        high_ref,
        low_ref,
        total_ref,
    ) = rest[-12:]
    count, channels = resid_ref.shape
    step = pl.program_id(0)
    own_at = pl.ds(pl.multiple_of(index_ref[0] * channels, channels), channels)
    other_at = pl.ds(pl.multiple_of((1 - index_ref[0]) * channels, channels), channels)

    @pl.when(step == 0)
    def _():
        resid, other = resid_ref[...], other_ref[...]
        width = 2.0 * channels
        mean = (
            jnp.sum(resid, axis=1, keepdims=True) + jnp.sum(other, axis=1, keepdims=True)
        ) / width
        squares = jnp.sum(resid * resid, axis=1, keepdims=True) + jnp.sum(
            other * other, axis=1, keepdims=True
        )
        scale = lax.rsqrt(squares / width - mean * mean + epsilon)
        lane = lax.broadcasted_iota(jnp.int32, (count, 128), 1)
        sums_ref[...] = jnp.where(lane == 2, scale, 0.0)
        total_ref[...] = jnp.zeros(total_ref.shape, jnp.float32)
        unit = (resid - mean) * scale
        unit_ref[...] = unit
        same = index_ref[1] == 1
        for values, at, first in (
            (unit, own_at, same),
            ((other - mean) * scale, other_at, jnp.logical_not(same)),
        ):
            normed = values * norm_ref[0:1, at] + norm_ref[1:2, at]
            high, low = split(normed)
            high_ref[:, at] = high
            low_ref[:, at] = low

            @pl.when(first)
            def _():
                keep_ref[...] = normed.T

            @pl.when(jnp.logical_not(first))
            def _():
                send_ref[...] = normed.T

    weight, weight_low = split(weight_ref[...])
    size = weight.shape[1]
    total = jnp.zeros((8, size), jnp.float32)
    chunk = min(count, 256)
    for start in range(0, count, chunk):
        at = slice(start, start + chunk)
        high, low = high_ref[at], low_ref[at]
        pre = dot(high, weight) + dot(low, weight) + dot(high, weight_low) + line_ref[0:1]
        below = 0.5 + 0.5 * lax.erf(pre * 0.7071067811865476)
        density = 0.3989422804014327 * jnp.exp(-0.5 * pre * pre)
        hidden_ref[at] = pre * below
        grad = back_ref[at] * (below + pre * density)
        grad_ref[at] = grad
        total = total + jnp.sum(grad.reshape(chunk // 8, 8, size), axis=0)
        first = jnp.sum(grad * line_ref[1:2], axis=1, keepdims=True)
        second = jnp.sum(grad * (pre - line_ref[2:3]), axis=1, keepdims=True)
        lane = lax.broadcasted_iota(jnp.int32, (chunk, 128), 1)
        sums_ref[at] += jnp.where(lane == 0, first, jnp.where(lane == 1, second, 0.0))
        high, low = split(grad)
        total_ref[at] += (
            turned_dot(high, weight) + turned_dot(low, weight) + turned_dot(high, weight_low)
        )
    bias_ref[...] = total

    @pl.when(step == pl.num_programs(0) - 1)
    def _():
        kept_ref[...] = total_ref[:, own_at]
        sent_ref[...] = total_ref[:, other_at]


def feed_forward(index, resid, other, norm, weight, lines, back, held, tokens, place, spans):
    count, channels = resid.shape
    width, hidden = weight.shape
    size = min(512, hidden)
    full = spans * count
    held = list(held)

    def whole(j, c):
        return (0, 0)

    wide = pl.BlockSpec((count, size), lambda j, c: (place, j))
    narrow = pl.BlockSpec((count, channels), whole)
    turned = pl.BlockSpec((channels, count), lambda j, c: (0, place))
    spot = pl.BlockSpec((count, channels), lambda j, c: (place, 0))
    return pl.pallas_call(
        feed_forward_kernel,
        grid_spec=pltpu.PrefetchScalarGridSpec(
            num_scalar_prefetch=1,
            grid=(hidden // size,),
            in_specs=[
                narrow,
                narrow,
                pl.BlockSpec((8, width), whole),
                pl.BlockSpec((width, size), lambda j, c: (0, j)),
                pl.BlockSpec((8, size), lambda j, c: (0, j)),
                wide,
            ]
            + [anywhere] * (len(held) + len(tokens)),
            out_specs=[
                wide,
                wide,
                turned,
                turned,
                spot,
                spot,
                pl.BlockSpec((count, 128), whole),
                pl.BlockSpec((8, size), lambda j, c: (0, j)),
                narrow,
            ],
            scratch_shapes=[
                pltpu.VMEM((count, width), jnp.bfloat16),
                pltpu.VMEM((count, width), jnp.bfloat16),
                pltpu.VMEM((count, width), jnp.float32),
            ],
        ),
        out_shape=[
            jax.ShapeDtypeStruct(shape, jnp.float32)
            for shape in (
                (full, hidden),
                (full, hidden),
                (channels, full),
                (channels, full),
                (full, channels),
                (full, channels),
                (count, 128),
                (8, hidden),
                (count, channels),
            )
        ],
        input_output_aliases={7 + i: i for i in range(len(held))},
        compiler_params=pltpu.CompilerParams(vmem_limit_bytes=56 * 1024 * 1024),
        cost_estimate=pl.CostEstimate(
            flops=count * width * hidden * 12 * window,
            bytes_accessed=4 * (width * hidden + 3 * count * hidden + 8 * count * channels),
            transcendentals=2 * count * hidden,
        ),
        name="feed_forward",
    )(index, resid, other, norm, weight, lines, back, *held, *tokens)


def weight_kernel(rows, turns, index_ref, keep_ref, send_ref, right_ref, *rest):
    high_ref, low_ref = rest[-2:]
    kept_ref, *sent_refs = rest[-3 - turns : -2]
    size = keep_ref.shape[0]
    turn = pl.program_id(0)

    @pl.when(turn == 0)
    def _():
        for at, ref in ((0, send_ref), (size, keep_ref)):
            high, low = split(ref[...])
            high_ref[at : at + size] = high
            low_ref[at : at + size] = low

    right, right_low = split(right_ref[...])
    chunk = min(size, 256)

    def parts(at, ref):
        for start in range(0, size, chunk):
            rows_at = slice(at + start, at + start + chunk)
            left, left_low = high_ref[rows_at], low_ref[rows_at]
            part = dot(left, right) + dot(left_low, right) + dot(left, right_low)
            for first in range(0, chunk, rows):
                block = (start + first) // rows
                stays = (block % 2 == index_ref[2]).astype(jnp.int32)
                to = pl.multiple_of(stays * (size // 2) + block // 2 * rows, rows)
                ref[pl.ds(to, rows)] = part[first : first + rows]

    parts(size, kept_ref)
    for piece in range(turns):

        @pl.when(turn == piece)
        def _():
            parts(0, sent_refs[piece])


def weight_grad(index, groups, keep, send, right, tokens):
    size, depth = keep.shape
    columns = right.shape[1]
    block = min(512, columns)
    turns = columns // block
    whole = pl.BlockSpec((size, depth), lambda j, c: (0, 0))
    kept, *sent = pl.pallas_call(
        partial(weight_kernel, size // groups, turns),
        grid_spec=pltpu.PrefetchScalarGridSpec(
            num_scalar_prefetch=1,
            grid=(turns,),
            in_specs=[whole, whole, pl.BlockSpec((depth, block), lambda j, c: (0, j))]
            + [anywhere] * len(tokens),
            out_specs=[pl.BlockSpec((size, block), lambda j, c: (0, j))]
            + [pl.BlockSpec((size, block), lambda j, c: (0, 0))] * turns,
            scratch_shapes=[pltpu.VMEM((2 * size, depth), jnp.bfloat16)] * 2,
        ),
        out_shape=[jax.ShapeDtypeStruct((size, columns), jnp.float32)]
        + [jax.ShapeDtypeStruct((size, block), jnp.float32)] * turns,
        compiler_params=pltpu.CompilerParams(vmem_limit_bytes=56 * 1024 * 1024),
        cost_estimate=pl.CostEstimate(
            flops=12 * window * size * depth * columns,
            bytes_accessed=4 * (2 * size * depth + depth * columns + 2 * size * columns),
            transcendentals=0,
        ),
        name="weight_gradient",
    )(index, keep, send, right, *tokens)
    return (kept, sent)


def glu_back_kernel(spans, index_ref, keep_ref, unit_ref, norm_ref, grad_ref, weight_ref, *rest):
    by_span = [rest[i * spans : (i + 1) * spans] for i in range(5)]
    out = rest[-(7 + spans) :]
    resid_ref, both_ref, kept_ref, gain_ref, bias_ref = out[:5]
    sent_refs = out[5 : 5 + spans]
    high_ref, low_ref = out[5 + spans :]
    full, channels = keep_ref.shape
    count = full // spans
    width = 2.0 * channels

    @pl.when(pl.program_id(0) == 0)
    def _():
        chunk = min(count, 128)
        gains = jnp.zeros((8, channels), jnp.float32)
        biases, value_sums, gate_sums, grad_sums = gains, gains, gains, gains

        def fold(values):
            return jnp.sum(values.reshape(chunk // 8, 8, channels), axis=0)

        for start in range(0, full, chunk):
            at = slice(start, start + chunk)
            span, local = start // count, slice(start % count, start % count + chunk)
            other, own_sums, other_sums, value, gate = [refs[span][local] for refs in by_span]
            grad_normed = keep_ref[at] + other
            sums = own_sums + other_sums
            total, along, scale = sums[:, 0:1], sums[:, 1:2], own_sums[:, 2:3]
            unit = unit_ref[at]
            grad_resid = grad_ref[at] + scale * (
                grad_normed * norm_ref[0:1] - total / width - unit * (along / width)
            )
            resid_ref[at] = grad_resid
            grad_value = grad_resid * gate
            grad_gate = grad_value * value * (1.0 - gate)
            gains = gains + fold(grad_normed * unit)
            biases = biases + fold(grad_normed)
            value_sums = value_sums + fold(grad_value)
            gate_sums = gate_sums + fold(grad_gate)
            grad_sums = grad_sums + fold(grad_ref[at])
            for first, values in ((0, grad_value), (channels, grad_gate)):
                lanes = slice(first, first + channels)
                both_ref[at, lanes] = values
                high, low = split(values)
                high_ref[at, lanes] = high
                low_ref[at, lanes] = low
        gain_ref[:, :channels] = gains
        gain_ref[:, channels : 2 * channels] = biases
        gain_ref[:, 2 * channels :] = grad_sums
        bias_ref[:, :channels] = value_sums
        bias_ref[:, channels:] = gate_sums

    weight, weight_low = split(weight_ref[...])
    sending = pl.program_id(0) < pl.num_programs(0) // 2
    for span in range(spans):
        at = slice(span * count, (span + 1) * count)
        high = high_ref[at]
        mixed = (
            turned_dot(weight, high) + turned_dot(weight, low_ref[at]) + turned_dot(weight_low, high)
        )

        @pl.when(sending)
        def _():
            sent_refs[span][...] = mixed

        @pl.when(jnp.logical_not(sending))
        def _():
            kept_ref[:, at] = mixed


def glu_back(index, keep, unit, norm, grad, weight, others, sums, other_sums, values, gates, tokens):
    full, channels = keep.shape
    width, columns = weight.shape
    spans = len(others)
    count = full // spans
    block = min(256, channels)
    turns = channels // block

    def whole(j, c):
        return (0, 0)

    def rows_at(j, c):
        return (jnp.where(j < turns, (1 - c[0]) * turns + j, (c[0] - 1) * turns + j), 0)

    wide = pl.BlockSpec((full, channels), whole)
    span_wide = pl.BlockSpec((count, channels), whole)
    span_few = pl.BlockSpec((count, 128), whole)
    few = pl.BlockSpec((8, columns), whole)
    return pl.pallas_call(
        partial(glu_back_kernel, spans),
        grid_spec=pltpu.PrefetchScalarGridSpec(
            num_scalar_prefetch=1,
            grid=(2 * turns,),
            in_specs=[wide, wide, pl.BlockSpec((8, channels), whole), wide]
            + [pl.BlockSpec((block, columns), rows_at)]
            + ([span_wide] * spans + [span_few] * (2 * spans) + [span_wide] * (2 * spans))
            + [anywhere] * len(tokens),
            out_specs=[
                wide,
                pl.BlockSpec((full, columns), whole),
                pl.BlockSpec((block, full), lambda j, c: (jnp.maximum(j - turns, 0), 0)),
                pl.BlockSpec((8, 3 * channels), whole),
                few,
            ]
            + [pl.BlockSpec((block, count), lambda j, c: (jnp.minimum(j, turns - 1), 0))] * spans,
            scratch_shapes=[pltpu.VMEM((full, columns), jnp.bfloat16)] * 2,
        ),
        out_shape=[
            jax.ShapeDtypeStruct(shape, jnp.float32)
            for shape in (
                (full, channels),
                (full, columns),
                (channels, full),
                (8, 3 * channels),
                (8, columns),
            )
            + ((channels, count),) * spans
        ],
        compiler_params=pltpu.CompilerParams(vmem_limit_bytes=60 * 1024 * 1024),
        cost_estimate=pl.CostEstimate(
            flops=6 * window * full * width * columns,
            bytes_accessed=4 * (11 * full * channels + width * columns),
            transcendentals=0,
        ),
        name="glu_backward",
    )(
        index,
        keep,
        unit,
        norm,
        grad,
        weight,
        *others,
        *sums,
        *other_sums,
        *values,
        *gates,
        *tokens,
    )


def body(
    inputs,
    cotangent,
    norm1_gain,
    norm1_bias,
    log_step,
    decay_log,
    freq,
    out_coef,
    skip,
    glu_weight,
    glu_bias,
    norm2_gain,
    norm2_bias,
    ffn_in,
    ffn_in_bias,
    ffn_out,
    ffn_out_bias,
):
    sequences, rows, channels = inputs.shape
    groups = lax.axis_size("seq")
    seq_index = lax.axis_index("seq")
    chan_index = lax.axis_index("chan")
    dp_index = lax.axis_index("dp")
    width = channels * lax.axis_size("chan")
    count = sequences * rows
    part = channels // groups
    steps = [1 << bit for bit in range(groups.bit_length() - 1)]
    bands = 2
    band = channels // bands
    share = part // bands
    spans = 2
    span = count // spans
    spots = [slice(i * span, (i + 1) * span) for i in range(spans)]

    def to_chan(values):
        return lax.ppermute(values, "chan", swap)

    def to_seq(values, step):
        return lax.ppermute(values, "seq", [(a, a ^ step) for a in range(groups)])

    def spread(values):
        return lax.all_to_all(values, "seq", 0, 0, tiled=True)

    def own_part(values, dim):
        pieces = [
            lax.dynamic_slice_in_dim(values, i * band + seq_index * share, share, dim)
            for i in range(bands)
        ]
        return jnp.concatenate(pieces, axis=dim)

    def in_order(own, other):
        first = chan_index == 0
        return jnp.concatenate(
            [jnp.where(first, own, other), jnp.where(first, other, own)], axis=1
        )

    def halve(values, step, *earlier):
        pairs = values.reshape(-1, 2, *values.shape[1:])
        mine = (seq_index & step) // step
        keep = lax.dynamic_index_in_dim(pairs, mine, 1, keepdims=False)
        send = lax.dynamic_index_in_dim(pairs, 1 - mine, 1, keepdims=False)
        got = to_seq(send, step)
        return keep + (tie(got, *earlier) if earlier else got)

    def finish(values, start):
        for step in steps[start:]:
            values = halve(values, step)
        return values[0]

    own_at = chan_index * channels
    other_at = channels - own_at

    flat = inputs.reshape(count, channels)
    grad_out = cotangent.reshape(count, channels)
    stats = jnp.concatenate([jnp.sum(inputs, axis=2), jnp.sum(inputs * inputs, axis=2)], axis=0)
    stats = lax.psum(stats, "chan")
    mean = stats[:sequences] / width
    scale1 = lax.rsqrt(stats[sequences:] / width - mean * mean + epsilon).reshape(count, 1)
    unit1 = (flat - mean.reshape(count, 1)) * scale1
    grad_out_other = to_chan(tie(grad_out, stats))
    same = chan_index == dp_index
    index = jnp.stack([chan_index, same.astype(jnp.int32), seq_index & 1]).astype(jnp.int32)

    def kept_and_sent(own, other):
        return (jnp.where(same, own, other), jnp.where(same, other, own))

    columns_own = lax.dynamic_slice_in_dim(ffn_out, own_at, channels, 1)
    columns_other = lax.dynamic_slice_in_dim(ffn_out, other_at, channels, 1)
    grad_hidden = contract(grad_out, columns_own, 1, 1)
    grad_hidden_own = grad_hidden
    grad_hidden = grad_hidden + contract(grad_out_other, columns_other, 1, 1)
    norms = jnp.stack([norm2_gain, norm2_bias] + [jnp.zeros((channels,), jnp.float32)] * 6)
    norms = in_order(norms, to_chan(tie(norms, grad_out_other)))
    lines = jnp.dot(norms, ffn_in, precision=highest, preferred_element_type=jnp.float32)
    lines = jnp.stack(
        [ffn_in_bias, lines[0], ffn_in_bias + lines[1]] + [jnp.zeros_like(ffn_in_bias)] * 5
    )

    modes, modes_back = jax.vjp(
        state_modes,
        own_part(log_step, 0),
        own_part(decay_log, 0),
        own_part(freq, 0),
        own_part(out_coef, 1),
    )
    weight_real, weight_imag, scaled_real, scaled_imag = modes
    fine_at = jnp.arange(rows, dtype=jnp.int32).astype(jnp.float32)
    coarse_at = (jnp.arange(groups, dtype=jnp.int32) * rows).astype(jnp.float32)
    fine_real, fine_imag = powers(fine_at, scaled_real, scaled_imag)
    coarse_real, coarse_imag = powers(coarse_at, scaled_real, scaled_imag)
    fine = jnp.concatenate([fine_real, fine_imag], axis=1)
    start_real = weight_real[:, :, None] * coarse_real - weight_imag[:, :, None] * coarse_imag
    start_imag = weight_real[:, :, None] * coarse_imag + weight_imag[:, :, None] * coarse_real
    kernel = 2.0 * jnp.einsum(
        "hnd,hnb->hdb",
        jnp.concatenate([start_real, -start_imag], axis=1),
        fine,
        precision=highest,
        preferred_element_type=jnp.float32,
    )
    table = jnp.stack(
        [own_part(norm1_gain, 0), own_part(norm1_bias, 0), own_part(skip, 0)]
        + [jnp.zeros((part,), jnp.float32)] * 5,
        axis=1,
    )
    table = jnp.broadcast_to(table[:, :, None], (part, 8, rows))
    kernel_turned = jnp.roll(kernel[:, :, ::-1], 1, axis=2)
    kernels_turned = [kernel_turned[i * share : (i + 1) * share] for i in range(bands)]
    kernels = [kernel[i * share : (i + 1) * share] for i in range(bands)]
    tables = [table[i * share : (i + 1) * share] for i in range(bands)]

    unit_parts, slope_parts, mixed, mixed_other = [], [], [], []
    for i in range(bands):
        turned = unit1[:, i * band : (i + 1) * band].T.reshape(groups, share, sequences, rows)
        unit_parts.append(spread(tie(turned, kernel, grad_hidden_own) if i else turned))
    for i in range(bands):
        tokens = (grad_hidden, lines) if i else (grad_out_other,)
        mixed_part, slope_part = long_conv(unit_parts[i], kernels[i], tables[i], tokens)
        slope_parts.append(slope_part)
        arrived = spread(mixed_part).reshape(band, count)
        if i:
            arrived = tie(arrived, mixed_other[0])
        mixed.append(arrived)
        mixed_other.append(to_chan(arrived))

    glu_flat = glu_weight.reshape(width, 2 * channels)
    glu_own = lax.dynamic_slice_in_dim(glu_flat, own_at, channels, 0)
    glu_rows_other = lax.dynamic_slice_in_dim(glu_flat, other_at, channels, 0)
    both_held = glu_bias.reshape(1, 2 * channels)
    for i in range(bands):
        both_held = both_held + contract(mixed[i], glu_own[i * band : (i + 1) * band], 0, 0)
    for i in range(bands - 1):
        both_held = both_held + contract(mixed_other[i], glu_rows_other[i * band : (i + 1) * band], 0, 0)
    values, gates, resids, resids_other = [], [], [], []
    for at in spots:
        both = both_held[at] + contract(
            mixed_other[-1][:, at], glu_rows_other[(bands - 1) * band :], 0, 0
        )
        values.append(both[:, :channels])
        gates.append(jax.nn.sigmoid(both[:, channels:]))
        resids.append(flat[at] + values[-1] * gates[-1])
        resids_other.append(to_chan(resids[-1]))

    grad_out_turned = [v.T for v in kept_and_sent(grad_out, tie(grad_out_other, resids[1]))]
    mixed_pair = kept_and_sent(
        jnp.concatenate(mixed, axis=0), tie(jnp.concatenate(mixed_other, axis=0), resids[1])
    )
    held, tokens = (), (*grad_out_turned, *mixed_pair, *kernels_turned)
    row_sums, hidden_sums, sent = [], [], []
    for i in range(spans):
        *held, row_sum, hidden_sum, send = feed_forward(
            index, resids[i], resids_other[i], norms, ffn_in, lines, grad_hidden, held, tokens, i, spans
        )
        tokens = ()
        row_sums.append(row_sum)
        hidden_sums.append(hidden_sum)
        sent.append(send)
    hidden, grad_pre, normed_keep, normed_send, units, kept = held
    arrived = [to_chan(v) for v in sent]
    other_sums = [to_chan(v) for v in row_sums]

    def to_dp(values):
        return lax.ppermute(values, "dp", swap)

    def ready(keep, others, first, last):
        half, size = keep.shape[0] // 2, others[0].shape[1]
        other = jnp.concatenate([v[:half] for v in others[first:last]], axis=1)
        total = keep[:half, first * size : last * size] + other
        return total.reshape(groups // 2, -1, total.shape[1])

    def joined(keep, others, got, first, last):
        half, size = keep.shape[0] // 2, others[0].shape[1]
        other = jnp.concatenate([v[half:] for v in others[first:last]], axis=1)
        return (keep[half:, first * size : last * size] + other).reshape(got.shape) + got

    out_keep, out_send = weight_grad(
        index, groups, *grad_out_turned, hidden, (sent[1], arrived[0], other_sums[0])
    )
    out_other = [to_dp(v) for v in out_send]
    pieces = len(out_other)
    middle, late = pieces // 2, pieces - pieces // 4
    out_keep = tie(out_keep, arrived[1], other_sums[1])
    out_ready = [
        ready(out_keep, out_other, 0, middle),
        ready(out_keep, out_other, middle, pieces),
    ]

    grad_resid, grad_both, mixed_kept, norm_sums, glu_sums, *mixed_sent = glu_back(
        index,
        kept,
        units,
        jnp.broadcast_to(norm2_gain, (8, channels)),
        grad_out,
        glu_flat,
        arrived,
        row_sums,
        other_sums,
        values,
        gates,
        out_ready,
    )
    out_got = [to_seq(v, steps[0]) for v in out_ready]
    out_first = joined(out_keep, out_other, tie(out_got[0], mixed_sent[1]), 0, middle)
    in_keep, in_send = weight_grad(
        index, groups, normed_keep, normed_send, grad_pre, (mixed_sent[1], out_first)
    )
    in_other = [to_dp(v) for v in in_send]

    few = sequences // spans
    spread_spans = []
    tokens = (in_send[0],)
    for i, at in enumerate(spots):
        total = mixed_kept[:, at] + tie(to_chan(mixed_sent[i]), *tokens)
        moved = total.reshape(bands, groups, share, few, rows)
        spread_spans.append(lax.all_to_all(moved, "seq", 1, 1, tiled=True))
        if not i:
            out_second = joined(out_keep, out_other, tie(out_got[1], moved), middle, pieces)
            glu_keep, glu_send = weight_grad(
                index, groups, *mixed_pair, grad_both, (moved, out_second)
            )
            glu_other = [to_dp(v) for v in glu_send]
            in_keep = tie(in_keep, glu_send[0])
            in_ready = [
                ready(in_keep, in_other, 0, late),
                ready(in_keep, in_other, late, pieces),
            ]
            tokens = (*in_ready, spread_spans[0])
    grad_parts = jnp.concatenate(spread_spans, axis=3)
    hidden = tie(hidden, out_keep, moved)
    output_send = contract(hidden, columns_other, 1, 0)
    glu_keep = tie(glu_keep, output_send)
    glu_ready = ready(glu_keep, glu_other, 0, len(glu_other))
    in_got = [to_seq(v, steps[0]) for v in in_ready]
    out_half = jnp.concatenate([out_first, out_second], axis=2)
    out_more = halve(out_half, steps[1], output_send)
    in_first = joined(in_keep, in_other, tie(in_got[0], output_send), 0, late)
    glu_got = to_seq(glu_ready, steps[0])
    backs, grad_kernels, conv_sums = [], [], []
    for i in range(bands):
        if i:
            in_second = joined(in_keep, in_other, tie(in_got[1], backs[0][0]), late, pieces)
            out_most = halve(out_more, steps[2], backs[0][0]) if len(steps) > 2 else out_more
            tokens = (in_second, out_most)
        else:
            tokens = (glu_ready, in_first, out_more)
        back, grad_kernel, conv_sum = long_conv_back(
            unit_parts[i], slope_parts[i], grad_parts[i], kernels_turned[i], tables[i], tokens
        )
        if i:
            back = tie(back, backs[0][1])
            hidden = tie(hidden, output_send, back)
            output_keep = contract(hidden, columns_own, 1, 0)
            output = to_chan(output_send) + (
                output_keep + jnp.concatenate(resids, axis=0) + ffn_out_bias
            )
            glu_half = joined(glu_keep, glu_other, tie(glu_got, output_keep), 0, len(glu_other))
            in_more = halve(
                jnp.concatenate([in_first, in_second], axis=2), steps[1], output_keep
            )
        backs.append((back, spread(back).reshape(band, count)))
        grad_kernels.append(grad_kernel)
        conv_sums.append(conv_sum)
    backs = [v[1] for v in backs]
    scaled = jnp.concatenate([v.T for v in backs], axis=1)
    sums = jnp.stack([jnp.sum(scaled, axis=1), jnp.sum(scaled * unit1, axis=1)])
    sums = sums + to_chan(sums)
    total, along = sums[0][:, None], sums[1][:, None]
    grad_inputs = tie(grad_resid, backs[1]) + scale1 * (
        scaled - total / width - unit1 * (along / width)
    )

    grad_kernel = jnp.concatenate(grad_kernels, axis=0)
    pulled = jnp.einsum(
        "hdb,hnb->hnd",
        jnp.concatenate([grad_kernel, grad_kernel * fine_at], axis=1),
        fine,
        precision=highest,
        preferred_element_type=jnp.float32,
    )
    modes_count = freq.shape[1]
    flat_real, flat_imag = pulled[:, :modes_count, :groups], pulled[:, modes_count:, :groups]
    slant_real = pulled[:, :modes_count, groups:] + coarse_at * flat_real
    slant_imag = pulled[:, modes_count:, groups:] + coarse_at * flat_imag
    zero_real = jnp.sum(coarse_real * flat_real - coarse_imag * flat_imag, axis=2)
    zero_imag = jnp.sum(coarse_real * flat_imag + coarse_imag * flat_real, axis=2)
    one_real = jnp.sum(coarse_real * slant_real - coarse_imag * slant_imag, axis=2)
    one_imag = jnp.sum(coarse_real * slant_imag + coarse_imag * slant_real, axis=2)
    grad_step, grad_decay, grad_freq, grad_coef = modes_back(
        (
            2.0 * zero_real,
            -2.0 * zero_imag,
            2.0 * (weight_real * one_real - weight_imag * one_imag),
            -2.0 * (weight_real * one_imag + weight_imag * one_real),
        )
    )
    sums = jnp.sum(jnp.concatenate(conv_sums, axis=0), axis=2)
    states = jnp.concatenate(
        [grad_decay, grad_freq, grad_coef[0], grad_coef[1], sums[:, :3], grad_step[:, None]], axis=1
    )
    locals_flat = jnp.concatenate(
        [
            jnp.sum(glu_sums, axis=0),
            jnp.sum(norm_sums, axis=0),
            jnp.sum(sum(hidden_sums), axis=0),
        ]
    )
    columns = 2 * rows
    own_states = jnp.pad(states, ((0, 0), (0, columns - states.shape[1]))).reshape(-1, rows)
    few = own_states.shape[0]
    smalls = jnp.concatenate([own_states, locals_flat.reshape(-1, rows)], axis=0)
    glu_more = halve(glu_half, steps[1])
    smalls = tie(smalls + to_dp(smalls), backs[1], glu_more)
    smalls = spread(jnp.broadcast_to(smalls, (groups, *smalls.shape)))
    states = smalls[:, :few].reshape(groups, bands, share, columns)
    states = states.swapaxes(0, 1).reshape(channels, columns)
    locals_flat = jnp.sum(smalls[:, few:], axis=0).reshape(-1)
    grad_ffn_out = finish(out_most, 3).T
    grad_ffn_in = finish(in_more, 2)
    grad_glu = finish(glu_more, 2)
    c = channels
    return (
        output.reshape(sequences, rows, channels),
        grad_inputs.reshape(sequences, rows, channels),
        states[:, 4 * modes_count],
        states[:, 4 * modes_count + 1],
        states[:, 4 * modes_count + 3],
        states[:, :modes_count],
        states[:, modes_count : 2 * modes_count],
        jnp.stack(
            [
                states[:, 2 * modes_count : 3 * modes_count],
                states[:, 3 * modes_count : 4 * modes_count],
            ]
        ),
        states[:, 4 * modes_count + 2],
        grad_glu.reshape(-1, 2, channels),
        locals_flat[: 2 * c].reshape(2, c),
        locals_flat[2 * c : 3 * c],
        locals_flat[3 * c : 4 * c],
        grad_ffn_in,
        locals_flat[5 * c :],
        grad_ffn_out,
        locals_flat[4 * c : 5 * c],
    )


def solution(mesh):
    placed = (
        P("dp", "seq", "chan"),
        P("dp", "seq", "chan"),
        P("chan"),
        P("chan"),
        P("chan"),
        P("chan", None),
        P("chan", None),
        P(None, "chan", None),
        P("chan"),
        P(None, None, "chan"),
        P(None, "chan"),
        P("chan"),
        P("chan"),
        P(None, "chan"),
        P("chan"),
        P("chan", None),
        P("chan"),
    )
    return jax.shard_map(
        body,
        mesh=mesh,
        in_specs=placed,
        out_specs=(
            P("dp", "seq", "chan"),
            P("dp", "seq", "chan"),
            P("chan"),
            P("chan"),
            P("chan"),
            P("chan", None),
            P("chan", None),
            P(None, "chan", None),
            P("chan"),
            P(("dp", "seq"), None, "chan"),
            P(None, "chan"),
            P("chan"),
            P("chan"),
            P(("dp", "seq"), "chan"),
            P("chan"),
            P("chan", ("dp", "seq")),
            P("chan"),
        ),
        check_vma=False,
    )
```

```python
from functools import partial

import jax
import jax.numpy as jnp
from jax import lax
from jax.experimental import pallas as pl
from jax.experimental.pallas import tpu as pltpu
from jax.sharding import PartitionSpec as P

epsilon = 1e-05
high = lax.Precision.HIGH
highest = lax.Precision.HIGHEST
swap = [(0, 1), (1, 0)]
anywhere = pl.BlockSpec(memory_space=pl.ANY)
window = 30


def tie(values, *earlier):
    def kernel(*refs):
        pass

    return pl.pallas_call(
        kernel,
        in_specs=[anywhere] * (1 + len(earlier)),
        out_specs=anywhere,
        out_shape=jax.ShapeDtypeStruct(values.shape, values.dtype),
        input_output_aliases={0: 0},
        name="tie",
    )(values, *earlier)


def split(values):
    first = values.astype(jnp.bfloat16)
    return (first, (values - first.astype(jnp.float32)).astype(jnp.bfloat16))


def dot(left, right):
    return jnp.dot(left, right, preferred_element_type=jnp.float32)


def contract(left, right, left_dim, right_dim):
    return lax.dot_general(
        left,
        right,
        (((left_dim,), (right_dim,)), ((), ())),
        precision=high,
        preferred_element_type=jnp.float32,
    )


def state_modes(log_step, decay_log, freq, out_coef):
    step = jnp.exp(log_step)[:, None]
    real_rate = -jnp.exp(decay_log)
    scaled_real = step * real_rate
    scaled_imag = step * freq
    minus_real = (
        jnp.expm1(scaled_real) * jnp.cos(scaled_imag) - 2.0 * jnp.sin(0.5 * scaled_imag) ** 2
    )
    minus_imag = jnp.exp(scaled_real) * jnp.sin(scaled_imag)
    modulus = real_rate * real_rate + freq * freq
    ratio_real = (minus_real * real_rate + minus_imag * freq) / modulus
    ratio_imag = (minus_imag * real_rate - minus_real * freq) / modulus
    weight_real = out_coef[0] * ratio_real - out_coef[1] * ratio_imag
    weight_imag = out_coef[0] * ratio_imag + out_coef[1] * ratio_real
    return (weight_real, weight_imag, scaled_real, scaled_imag)


def powers(positions, scaled_real, scaled_imag):
    where = positions[None, None, :]
    magnitude = jnp.exp(where * scaled_real[:, :, None])
    angle = where * scaled_imag[:, :, None]
    return (magnitude * jnp.cos(angle), magnitude * jnp.sin(angle))


def split(values):
    first = values.astype(jnp.bfloat16)
    return (first, (values - first.astype(jnp.float32)).astype(jnp.bfloat16))

def dot(left, right):
    return jnp.dot(left, right, preferred_element_type=jnp.float32)

def toeplitz_pair(line_ref, channel, lag, before, keep, turn):
    size, rows = keep.shape
    out = []
    for step in range(2):
        line = line_ref[channel, pl.ds(lag + step, 1), :]
        now = pltpu.roll(jnp.broadcast_to(line, (size, rows)), turn, 1, stride=1, stride_axis=0)
        out.append(jnp.where(keep, now, before))
        before = now
    high, low = split(jnp.concatenate(out, axis=1))
    return (jnp.concatenate([high, high, low, jnp.zeros_like(low)], axis=0), before)


def half_blocks(values, left):
    size = values.shape[1] // 2
    high = values.astype(jnp.bfloat16).astype(jnp.float32)
    low = values - high
    high_turned, low_turned = pltpu.roll(high, size, 1), pltpu.roll(low, size, 1)
    first = jnp.concatenate([jnp.where(left, high, low_turned), high], axis=1)
    second = jnp.concatenate([jnp.where(left, high_turned, low), high_turned], axis=1)
    return jnp.concatenate([first, second], axis=0).astype(jnp.bfloat16)


def conv_kernel(unit_ref, kernel_ref, table_ref, *rest):
    mixed_ref, slope_ref = rest[-2:]
    groups, block, sequences, rows = unit_ref.shape
    count, half = groups * sequences, rows // 2
    keep = lax.broadcasted_iota(jnp.int32, (half, rows), 1) >= lax.broadcasted_iota(
        jnp.int32, (half, rows), 0
    )
    left = lax.broadcasted_iota(jnp.int32, (count, rows), 1) < half

    def one(channel, carry):
        unit = unit_ref[:, channel].reshape(count, rows)
        gain = table_ref[channel, 0:1, :]
        bias = table_ref[channel, 1:2, :]
        skip = table_ref[channel, 2:3, :]
        normed = unit * gain + bias
        signal = half_blocks(normed, left)
        before = jnp.zeros((half, rows), jnp.float32)
        even, odd = [0.0] * groups, [0.0] * groups
        for lag in range(0, groups, 2):
            table, before = toeplitz_pair(kernel_ref, channel, lag, before, keep, 0)
            part = dot(signal, table)
            for step in range(2):
                lanes = slice(step * rows, (step + 1) * rows)
                for group in range(groups - lag - step):
                    at, to = group * sequences, group + lag + step
                    even[to] += part[at : at + sequences, lanes]
                    odd[to] += part[count + at : count + at + sequences, lanes]
        turned = pltpu.roll(jnp.concatenate(odd, axis=0), half, 1)
        late = jnp.concatenate(
            [jnp.zeros((sequences, rows), jnp.float32), turned[: count - sequences]], axis=0
        )
        inner = (
            jnp.concatenate(even, axis=0) + jnp.where(left, late, turned) + skip * normed
        )
        below = 0.5 + 0.5 * lax.erf(inner * 0.7071067811865476)
        density = 0.3989422804014327 * jnp.exp(-0.5 * inner * inner)
        mixed_ref[:, channel] = (inner * below).reshape(groups, sequences, rows)
        slope_ref[:, channel] = (below + inner * density).reshape(groups, sequences, rows)
        return carry

    lax.fori_loop(0, block, one, 0, unroll=block)


def conv_back_kernel(spans, unit_ref, slope_ref, kernel_ref, table_ref, *rest):
    grad_refs = rest[:spans]
    back_ref, lags_ref, sums_ref, cross_ref = rest[-4:]
    groups, block, sequences, rows = unit_ref.shape
    count, half = groups * sequences, rows // 2
    keep = (
        lax.broadcasted_iota(jnp.int32, (half, rows), 1)
        <= lax.broadcasted_iota(jnp.int32, (half, rows), 0) + half
    )
    left = lax.broadcasted_iota(jnp.int32, (count, rows), 1) < half
    line_at = lax.broadcasted_iota(jnp.int32, (8, rows), 1)
    tile_row = lax.broadcasted_iota(jnp.int32, (8, rows), 0)

    def diagonals(channel, carry):
        lines = [None] * groups
        for tile in range(half // 8):
            turned = []
            for lag in range(groups):
                now = cross_ref[
                    channel,
                    lag // 2,
                    8 * tile : 8 * tile + 8,
                    (lag % 2) * rows : (lag % 2 + 1) * rows,
                ]
                turned.append(pltpu.roll(now, rows - 8 * tile, 1) if tile else now)
            turned.append(jnp.zeros((8, rows), jnp.float32))
            for lag in range(groups):
                now = turned[lag]
                if tile:
                    now = jnp.where(line_at < rows - 8 * tile, now, turned[lag + 1])
                lines[lag] = now if lines[lag] is None else lines[lag] + now
        lines.append(jnp.zeros((8, rows), jnp.float32))
        for lag in range(groups):
            line = lines[lag]
            for bit in (1, 2, 4):
                line = jnp.where(tile_row & bit != 0, pltpu.roll(line, rows - bit, 1), line)
            lines[lag] = line
        for lag in range(groups):
            line = jnp.where(line_at + tile_row < rows, lines[lag], lines[lag + 1])
            lags_ref[channel, lag : lag + 1, :] = jnp.sum(line, axis=0, keepdims=True)
        return carry

    def one(channel, carry):
        unit = unit_ref[:, channel].reshape(count, rows)
        gain = table_ref[channel, 0:1, :]
        bias = table_ref[channel, 1:2, :]
        skip = table_ref[channel, 2:3, :]
        normed = unit * gain + bias
        grad = jnp.concatenate([ref[:, 0, channel] for ref in grad_refs], axis=1)
        grad = (grad * slope_ref[:, channel]).reshape(count, rows)
        nothing = jnp.zeros((sequences, rows), jnp.float32)
        signal = half_blocks(grad, left)
        turned = pltpu.roll(grad, half, 1)
        between = jnp.where(
            left, turned, jnp.concatenate([turned[sequences:], nothing], axis=0)
        )
        sides = jnp.concatenate([normed, pltpu.roll(normed, half, 1)], axis=0)
        sides, sides_low = split(sides.T[:half])
        sides = jnp.concatenate([sides, sides_low, sides], axis=1)
        before = jnp.zeros((half, rows), jnp.float32)
        even, odd = [0.0] * groups, [0.0] * groups
        for lag in range(0, groups, 2):
            table, before = toeplitz_pair(kernel_ref, channel, lag, before, keep, half)
            part = dot(signal, table)
            moved = []
            for step in range(2):
                lanes = slice(step * rows, (step + 1) * rows)
                shift = (lag + step) * sequences
                for group in range(groups - lag - step):
                    at = group * sequences + shift
                    even[group] += part[at : at + sequences, lanes]
                    odd[group] += part[count + at : count + at + sequences, lanes]
                pad = [jnp.zeros((shift, rows), jnp.float32)] if shift else []
                moved.append(
                    jnp.concatenate([grad[shift:], *pad, between[shift:], *pad], axis=0)
                )
            right, right_low = split(jnp.concatenate(moved, axis=1))
            cross_ref[channel, lag // 2] = dot(
                sides, jnp.concatenate([right, right, right_low], axis=0)
            )
        turned = pltpu.roll(jnp.concatenate(even, axis=0), half, 1)
        early = jnp.concatenate([turned[sequences:], nothing], axis=0)
        total = jnp.concatenate(odd, axis=0) + jnp.where(left, turned, early) + skip * grad
        back_ref[:, channel] = (total * gain).reshape(groups, sequences, rows)
        sums_ref[channel, 0:1, :] = jnp.sum(total * unit, axis=0, keepdims=True)
        sums_ref[channel, 1:2, :] = jnp.sum(total, axis=0, keepdims=True)
        sums_ref[channel, 2:3, :] = jnp.sum(grad * normed, axis=0, keepdims=True)
        sums_ref[channel, 3:8, :] = jnp.zeros((5, rows), jnp.float32)
        return carry

    lax.fori_loop(0, block, one, 0, unroll=min(4, block))
    lax.fori_loop(0, block, diagonals, 0, unroll=min(2, block))


def channel_blocks(groups, part):
    block = max(1, 64 // groups)
    return block if part % block == 0 else 1


def long_conv(unit, kernel, table, tokens):
    groups, part, sequences, rows = unit.shape
    block = channel_blocks(groups, part)
    wide = pl.BlockSpec((groups, block, sequences, rows), lambda i: (0, i, 0, 0))
    return pl.pallas_call(
        conv_kernel,
        grid=(part // block,),
        in_specs=[
            wide,
            pl.BlockSpec((block, groups, rows), lambda i: (i, 0, 0)),
            pl.BlockSpec((block, 8, rows), lambda i: (i, 0, 0)),
        ]
        + [anywhere] * len(tokens),
        out_specs=[wide, wide],
        out_shape=[jax.ShapeDtypeStruct(unit.shape, jnp.float32)] * 2,
        compiler_params=pltpu.CompilerParams(vmem_limit_bytes=48 * 1024 * 1024),
        cost_estimate=pl.CostEstimate(
            flops=part * groups * groups * sequences * rows * rows * 6 * window,
            bytes_accessed=12 * unit.size,
            transcendentals=2 * unit.size,
        ),
        name="conv_forward",
    )(unit, kernel, table, *tokens)

def long_conv_back(unit, slope, grads, band, kernel, table, tokens):
    groups, part, sequences, rows = unit.shape
    block = channel_blocks(groups, part)
    wide = pl.BlockSpec((groups, block, sequences, rows), lambda i: (0, i, 0, 0))
    lags = pl.BlockSpec((block, groups, rows), lambda i: (i, 0, 0))
    few = pl.BlockSpec((block, 8, rows), lambda i: (i, 0, 0))
    return pl.pallas_call(
        partial(conv_back_kernel, len(grads)),
        grid=(part // block,),
        in_specs=[wide, wide, lags, few]
        + [pl.BlockSpec((groups, 1, block, *v.shape[3:]), lambda i: (0, band, i, 0, 0)) for v in grads]
        + [anywhere] * len(tokens),
        out_specs=[wide, lags, few],
        out_shape=[
            jax.ShapeDtypeStruct(unit.shape, jnp.float32),
            jax.ShapeDtypeStruct(kernel.shape, jnp.float32),
            jax.ShapeDtypeStruct((part, 8, rows), jnp.float32),
        ],
        scratch_shapes=[pltpu.VMEM((block, groups // 2, rows // 2, 2 * rows), jnp.float32)],
        compiler_params=pltpu.CompilerParams(vmem_limit_bytes=48 * 1024 * 1024),
        cost_estimate=pl.CostEstimate(
            flops=part * groups * groups * sequences * rows * rows * 12 * window,
            bytes_accessed=16 * unit.size,
            transcendentals=0,
        ),
        name="conv_backward",
    )(unit, slope, kernel, table, *grads, *tokens)


def turned_dot(left, right):
    return lax.dot_general(
        left, right, (((1,), (1,)), ((), ())), preferred_element_type=jnp.float32
    )


def feed_forward_kernel(
    index_ref, resid_ref, other_ref, norm_ref, weight_ref, line_ref, back_ref, *rest
):
    (
        hidden_ref,
        grad_ref,
        keep_ref,
        send_ref,
        unit_ref,
        kept_ref,
        sums_ref,
        bias_ref,
        sent_ref,
        high_ref,
        low_ref,
        total_ref,
    ) = rest[-12:]
    count, channels = resid_ref.shape
    step = pl.program_id(0)
    own_at = pl.ds(pl.multiple_of(index_ref[0] * channels, channels), channels)
    other_at = pl.ds(pl.multiple_of((1 - index_ref[0]) * channels, channels), channels)

    @pl.when(step == 0)
    def _():
        resid, other = resid_ref[...], other_ref[...]
        width = 2.0 * channels
        mean = (
            jnp.sum(resid, axis=1, keepdims=True) + jnp.sum(other, axis=1, keepdims=True)
        ) / width
        squares = jnp.sum(resid * resid, axis=1, keepdims=True) + jnp.sum(
            other * other, axis=1, keepdims=True
        )
        scale = lax.rsqrt(squares / width - mean * mean + epsilon)
        lane = lax.broadcasted_iota(jnp.int32, (count, 128), 1)
        sums_ref[...] = jnp.where(lane == 2, scale, 0.0)
        total_ref[...] = jnp.zeros(total_ref.shape, jnp.float32)
        unit = (resid - mean) * scale
        unit_ref[...] = unit
        same = index_ref[1] == 1
        for values, at, first in (
            (unit, own_at, same),
            ((other - mean) * scale, other_at, jnp.logical_not(same)),
        ):
            normed = values * norm_ref[0:1, at] + norm_ref[1:2, at]
            high, low = split(normed)
            high_ref[:, at] = high
            low_ref[:, at] = low

            @pl.when(first)
            def _():
                keep_ref[...] = normed.T

            @pl.when(jnp.logical_not(first))
            def _():
                send_ref[...] = normed.T

    weight, weight_low = split(weight_ref[...])
    size = weight.shape[1]
    total = jnp.zeros((8, size), jnp.float32)
    chunk = min(count, 256)
    for start in range(0, count, chunk):
        at = slice(start, start + chunk)
        high, low = high_ref[at], low_ref[at]
        pre = dot(high, weight) + dot(low, weight) + dot(high, weight_low) + line_ref[0:1]
        below = 0.5 + 0.5 * lax.erf(pre * 0.7071067811865476)
        density = 0.3989422804014327 * jnp.exp(-0.5 * pre * pre)
        hidden_ref[at] = pre * below
        grad = back_ref[at] * (below + pre * density)
        grad_ref[at] = grad
        total = total + jnp.sum(grad.reshape(chunk // 8, 8, size), axis=0)
        first = jnp.sum(grad * line_ref[1:2], axis=1, keepdims=True)
        second = jnp.sum(grad * (pre - line_ref[2:3]), axis=1, keepdims=True)
        lane = lax.broadcasted_iota(jnp.int32, (chunk, 128), 1)
        sums_ref[at] += jnp.where(lane == 0, first, jnp.where(lane == 1, second, 0.0))
        high, low = split(grad)
        total_ref[at] += (
            turned_dot(high, weight) + turned_dot(low, weight) + turned_dot(high, weight_low)
        )
    bias_ref[...] = total

    @pl.when(step == pl.num_programs(0) - 1)
    def _():
        kept_ref[...] = total_ref[:, own_at]
        sent_ref[...] = total_ref[:, other_at]


def feed_forward(index, resid, other, norm, weight, lines, back, held, tokens, place, spans):
    count, channels = resid.shape
    width, hidden = weight.shape
    size = min(512, hidden)
    full = spans * count
    held = list(held)

    def whole(j, c):
        return (0, 0)

    wide = pl.BlockSpec((count, size), lambda j, c: (place, j))
    narrow = pl.BlockSpec((count, channels), whole)
    turned = pl.BlockSpec((channels, count), lambda j, c: (0, place))
    spot = pl.BlockSpec((count, channels), lambda j, c: (place, 0))
    return pl.pallas_call(
        feed_forward_kernel,
        grid_spec=pltpu.PrefetchScalarGridSpec(
            num_scalar_prefetch=1,
            grid=(hidden // size,),
            in_specs=[
                narrow,
                narrow,
                pl.BlockSpec((8, width), whole),
                pl.BlockSpec((width, size), lambda j, c: (0, j)),
                pl.BlockSpec((8, size), lambda j, c: (0, j)),
                wide,
            ]
            + [anywhere] * (len(held) + len(tokens)),
            out_specs=[
                wide,
                wide,
                turned,
                turned,
                spot,
                spot,
                pl.BlockSpec((count, 128), whole),
                pl.BlockSpec((8, size), lambda j, c: (0, j)),
                narrow,
            ],
            scratch_shapes=[
                pltpu.VMEM((count, width), jnp.bfloat16),
                pltpu.VMEM((count, width), jnp.bfloat16),
                pltpu.VMEM((count, width), jnp.float32),
            ],
        ),
        out_shape=[
            jax.ShapeDtypeStruct(shape, jnp.float32)
            for shape in (
                (full, hidden),
                (full, hidden),
                (channels, full),
                (channels, full),
                (full, channels),
                (full, channels),
                (count, 128),
                (8, hidden),
                (count, channels),
            )
        ],
        input_output_aliases={7 + i: i for i in range(len(held))},
        compiler_params=pltpu.CompilerParams(vmem_limit_bytes=56 * 1024 * 1024),
        cost_estimate=pl.CostEstimate(
            flops=count * width * hidden * 12 * window,
            bytes_accessed=4 * (width * hidden + 3 * count * hidden + 8 * count * channels),
            transcendentals=2 * count * hidden,
        ),
        name="feed_forward",
    )(index, resid, other, norm, weight, lines, back, *held, *tokens)


def weight_kernel(rows, turns, index_ref, keep_ref, send_ref, right_ref, *rest):
    high_ref, low_ref = rest[-2:]
    kept_ref, *sent_refs = rest[-3 - turns : -2]
    parts_of = max(1, turns // 2)
    size = keep_ref.shape[0]
    turn = pl.program_id(0)

    @pl.when(turn == 0)
    def _():
        for at, ref in ((0, send_ref), (size, keep_ref)):
            high, low = split(ref[...])
            high_ref[at : at + size] = high
            low_ref[at : at + size] = low

    right, right_low = split(right_ref[...])
    chunk = min(size, 256)

    def parts(at, place):
        for start in range(0, size, chunk):
            rows_at = slice(at + start, at + start + chunk)
            left, left_low = high_ref[rows_at], low_ref[rows_at]
            part = dot(left, right) + dot(left_low, right) + dot(left, right_low)
            for first in range(0, chunk, rows):
                block = (start + first) // rows
                place(block, part[first : first + rows])

    def keep(block, values):
        stays = (block % 2 == index_ref[2]).astype(jnp.int32)
        to = pl.multiple_of(stays * (size // 2) + block // 2 * rows, rows)
        kept_ref[pl.ds(to, rows)] = values

    parts(size, keep)
    for piece in range(turns):
        group, lane = piece // 2, piece % 2 * right.shape[1]

        def send(block, values):
            at = (pl.ds(block // 2 * rows, rows), pl.ds(lane, values.shape[1]))
            goes = block % 2 != index_ref[2]

            @pl.when(goes)
            def _():
                sent_refs[group][at] = values

            @pl.when(jnp.logical_not(goes))
            def _():
                sent_refs[parts_of + group][at] = values

        @pl.when(turn == piece)
        def _():
            parts(0, send)


def weight_grad(index, groups, keep, send, right, tokens):
    size, depth = keep.shape
    columns = right.shape[1]
    block = min(512, columns)
    turns = columns // block
    whole = pl.BlockSpec((size, depth), lambda j, c: (0, 0))
    kept, *sent = pl.pallas_call(
        partial(weight_kernel, size // groups, turns),
        grid_spec=pltpu.PrefetchScalarGridSpec(
            num_scalar_prefetch=1,
            grid=(turns,),
            in_specs=[whole, whole, pl.BlockSpec((depth, block), lambda j, c: (0, j))]
            + [anywhere] * len(tokens),
            out_specs=[pl.BlockSpec((size, block), lambda j, c: (0, j))]
            + [pl.BlockSpec((size // 2, 2 * block), lambda j, c: (0, 0))] * turns,
            scratch_shapes=[pltpu.VMEM((2 * size, depth), jnp.bfloat16)] * 2,
        ),
        out_shape=[jax.ShapeDtypeStruct((size, columns), jnp.float32)]
        + [jax.ShapeDtypeStruct((size // 2, 2 * block), jnp.float32)] * turns,
        compiler_params=pltpu.CompilerParams(vmem_limit_bytes=56 * 1024 * 1024),
        cost_estimate=pl.CostEstimate(
            flops=12 * window * size * depth * columns,
            bytes_accessed=4 * (2 * size * depth + depth * columns + 2 * size * columns),
            transcendentals=0,
        ),
        name="weight_gradient",
    )(index, keep, send, right, *tokens)
    return (kept, sent)


def glu_back_kernel(spans, index_ref, keep_ref, unit_ref, norm_ref, grad_ref, weight_ref, *rest):
    by_span = [rest[i * spans : (i + 1) * spans] for i in range(5)]
    out = rest[-(7 + spans) :]
    resid_ref, both_ref, kept_ref, gain_ref, bias_ref = out[:5]
    sent_refs = out[5 : 5 + spans]
    high_ref, low_ref = out[5 + spans :]
    full, channels = keep_ref.shape
    count = full // spans
    width = 2.0 * channels

    @pl.when(pl.program_id(0) == 0)
    def _():
        chunk = min(count, 128)
        gains = jnp.zeros((8, channels), jnp.float32)
        biases, value_sums, gate_sums, grad_sums = gains, gains, gains, gains

        def fold(values):
            return jnp.sum(values.reshape(chunk // 8, 8, channels), axis=0)

        for start in range(0, full, chunk):
            at = slice(start, start + chunk)
            span, local = start // count, slice(start % count, start % count + chunk)
            other, own_sums, other_sums, value, gate = [refs[span][local] for refs in by_span]
            grad_normed = keep_ref[at] + other
            sums = own_sums + other_sums
            total, along, scale = sums[:, 0:1], sums[:, 1:2], own_sums[:, 2:3]
            unit = unit_ref[at]
            grad_resid = grad_ref[at] + scale * (
                grad_normed * norm_ref[0:1] - total / width - unit * (along / width)
            )
            resid_ref[at] = grad_resid
            grad_value = grad_resid * gate
            grad_gate = grad_value * value * (1.0 - gate)
            gains = gains + fold(grad_normed * unit)
            biases = biases + fold(grad_normed)
            value_sums = value_sums + fold(grad_value)
            gate_sums = gate_sums + fold(grad_gate)
            grad_sums = grad_sums + fold(grad_ref[at])
            for first, values in ((0, grad_value), (channels, grad_gate)):
                lanes = slice(first, first + channels)
                both_ref[at, lanes] = values
                high, low = split(values)
                high_ref[at, lanes] = high
                low_ref[at, lanes] = low
        gain_ref[:, :channels] = gains
        gain_ref[:, channels : 2 * channels] = biases
        gain_ref[:, 2 * channels :] = grad_sums
        bias_ref[:, :channels] = value_sums
        bias_ref[:, channels:] = gate_sums

    weight, weight_low = split(weight_ref[...])
    sending = pl.program_id(0) < pl.num_programs(0) // 2
    for span in range(spans):
        at = slice(span * count, (span + 1) * count)
        high = high_ref[at]
        mixed = (
            turned_dot(weight, high) + turned_dot(weight, low_ref[at]) + turned_dot(weight_low, high)
        )

        @pl.when(sending)
        def _():
            sent_refs[span][...] = mixed

        @pl.when(jnp.logical_not(sending))
        def _():
            kept_ref[:, at] = mixed


def glu_back(index, keep, unit, norm, grad, weight, others, sums, other_sums, values, gates, tokens):
    full, channels = keep.shape
    width, columns = weight.shape
    spans = len(others)
    count = full // spans
    block = min(256, channels)
    turns = channels // block

    def whole(j, c):
        return (0, 0)

    def rows_at(j, c):
        return (jnp.where(j < turns, (1 - c[0]) * turns + j, (c[0] - 1) * turns + j), 0)

    wide = pl.BlockSpec((full, channels), whole)
    span_wide = pl.BlockSpec((count, channels), whole)
    span_few = pl.BlockSpec((count, 128), whole)
    few = pl.BlockSpec((8, columns), whole)
    return pl.pallas_call(
        partial(glu_back_kernel, spans),
        grid_spec=pltpu.PrefetchScalarGridSpec(
            num_scalar_prefetch=1,
            grid=(2 * turns,),
            in_specs=[wide, wide, pl.BlockSpec((8, channels), whole), wide]
            + [pl.BlockSpec((block, columns), rows_at)]
            + ([span_wide] * spans + [span_few] * (2 * spans) + [span_wide] * (2 * spans))
            + [anywhere] * len(tokens),
            out_specs=[
                wide,
                pl.BlockSpec((full, columns), whole),
                pl.BlockSpec((block, full), lambda j, c: (jnp.maximum(j - turns, 0), 0)),
                pl.BlockSpec((8, 3 * channels), whole),
                few,
            ]
            + [pl.BlockSpec((block, count), lambda j, c: (jnp.minimum(j, turns - 1), 0))] * spans,
            scratch_shapes=[pltpu.VMEM((full, columns), jnp.bfloat16)] * 2,
        ),
        out_shape=[
            jax.ShapeDtypeStruct(shape, jnp.float32)
            for shape in (
                (full, channels),
                (full, columns),
                (channels, full),
                (8, 3 * channels),
                (8, columns),
            )
            + ((channels, count),) * spans
        ],
        compiler_params=pltpu.CompilerParams(vmem_limit_bytes=60 * 1024 * 1024),
        cost_estimate=pl.CostEstimate(
            flops=6 * window * full * width * columns,
            bytes_accessed=4 * (11 * full * channels + width * columns),
            transcendentals=0,
        ),
        name="glu_backward",
    )(
        index,
        keep,
        unit,
        norm,
        grad,
        weight,
        *others,
        *sums,
        *other_sums,
        *values,
        *gates,
        *tokens,
    )


def first_norm_kernel(inputs_ref, resid_ref, rows_ref, *rest):
    out_ref = rest[-1]
    bands = len(rest) // 2
    channels = inputs_ref.shape[1]
    width = 2.0 * channels
    columns = rows_ref[...].T
    mean, scale, total, along = [columns[:, i : i + 1] for i in range(4)]
    for band in range(bands):
        scaled = rest[band][...].T
        lanes = slice(band * scaled.shape[1], (band + 1) * scaled.shape[1])
        unit = (inputs_ref[:, lanes] - mean) * scale
        out_ref[:, lanes] = resid_ref[:, lanes] + scale * (
            scaled - total / width - unit * (along / width)
        )


def first_norm_back(inputs, resid, rows, backs, tokens):
    count, channels = inputs.shape
    block = min(256, count)
    wide = pl.BlockSpec((block, channels), lambda j: (j, 0))
    bands = [pl.BlockSpec((v.shape[0], block), lambda j: (0, j)) for v in backs]
    tokens = list(tokens) + [backs[0]] * (len(backs) - len(tokens))
    return pl.pallas_call(
        first_norm_kernel,
        grid=(count // block,),
        in_specs=[wide, wide, pl.BlockSpec((8, block), lambda j: (0, j))]
        + bands
        + [anywhere] * len(tokens),
        out_specs=wide,
        out_shape=jax.ShapeDtypeStruct((count, channels), jnp.float32),
        compiler_params=pltpu.CompilerParams(vmem_limit_bytes=32 * 1024 * 1024),
        name="first_norm_backward",
    )(inputs, resid, rows, *backs, *tokens)


def body(
    inputs,
    cotangent,
    norm1_gain,
    norm1_bias,
    log_step,
    decay_log,
    freq,
    out_coef,
    skip,
    glu_weight,
    glu_bias,
    norm2_gain,
    norm2_bias,
    ffn_in,
    ffn_in_bias,
    ffn_out,
    ffn_out_bias,
):
    sequences, rows, channels = inputs.shape
    groups = lax.axis_size("seq")
    seq_index = lax.axis_index("seq")
    chan_index = lax.axis_index("chan")
    dp_index = lax.axis_index("dp")
    width = channels * lax.axis_size("chan")
    count = sequences * rows
    part = channels // groups
    steps = [1 << bit for bit in range(groups.bit_length() - 1)]
    bands = 2
    band = channels // bands
    share = part // bands
    spans = 2
    span = count // spans
    spots = [slice(i * span, (i + 1) * span) for i in range(spans)]

    def to_chan(values):
        return lax.ppermute(values, "chan", swap)

    def to_seq(values, step):
        return lax.ppermute(values, "seq", [(a, a ^ step) for a in range(groups)])

    def spread(values):
        return lax.all_to_all(values, "seq", 0, 0, tiled=True)

    def own_part(values, dim):
        pieces = [
            lax.dynamic_slice_in_dim(values, i * band + seq_index * share, share, dim)
            for i in range(bands)
        ]
        return jnp.concatenate(pieces, axis=dim)

    def in_order(own, other):
        first = chan_index == 0
        return jnp.concatenate(
            [jnp.where(first, own, other), jnp.where(first, other, own)], axis=1
        )

    def halve(values, step, *earlier):
        pairs = values.reshape(-1, 2, *values.shape[1:])
        mine = (seq_index & step) // step
        keep = lax.dynamic_index_in_dim(pairs, mine, 1, keepdims=False)
        send = lax.dynamic_index_in_dim(pairs, 1 - mine, 1, keepdims=False)
        got = to_seq(send, step)
        return keep + (tie(got, *earlier) if earlier else got)

    def finish(values, start, *earlier):
        for step in steps[start:]:
            values = halve(values, step, *earlier)
        return values[0]

    def halves_of(values, step):
        pairs = values.reshape(-1, 2, *values.shape[1:])
        mine = (seq_index & step) // step
        return [lax.dynamic_index_in_dim(pairs, at, 1, keepdims=False) for at in (mine, 1 - mine)]

    own_at = chan_index * channels
    other_at = channels - own_at

    flat = inputs.reshape(count, channels)
    grad_out = cotangent.reshape(count, channels)
    stats = jnp.concatenate([jnp.sum(inputs, axis=2), jnp.sum(inputs * inputs, axis=2)], axis=0)
    stats = lax.psum(stats, "chan")
    mean = stats[:sequences] / width
    scale1 = lax.rsqrt(stats[sequences:] / width - mean * mean + epsilon).reshape(count, 1)
    unit1 = (flat - mean.reshape(count, 1)) * scale1
    grad_out_other = to_chan(tie(grad_out, stats))
    same = chan_index == dp_index
    index = jnp.stack([chan_index, same.astype(jnp.int32), seq_index & 1]).astype(jnp.int32)

    def kept_and_sent(own, other):
        return (jnp.where(same, own, other), jnp.where(same, other, own))

    columns_own = lax.dynamic_slice_in_dim(ffn_out, own_at, channels, 1)
    columns_other = lax.dynamic_slice_in_dim(ffn_out, other_at, channels, 1)
    grad_hidden = contract(grad_out, columns_own, 1, 1)
    grad_hidden_own = grad_hidden
    grad_hidden = grad_hidden + contract(grad_out_other, columns_other, 1, 1)
    norms = jnp.stack([norm2_gain, norm2_bias] + [jnp.zeros((channels,), jnp.float32)] * 6)
    norms = in_order(norms, to_chan(tie(norms, grad_out_other)))
    lines = jnp.dot(norms, ffn_in, precision=highest, preferred_element_type=jnp.float32)
    lines = jnp.stack(
        [ffn_in_bias, lines[0], ffn_in_bias + lines[1]] + [jnp.zeros_like(ffn_in_bias)] * 5
    )

    modes, modes_back = jax.vjp(
        state_modes,
        own_part(log_step, 0),
        own_part(decay_log, 0),
        own_part(freq, 0),
        own_part(out_coef, 1),
    )
    weight_real, weight_imag, scaled_real, scaled_imag = modes
    fine_at = jnp.arange(rows, dtype=jnp.int32).astype(jnp.float32)
    coarse_at = (jnp.arange(groups, dtype=jnp.int32) * rows).astype(jnp.float32)
    fine_real, fine_imag = powers(fine_at, scaled_real, scaled_imag)
    coarse_real, coarse_imag = powers(coarse_at, scaled_real, scaled_imag)
    fine = jnp.concatenate([fine_real, fine_imag], axis=1)
    start_real = weight_real[:, :, None] * coarse_real - weight_imag[:, :, None] * coarse_imag
    start_imag = weight_real[:, :, None] * coarse_imag + weight_imag[:, :, None] * coarse_real
    kernel = 2.0 * jnp.einsum(
        "hnd,hnb->hdb",
        jnp.concatenate([start_real, -start_imag], axis=1),
        fine,
        precision=highest,
        preferred_element_type=jnp.float32,
    )
    table = jnp.stack(
        [own_part(norm1_gain, 0), own_part(norm1_bias, 0), own_part(skip, 0)]
        + [jnp.zeros((part,), jnp.float32)] * 5,
        axis=1,
    )
    table = jnp.broadcast_to(table[:, :, None], (part, 8, rows))
    kernel_turned = jnp.roll(kernel[:, :, ::-1], 1, axis=2)
    kernels_turned = [kernel_turned[i * share : (i + 1) * share] for i in range(bands)]
    kernels = [kernel[i * share : (i + 1) * share] for i in range(bands)]
    tables = [table[i * share : (i + 1) * share] for i in range(bands)]

    unit_parts, unit_turned, slope_parts, mixed, mixed_other = [], [], [], [], []
    for i in range(bands):
        turned = unit1[:, i * band : (i + 1) * band].T.reshape(groups, share, sequences, rows)
        unit_turned.append(turned)
        unit_parts.append(spread(tie(turned, kernel, grad_hidden_own) if i else turned))
    for i in range(bands):
        tokens = (grad_hidden, lines) if i else ()
        mixed_part, slope_part = long_conv(unit_parts[i], kernels[i], tables[i], tokens)
        slope_parts.append(slope_part)
        arrived = spread(mixed_part).reshape(band, count)
        if i:
            arrived = tie(arrived, mixed_other[0])
        mixed.append(arrived)
        mixed_other.append(to_chan(arrived))

    glu_flat = glu_weight.reshape(width, 2 * channels)
    glu_own = lax.dynamic_slice_in_dim(glu_flat, own_at, channels, 0)
    glu_rows_other = lax.dynamic_slice_in_dim(glu_flat, other_at, channels, 0)
    both_held = glu_bias.reshape(1, 2 * channels)
    for i in range(bands):
        both_held = both_held + contract(mixed[i], glu_own[i * band : (i + 1) * band], 0, 0)
    for i in range(bands - 1):
        both_held = both_held + contract(mixed_other[i], glu_rows_other[i * band : (i + 1) * band], 0, 0)
    values, gates, resids, resids_other = [], [], [], []
    for at in spots:
        both = both_held[at] + contract(
            mixed_other[-1][:, at], glu_rows_other[(bands - 1) * band :], 0, 0
        )
        values.append(both[:, :channels])
        gates.append(jax.nn.sigmoid(both[:, channels:]))
        resids.append(flat[at] + values[-1] * gates[-1])
        resids_other.append(to_chan(resids[-1]))

    grad_out_turned = [v.T for v in kept_and_sent(grad_out, tie(grad_out_other, resids[1]))]
    mixed_pair = kept_and_sent(
        jnp.concatenate(mixed, axis=0), tie(jnp.concatenate(mixed_other, axis=0), resids[1])
    )
    held, tokens = (), (*grad_out_turned, *mixed_pair, *kernels_turned)
    row_sums, hidden_sums, sent = [], [], []
    for i in range(spans):
        *held, row_sum, hidden_sum, send = feed_forward(
            index, resids[i], resids_other[i], norms, ffn_in, lines, grad_hidden, held, tokens, i, spans
        )
        tokens = ()
        row_sums.append(row_sum)
        hidden_sums.append(hidden_sum)
        sent.append(send)
    hidden, grad_pre, normed_keep, normed_send, units, kept = held
    arrived = [to_chan(v) for v in sent]
    other_sums = [to_chan(v) for v in row_sums]

    def to_dp(values):
        return lax.ppermute(values, "dp", swap)

    def ready(keep, others, groups_at):
        half, size = keep.shape[0] // 2, others[0].shape[1]
        total = jnp.concatenate([keep[:half, g * size : (g + 1) * size] + others[g] for g in groups_at], axis=1)
        return total.reshape(groups // 2, -1, total.shape[1])

    def joined(keep, others, got, groups_at):
        half, size = keep.shape[0] // 2, others[0].shape[1]
        stay = others[len(others) // 2 :]
        total = jnp.concatenate([keep[half:, g * size : (g + 1) * size] + stay[g] for g in groups_at], axis=1)
        return total.reshape(got.shape) + got

    out_keep, out_send = weight_grad(
        index, groups, *grad_out_turned, hidden, (sent[1], arrived[0], other_sums[0])
    )
    out_other = [to_dp(v) for v in out_send]
    every = range(len(out_other) // 2)
    out_keep = tie(out_keep, arrived[1], other_sums[1])
    out_ready = [ready(out_keep, out_other, [g]) for g in every]

    grad_resid, grad_both, mixed_kept, norm_sums, glu_sums, *mixed_sent = glu_back(
        index,
        kept,
        units,
        jnp.broadcast_to(norm2_gain, (8, channels)),
        grad_out,
        glu_flat,
        arrived,
        row_sums,
        other_sums,
        values,
        gates,
        out_ready,
    )
    locals_flat = jnp.concatenate(
        [
            jnp.sum(glu_sums, axis=0),
            jnp.sum(norm_sums, axis=0),
            jnp.sum(sum(hidden_sums), axis=0),
        ]
    )
    out_got = [to_seq(v, steps[0]) for v in out_ready]
    out_first = joined(out_keep, out_other, tie(out_got[0], mixed_sent[1]), [0])
    in_keep, in_send = weight_grad(
        index, groups, normed_keep, normed_send, grad_pre, (mixed_sent[1], out_first)
    )
    in_other = [to_dp(v) for v in in_send]

    few = sequences // spans
    spread_spans = []
    tokens = (in_send[0],)
    for i, at in enumerate(spots):
        total = mixed_kept[:, at] + tie(to_chan(mixed_sent[i]), *tokens)
        moved = total.reshape(bands, groups, share, few, rows).swapaxes(0, 1)
        spread_spans.append(spread(moved))
        if not i:
            out_second = joined(out_keep, out_other, tie(out_got[1], moved), [1])
            in_keep = tie(in_keep, out_second)
            in_ready = ready(in_keep, in_other, every)
            glu_keep, glu_send = weight_grad(index, groups, *mixed_pair, grad_both, (in_ready,))
            glu_other = [to_dp(v) for v in glu_send]
            tokens = (glu_send[0], spread_spans[0])
    hidden = tie(hidden, out_keep, moved)
    output_send = contract(hidden, columns_other, 1, 0)
    glu_keep = tie(glu_keep, output_send)
    glu_other = [tie(v, output_send) for v in glu_other]
    glu_ready = ready(glu_keep, glu_other, [0])
    in_got = to_seq(in_ready, steps[0])
    out_half = jnp.concatenate([out_first, out_second], axis=2)
    out_more = halve(out_half, steps[1], output_send)
    in_half = joined(in_keep, in_other, tie(in_got, output_send), every)
    glu_got = to_seq(glu_ready, steps[0])
    grad_backs, backs, grad_kernels, conv_sums = [], [], [], []
    for i in range(bands):
        if i:
            before = grad_backs[0]
            out_most = halve(out_more, steps[2], before) if len(steps) > 2 else out_more
            glu_half = joined(glu_keep, glu_other, tie(glu_got, before), [0])
            tokens = (out_most, glu_half)
        else:
            tokens = (glu_ready, in_half, out_more)
        back, grad_kernel, conv_sum = long_conv_back(
            unit_parts[i], slope_parts[i], spread_spans, i, kernels_turned[i], tables[i], tokens
        )
        grad_backs.append(back)
        grad_kernels.append(grad_kernel)
        conv_sums.append(conv_sum)
    backs.append(spread(grad_backs[0]).reshape(band, count))

    grad_kernel = jnp.concatenate(grad_kernels, axis=0)
    pulled = jnp.einsum(
        "hdb,hnb->hnd",
        jnp.concatenate([grad_kernel, grad_kernel * fine_at], axis=1),
        fine,
        precision=highest,
        preferred_element_type=jnp.float32,
    )
    modes_count = freq.shape[1]
    flat_real, flat_imag = pulled[:, :modes_count, :groups], pulled[:, modes_count:, :groups]
    slant_real = pulled[:, :modes_count, groups:] + coarse_at * flat_real
    slant_imag = pulled[:, modes_count:, groups:] + coarse_at * flat_imag
    zero_real = jnp.sum(coarse_real * flat_real - coarse_imag * flat_imag, axis=2)
    zero_imag = jnp.sum(coarse_real * flat_imag + coarse_imag * flat_real, axis=2)
    one_real = jnp.sum(coarse_real * slant_real - coarse_imag * slant_imag, axis=2)
    one_imag = jnp.sum(coarse_real * slant_imag + coarse_imag * slant_real, axis=2)
    grad_step, grad_decay, grad_freq, grad_coef = modes_back(
        (
            2.0 * zero_real,
            -2.0 * zero_imag,
            2.0 * (weight_real * one_real - weight_imag * one_imag),
            -2.0 * (weight_real * one_imag + weight_imag * one_real),
        )
    )
    sums = jnp.sum(jnp.concatenate(conv_sums, axis=0), axis=2)
    states = jnp.concatenate(
        [grad_decay, grad_freq, grad_coef[0], grad_coef[1], sums[:, :3], grad_step[:, None]], axis=1
    )
    columns = states.shape[1]
    states = jnp.pad(states.reshape(-1), (0, -states.size % (8 * rows))).reshape(-1, rows)
    states_rows = states.shape[0]
    smalls = jnp.concatenate([states, locals_flat.reshape(-1, rows)], axis=0)
    smalls = smalls + to_dp(smalls)
    glu_more = halve(glu_half, steps[1], grad_backs[1])
    in_more = halve(in_half, steps[1], grad_backs[1])
    back = tie(grad_backs[1], backs[0], glu_more, in_more)
    backs.append(spread(back).reshape(band, count))
    last_step = steps[min(2, len(steps) - 1)]
    last_halves = [halves_of(v, last_step) for v in (in_more, glu_more)]
    smalls = jnp.broadcast_to(smalls, (groups, *smalls.shape))
    hidden = tie(hidden, output_send, back, smalls, *[v[1] for v in last_halves])
    output_keep = contract(hidden, columns_own, 1, 0)
    output = to_chan(output_send) + (
        output_keep + jnp.concatenate(resids, axis=0) + ffn_out_bias
    )
    smalls = spread(tie(smalls, backs[1], output))
    last_got = [to_seq(tie(v[1], backs[1], output), last_step) for v in last_halves]
    turned = tie(jnp.concatenate([v.reshape(band, count) for v in unit_turned], axis=0), backs[0])
    sums = [
        jnp.stack([jnp.sum(v, axis=0), jnp.sum(v * turned[i * band : (i + 1) * band], axis=0)])
        for i, v in enumerate(backs)
    ]
    sums = sum(sums).reshape(-1, rows)
    token_sums = (sums + to_chan(sums)).reshape(2, count)

    states = smalls[:, :states_rows].reshape(groups, -1)[:, : part * columns]
    states = states.reshape(groups, bands, share, columns).swapaxes(0, 1).reshape(channels, columns)
    states = tie(states.T, smalls).T
    locals_flat = jnp.sum(smalls[:, states_rows:], axis=0).reshape(-1)
    norm_rows = jnp.concatenate(
        [mean.reshape(1, count), scale1.reshape(1, count), token_sums, jnp.zeros((4, count), jnp.float32)],
        axis=0,
    )
    grad_inputs = first_norm_back(flat, grad_resid, norm_rows, backs, ())
    grad_ffn_out = finish(out_most, 3).T
    in_last, glu_last = [v[0] + tie(got, states, locals_flat) for v, got in zip(last_halves, last_got)]
    grad_ffn_in = finish(in_last, 3)
    grad_glu = finish(glu_last, 3)
    c = channels
    return (
        output.reshape(sequences, rows, channels),
        grad_inputs.reshape(sequences, rows, channels),
        states[:, 4 * modes_count],
        states[:, 4 * modes_count + 1],
        states[:, 4 * modes_count + 3],
        states[:, :modes_count],
        states[:, modes_count : 2 * modes_count],
        jnp.stack(
            [
                states[:, 2 * modes_count : 3 * modes_count],
                states[:, 3 * modes_count : 4 * modes_count],
            ]
        ),
        states[:, 4 * modes_count + 2],
        grad_glu.reshape(-1, 2, channels),
        locals_flat[: 2 * c].reshape(2, c),
        locals_flat[2 * c : 3 * c],
        locals_flat[3 * c : 4 * c],
        grad_ffn_in,
        locals_flat[5 * c :],
        grad_ffn_out,
        locals_flat[4 * c : 5 * c],
    )


def solution(mesh):
    placed = (
        P("dp", "seq", "chan"),
        P("dp", "seq", "chan"),
        P("chan"),
        P("chan"),
        P("chan"),
        P("chan", None),
        P("chan", None),
        P(None, "chan", None),
        P("chan"),
        P(None, None, "chan"),
        P(None, "chan"),
        P("chan"),
        P("chan"),
        P(None, "chan"),
        P("chan"),
        P("chan", None),
        P("chan"),
    )
    return jax.shard_map(
        body,
        mesh=mesh,
        in_specs=placed,
        out_specs=(
            P("dp", "seq", "chan"),
            P("dp", "seq", "chan"),
            P("chan"),
            P("chan"),
            P("chan"),
            P("chan", None),
            P("chan", None),
            P(None, "chan", None),
            P("chan"),
            P(("dp", "seq"), None, "chan"),
            P(None, "chan"),
            P("chan"),
            P("chan"),
            P(("dp", "seq"), "chan"),
            P("chan"),
            P("chan", ("dp", "seq")),
            P("chan"),
        ),
        check_vma=False,
    )
```

```python
from functools import partial

import jax
import jax.numpy as jnp
from jax import lax
from jax.experimental import pallas as pl
from jax.experimental.pallas import tpu as pltpu
from jax.sharding import PartitionSpec as P

epsilon = 1e-05
high = lax.Precision.HIGH
highest = lax.Precision.HIGHEST
swap = [(0, 1), (1, 0)]
anywhere = pl.BlockSpec(memory_space=pl.ANY)
window = 30


def tie(values, *earlier):
    def kernel(*refs):
        pass

    return pl.pallas_call(
        kernel,
        in_specs=[anywhere] * (1 + len(earlier)),
        out_specs=anywhere,
        out_shape=jax.ShapeDtypeStruct(values.shape, values.dtype),
        input_output_aliases={0: 0},
        name="tie",
    )(values, *earlier)


def split(values):
    first = values.astype(jnp.bfloat16)
    return (first, (values - first.astype(jnp.float32)).astype(jnp.bfloat16))


def dot(left, right):
    return jnp.dot(left, right, preferred_element_type=jnp.float32)


def contract(left, right, left_dim, right_dim):
    return lax.dot_general(
        left,
        right,
        (((left_dim,), (right_dim,)), ((), ())),
        precision=high,
        preferred_element_type=jnp.float32,
    )


def state_modes(log_step, decay_log, freq, out_coef):
    step = jnp.exp(log_step)[:, None]
    real_rate = -jnp.exp(decay_log)
    scaled_real = step * real_rate
    scaled_imag = step * freq
    minus_real = (
        jnp.expm1(scaled_real) * jnp.cos(scaled_imag) - 2.0 * jnp.sin(0.5 * scaled_imag) ** 2
    )
    minus_imag = jnp.exp(scaled_real) * jnp.sin(scaled_imag)
    modulus = real_rate * real_rate + freq * freq
    ratio_real = (minus_real * real_rate + minus_imag * freq) / modulus
    ratio_imag = (minus_imag * real_rate - minus_real * freq) / modulus
    weight_real = out_coef[0] * ratio_real - out_coef[1] * ratio_imag
    weight_imag = out_coef[0] * ratio_imag + out_coef[1] * ratio_real
    return (weight_real, weight_imag, scaled_real, scaled_imag)


def powers(positions, scaled_real, scaled_imag):
    where = positions[None, None, :]
    magnitude = jnp.exp(where * scaled_real[:, :, None])
    angle = where * scaled_imag[:, :, None]
    return (magnitude * jnp.cos(angle), magnitude * jnp.sin(angle))


def split(values):
    first = values.astype(jnp.bfloat16)
    return (first, (values - first.astype(jnp.float32)).astype(jnp.bfloat16))

def dot(left, right):
    return jnp.dot(left, right, preferred_element_type=jnp.float32)

def toeplitz_pair(line_ref, channel, lag, before, keep, turn):
    size, rows = keep.shape
    out = []
    for step in range(2):
        line = line_ref[channel, pl.ds(lag + step, 1), :]
        now = pltpu.roll(jnp.broadcast_to(line, (size, rows)), turn, 1, stride=1, stride_axis=0)
        out.append(jnp.where(keep, now, before))
        before = now
    high, low = split(jnp.concatenate(out, axis=1))
    return (jnp.concatenate([high, high, low, jnp.zeros_like(low)], axis=0), before)


def half_blocks(values, left):
    size = values.shape[1] // 2
    high = values.astype(jnp.bfloat16).astype(jnp.float32)
    low = values - high
    high_turned, low_turned = pltpu.roll(high, size, 1), pltpu.roll(low, size, 1)
    first = jnp.concatenate([jnp.where(left, high, low_turned), high], axis=1)
    second = jnp.concatenate([jnp.where(left, high_turned, low), high_turned], axis=1)
    return jnp.concatenate([first, second], axis=0).astype(jnp.bfloat16)


def conv_kernel(unit_ref, kernel_ref, table_ref, *rest):
    mixed_ref, slope_ref = rest[-2:]
    groups, block, sequences, rows = unit_ref.shape
    count, half = groups * sequences, rows // 2
    keep = lax.broadcasted_iota(jnp.int32, (half, rows), 1) >= lax.broadcasted_iota(
        jnp.int32, (half, rows), 0
    )
    left = lax.broadcasted_iota(jnp.int32, (count, rows), 1) < half

    def one(channel, carry):
        unit = unit_ref[:, channel].reshape(count, rows)
        gain = table_ref[channel, 0:1, :]
        bias = table_ref[channel, 1:2, :]
        skip = table_ref[channel, 2:3, :]
        normed = unit * gain + bias
        signal = half_blocks(normed, left)
        before = jnp.zeros((half, rows), jnp.float32)
        even, odd = [0.0] * groups, [0.0] * groups
        for lag in range(0, groups, 2):
            table, before = toeplitz_pair(kernel_ref, channel, lag, before, keep, 0)
            part = dot(signal, table)
            for step in range(2):
                lanes = slice(step * rows, (step + 1) * rows)
                for group in range(groups - lag - step):
                    at, to = group * sequences, group + lag + step
                    even[to] += part[at : at + sequences, lanes]
                    odd[to] += part[count + at : count + at + sequences, lanes]
        turned = pltpu.roll(jnp.concatenate(odd, axis=0), half, 1)
        late = jnp.concatenate(
            [jnp.zeros((sequences, rows), jnp.float32), turned[: count - sequences]], axis=0
        )
        inner = (
            jnp.concatenate(even, axis=0) + jnp.where(left, late, turned) + skip * normed
        )
        below = 0.5 + 0.5 * lax.erf(inner * 0.7071067811865476)
        density = 0.3989422804014327 * jnp.exp(-0.5 * inner * inner)
        mixed_ref[:, channel] = (inner * below).reshape(groups, sequences, rows)
        slope_ref[:, channel] = (below + inner * density).reshape(groups, sequences, rows)
        return carry

    lax.fori_loop(0, block, one, 0, unroll=block)


def conv_back_kernel(spans, unit_ref, slope_ref, kernel_ref, table_ref, *rest):
    grad_refs = rest[:spans]
    back_ref, lags_ref, sums_ref, cross_ref = rest[-4:]
    groups, block, sequences, rows = unit_ref.shape
    count, half = groups * sequences, rows // 2
    keep = (
        lax.broadcasted_iota(jnp.int32, (half, rows), 1)
        <= lax.broadcasted_iota(jnp.int32, (half, rows), 0) + half
    )
    left = lax.broadcasted_iota(jnp.int32, (count, rows), 1) < half
    line_at = lax.broadcasted_iota(jnp.int32, (8, rows), 1)
    tile_row = lax.broadcasted_iota(jnp.int32, (8, rows), 0)

    def diagonals(channel, carry):
        lines = [None] * groups
        for tile in range(half // 8):
            turned = []
            for lag in range(groups):
                now = cross_ref[
                    channel,
                    lag // 2,
                    8 * tile : 8 * tile + 8,
                    (lag % 2) * rows : (lag % 2 + 1) * rows,
                ]
                turned.append(pltpu.roll(now, rows - 8 * tile, 1) if tile else now)
            turned.append(jnp.zeros((8, rows), jnp.float32))
            for lag in range(groups):
                now = turned[lag]
                if tile:
                    now = jnp.where(line_at < rows - 8 * tile, now, turned[lag + 1])
                lines[lag] = now if lines[lag] is None else lines[lag] + now
        lines.append(jnp.zeros((8, rows), jnp.float32))
        for lag in range(groups):
            line = lines[lag]
            for bit in (1, 2, 4):
                line = jnp.where(tile_row & bit != 0, pltpu.roll(line, rows - bit, 1), line)
            lines[lag] = line
        for lag in range(groups):
            line = jnp.where(line_at + tile_row < rows, lines[lag], lines[lag + 1])
            lags_ref[channel, lag : lag + 1, :] = jnp.sum(line, axis=0, keepdims=True)
        return carry

    def one(channel, carry):
        unit = unit_ref[:, channel].reshape(count, rows)
        gain = table_ref[channel, 0:1, :]
        bias = table_ref[channel, 1:2, :]
        skip = table_ref[channel, 2:3, :]
        normed = unit * gain + bias
        grad = jnp.concatenate([ref[:, 0, channel] for ref in grad_refs], axis=1)
        grad = (grad * slope_ref[:, channel]).reshape(count, rows)
        nothing = jnp.zeros((sequences, rows), jnp.float32)
        signal = half_blocks(grad, left)
        turned = pltpu.roll(grad, half, 1)
        between = jnp.where(
            left, turned, jnp.concatenate([turned[sequences:], nothing], axis=0)
        )
        sides = jnp.concatenate([normed, pltpu.roll(normed, half, 1)], axis=0)
        sides, sides_low = split(sides.T[:half])
        sides = jnp.concatenate([sides, sides_low, sides], axis=1)
        before = jnp.zeros((half, rows), jnp.float32)
        even, odd = [0.0] * groups, [0.0] * groups
        for lag in range(0, groups, 2):
            table, before = toeplitz_pair(kernel_ref, channel, lag, before, keep, half)
            part = dot(signal, table)
            moved = []
            for step in range(2):
                lanes = slice(step * rows, (step + 1) * rows)
                shift = (lag + step) * sequences
                for group in range(groups - lag - step):
                    at = group * sequences + shift
                    even[group] += part[at : at + sequences, lanes]
                    odd[group] += part[count + at : count + at + sequences, lanes]
                pad = [jnp.zeros((shift, rows), jnp.float32)] if shift else []
                moved.append(
                    jnp.concatenate([grad[shift:], *pad, between[shift:], *pad], axis=0)
                )
            right, right_low = split(jnp.concatenate(moved, axis=1))
            cross_ref[channel, lag // 2] = dot(
                sides, jnp.concatenate([right, right, right_low], axis=0)
            )
        turned = pltpu.roll(jnp.concatenate(even, axis=0), half, 1)
        early = jnp.concatenate([turned[sequences:], nothing], axis=0)
        total = jnp.concatenate(odd, axis=0) + jnp.where(left, turned, early) + skip * grad
        back_ref[:, channel] = (total * gain).reshape(groups, sequences, rows)
        sums_ref[channel, 0:1, :] = jnp.sum(total * unit, axis=0, keepdims=True)
        sums_ref[channel, 1:2, :] = jnp.sum(total, axis=0, keepdims=True)
        sums_ref[channel, 2:3, :] = jnp.sum(grad * normed, axis=0, keepdims=True)
        sums_ref[channel, 3:8, :] = jnp.zeros((5, rows), jnp.float32)
        return carry

    lax.fori_loop(0, block, one, 0, unroll=min(4, block))
    lax.fori_loop(0, block, diagonals, 0, unroll=min(2, block))


def channel_blocks(groups, part):
    block = max(1, 64 // groups)
    return block if part % block == 0 else 1


def long_conv(unit, kernel, table, tokens):
    groups, part, sequences, rows = unit.shape
    block = channel_blocks(groups, part)
    wide = pl.BlockSpec((groups, block, sequences, rows), lambda i: (0, i, 0, 0))
    return pl.pallas_call(
        conv_kernel,
        grid=(part // block,),
        in_specs=[
            wide,
            pl.BlockSpec((block, groups, rows), lambda i: (i, 0, 0)),
            pl.BlockSpec((block, 8, rows), lambda i: (i, 0, 0)),
        ]
        + [anywhere] * len(tokens),
        out_specs=[wide, wide],
        out_shape=[jax.ShapeDtypeStruct(unit.shape, jnp.float32)] * 2,
        compiler_params=pltpu.CompilerParams(vmem_limit_bytes=48 * 1024 * 1024),
        cost_estimate=pl.CostEstimate(
            flops=part * groups * groups * sequences * rows * rows * 6 * window,
            bytes_accessed=12 * unit.size,
            transcendentals=2 * unit.size,
        ),
        name="conv_forward",
    )(unit, kernel, table, *tokens)

def long_conv_back(unit, slope, grads, band, kernel, table, tokens):
    groups, part, sequences, rows = unit.shape
    block = channel_blocks(groups, part)
    wide = pl.BlockSpec((groups, block, sequences, rows), lambda i: (0, i, 0, 0))
    lags = pl.BlockSpec((block, groups, rows), lambda i: (i, 0, 0))
    few = pl.BlockSpec((block, 8, rows), lambda i: (i, 0, 0))
    return pl.pallas_call(
        partial(conv_back_kernel, len(grads)),
        grid=(part // block,),
        in_specs=[wide, wide, lags, few]
        + [pl.BlockSpec((groups, 1, block, *v.shape[3:]), lambda i: (0, band, i, 0, 0)) for v in grads]
        + [anywhere] * len(tokens),
        out_specs=[wide, lags, few],
        out_shape=[
            jax.ShapeDtypeStruct(unit.shape, jnp.float32),
            jax.ShapeDtypeStruct(kernel.shape, jnp.float32),
            jax.ShapeDtypeStruct((part, 8, rows), jnp.float32),
        ],
        scratch_shapes=[pltpu.VMEM((block, groups // 2, rows // 2, 2 * rows), jnp.float32)],
        compiler_params=pltpu.CompilerParams(vmem_limit_bytes=48 * 1024 * 1024),
        cost_estimate=pl.CostEstimate(
            flops=part * groups * groups * sequences * rows * rows * 12 * window,
            bytes_accessed=16 * unit.size,
            transcendentals=0,
        ),
        name="conv_backward",
    )(unit, slope, kernel, table, *grads, *tokens)


def turned_dot(left, right):
    return lax.dot_general(
        left, right, (((1,), (1,)), ((), ())), preferred_element_type=jnp.float32
    )


def feed_forward_kernel(
    index_ref, resid_ref, other_ref, norm_ref, weight_ref, line_ref, back_ref, *rest
):
    (
        hidden_ref,
        grad_ref,
        keep_ref,
        send_ref,
        unit_ref,
        kept_ref,
        sums_ref,
        bias_ref,
        sent_ref,
        high_ref,
        low_ref,
        total_ref,
    ) = rest[-12:]
    count, channels = resid_ref.shape
    step = pl.program_id(0)
    own_at = pl.ds(pl.multiple_of(index_ref[0] * channels, channels), channels)
    other_at = pl.ds(pl.multiple_of((1 - index_ref[0]) * channels, channels), channels)

    @pl.when(step == 0)
    def _():
        resid, other = resid_ref[...], other_ref[...]
        width = 2.0 * channels
        mean = (
            jnp.sum(resid, axis=1, keepdims=True) + jnp.sum(other, axis=1, keepdims=True)
        ) / width
        squares = jnp.sum(resid * resid, axis=1, keepdims=True) + jnp.sum(
            other * other, axis=1, keepdims=True
        )
        scale = lax.rsqrt(squares / width - mean * mean + epsilon)
        lane = lax.broadcasted_iota(jnp.int32, (count, 128), 1)
        sums_ref[...] = jnp.where(lane == 2, scale, 0.0)
        total_ref[...] = jnp.zeros(total_ref.shape, jnp.float32)
        unit = (resid - mean) * scale
        unit_ref[...] = unit
        same = index_ref[1] == 1
        for values, at, first in (
            (unit, own_at, same),
            ((other - mean) * scale, other_at, jnp.logical_not(same)),
        ):
            normed = values * norm_ref[0:1, at] + norm_ref[1:2, at]
            high, low = split(normed)
            high_ref[:, at] = high
            low_ref[:, at] = low

            @pl.when(first)
            def _():
                keep_ref[...] = normed.T

            @pl.when(jnp.logical_not(first))
            def _():
                send_ref[...] = normed.T

    weight, weight_low = split(weight_ref[...])
    size = weight.shape[1]
    total = jnp.zeros((8, size), jnp.float32)
    chunk = min(count, 256)
    for start in range(0, count, chunk):
        at = slice(start, start + chunk)
        high, low = high_ref[at], low_ref[at]
        pre = dot(high, weight) + dot(low, weight) + dot(high, weight_low) + line_ref[0:1]
        below = 0.5 + 0.5 * lax.erf(pre * 0.7071067811865476)
        density = 0.3989422804014327 * jnp.exp(-0.5 * pre * pre)
        hidden_ref[at] = pre * below
        grad = back_ref[at] * (below + pre * density)
        grad_ref[at] = grad
        total = total + jnp.sum(grad.reshape(chunk // 8, 8, size), axis=0)
        first = jnp.sum(grad * line_ref[1:2], axis=1, keepdims=True)
        second = jnp.sum(grad * (pre - line_ref[2:3]), axis=1, keepdims=True)
        lane = lax.broadcasted_iota(jnp.int32, (chunk, 128), 1)
        sums_ref[at] += jnp.where(lane == 0, first, jnp.where(lane == 1, second, 0.0))
        high, low = split(grad)
        total_ref[at] += (
            turned_dot(high, weight) + turned_dot(low, weight) + turned_dot(high, weight_low)
        )
    bias_ref[...] = total

    @pl.when(step == pl.num_programs(0) - 1)
    def _():
        kept_ref[...] = total_ref[:, own_at]
        sent_ref[:, :channels] = total_ref[:, other_at]
        sent_ref[:, channels:] = sums_ref[...]


def feed_forward(index, resid, other, norm, weight, lines, back, held, tokens, place, spans):
    count, channels = resid.shape
    width, hidden = weight.shape
    size = min(512, hidden)
    full = spans * count
    held = list(held)

    def whole(j, c):
        return (0, 0)

    wide = pl.BlockSpec((count, size), lambda j, c: (place, j))
    narrow = pl.BlockSpec((count, channels), whole)
    turned = pl.BlockSpec((channels, count), lambda j, c: (0, place))
    spot = pl.BlockSpec((count, channels), lambda j, c: (place, 0))
    return pl.pallas_call(
        feed_forward_kernel,
        grid_spec=pltpu.PrefetchScalarGridSpec(
            num_scalar_prefetch=1,
            grid=(hidden // size,),
            in_specs=[
                narrow,
                narrow,
                pl.BlockSpec((8, width), whole),
                pl.BlockSpec((width, size), lambda j, c: (0, j)),
                pl.BlockSpec((8, size), lambda j, c: (0, j)),
                wide,
            ]
            + [anywhere] * (len(held) + len(tokens)),
            out_specs=[
                wide,
                wide,
                turned,
                turned,
                spot,
                spot,
                pl.BlockSpec((count, 128), whole),
                pl.BlockSpec((8, size), lambda j, c: (0, j)),
                pl.BlockSpec((count, channels + 128), whole),
            ],
            scratch_shapes=[
                pltpu.VMEM((count, width), jnp.bfloat16),
                pltpu.VMEM((count, width), jnp.bfloat16),
                pltpu.VMEM((count, width), jnp.float32),
            ],
        ),
        out_shape=[
            jax.ShapeDtypeStruct(shape, jnp.float32)
            for shape in (
                (full, hidden),
                (full, hidden),
                (channels, full),
                (channels, full),
                (full, channels),
                (full, channels),
                (count, 128),
                (8, hidden),
                (count, channels + 128),
            )
        ],
        input_output_aliases={7 + i: i for i in range(len(held))},
        compiler_params=pltpu.CompilerParams(vmem_limit_bytes=56 * 1024 * 1024),
        cost_estimate=pl.CostEstimate(
            flops=count * width * hidden * 12 * window,
            bytes_accessed=4 * (width * hidden + 3 * count * hidden + 8 * count * channels),
            transcendentals=2 * count * hidden,
        ),
        name="feed_forward",
    )(index, resid, other, norm, weight, lines, back, *held, *tokens)


def weight_kernel(rows, turns, index_ref, keep_ref, send_ref, right_ref, *rest):
    high_ref, low_ref = rest[-2:]
    kept_ref, *sent_refs = rest[-3 - turns : -2]
    parts_of = max(1, turns // 2)
    size = keep_ref.shape[0]
    turn = pl.program_id(0)

    @pl.when(turn == 0)
    def _():
        for at, ref in ((0, send_ref), (size, keep_ref)):
            high, low = split(ref[...])
            high_ref[at : at + size] = high
            low_ref[at : at + size] = low

    right, right_low = split(right_ref[...])
    chunk = min(size, 256)

    def parts(at, place):
        for start in range(0, size, chunk):
            rows_at = slice(at + start, at + start + chunk)
            left, left_low = high_ref[rows_at], low_ref[rows_at]
            part = dot(left, right) + dot(left_low, right) + dot(left, right_low)
            for first in range(0, chunk, rows):
                block = (start + first) // rows
                place(block, part[first : first + rows])

    def keep(block, values):
        stays = (block % 2 == index_ref[2]).astype(jnp.int32)
        to = pl.multiple_of(stays * (size // 2) + block // 2 * rows, rows)
        kept_ref[pl.ds(to, rows)] = values

    parts(size, keep)
    for piece in range(turns):
        group, lane = piece // 2, piece % 2 * right.shape[1]

        def send(block, values):
            at = (pl.ds(block // 2 * rows, rows), pl.ds(lane, values.shape[1]))
            goes = block % 2 != index_ref[2]

            @pl.when(goes)
            def _():
                sent_refs[group][at] = values

            @pl.when(jnp.logical_not(goes))
            def _():
                sent_refs[parts_of + group][at] = values

        @pl.when(turn == piece)
        def _():
            parts(0, send)


def weight_grad(index, groups, keep, send, right, tokens):
    size, depth = keep.shape
    columns = right.shape[1]
    block = min(512, columns)
    turns = columns // block
    whole = pl.BlockSpec((size, depth), lambda j, c: (0, 0))
    kept, *sent = pl.pallas_call(
        partial(weight_kernel, size // groups, turns),
        grid_spec=pltpu.PrefetchScalarGridSpec(
            num_scalar_prefetch=1,
            grid=(turns,),
            in_specs=[whole, whole, pl.BlockSpec((depth, block), lambda j, c: (0, j))]
            + [anywhere] * len(tokens),
            out_specs=[pl.BlockSpec((size, block), lambda j, c: (0, j))]
            + [pl.BlockSpec((size // 2, 2 * block), lambda j, c: (0, 0))] * turns,
            scratch_shapes=[pltpu.VMEM((2 * size, depth), jnp.bfloat16)] * 2,
        ),
        out_shape=[jax.ShapeDtypeStruct((size, columns), jnp.float32)]
        + [jax.ShapeDtypeStruct((size // 2, 2 * block), jnp.float32)] * turns,
        compiler_params=pltpu.CompilerParams(vmem_limit_bytes=56 * 1024 * 1024),
        cost_estimate=pl.CostEstimate(
            flops=12 * window * size * depth * columns,
            bytes_accessed=4 * (2 * size * depth + depth * columns + 2 * size * columns),
            transcendentals=0,
        ),
        name="weight_gradient",
    )(index, keep, send, right, *tokens)
    return (kept, sent)


def glu_back_kernel(spans, index_ref, keep_ref, unit_ref, norm_ref, grad_ref, weight_ref, *rest):
    by_span = [rest[i * spans : (i + 1) * spans] for i in range(4)]
    out = rest[-(7 + spans) :]
    resid_ref, both_ref, kept_ref, gain_ref, bias_ref = out[:5]
    sent_refs = out[5 : 5 + spans]
    high_ref, low_ref = out[5 + spans :]
    full, channels = keep_ref.shape
    count = full // spans
    width = 2.0 * channels

    @pl.when(pl.program_id(0) == 0)
    def _():
        chunk = min(count, 128)
        gains = jnp.zeros((8, channels), jnp.float32)
        biases, value_sums, gate_sums, grad_sums = gains, gains, gains, gains

        def fold(values):
            return jnp.sum(values.reshape(chunk // 8, 8, channels), axis=0)

        for start in range(0, full, chunk):
            at = slice(start, start + chunk)
            span, local = start // count, slice(start % count, start % count + chunk)
            other, own_sums, value, gate = [refs[span][local] for refs in by_span]
            grad_normed = keep_ref[at] + other[:, :channels]
            sums = own_sums + other[:, channels:]
            total, along, scale = sums[:, 0:1], sums[:, 1:2], own_sums[:, 2:3]
            unit = unit_ref[at]
            grad_resid = grad_ref[at] + scale * (
                grad_normed * norm_ref[0:1] - total / width - unit * (along / width)
            )
            resid_ref[at] = grad_resid
            grad_value = grad_resid * gate
            grad_gate = grad_value * value * (1.0 - gate)
            gains = gains + fold(grad_normed * unit)
            biases = biases + fold(grad_normed)
            value_sums = value_sums + fold(grad_value)
            gate_sums = gate_sums + fold(grad_gate)
            grad_sums = grad_sums + fold(grad_ref[at])
            for first, values in ((0, grad_value), (channels, grad_gate)):
                lanes = slice(first, first + channels)
                both_ref[at, lanes] = values
                high, low = split(values)
                high_ref[at, lanes] = high
                low_ref[at, lanes] = low
        gain_ref[:, :channels] = gains
        gain_ref[:, channels : 2 * channels] = biases
        gain_ref[:, 2 * channels :] = grad_sums
        bias_ref[:, :channels] = value_sums
        bias_ref[:, channels:] = gate_sums

    weight, weight_low = split(weight_ref[...])
    sending = pl.program_id(0) < pl.num_programs(0) // 2
    for span in range(spans):
        at = slice(span * count, (span + 1) * count)
        high = high_ref[at]
        mixed = (
            turned_dot(weight, high) + turned_dot(weight, low_ref[at]) + turned_dot(weight_low, high)
        )

        @pl.when(sending)
        def _():
            sent_refs[span][...] = mixed

        @pl.when(jnp.logical_not(sending))
        def _():
            kept_ref[:, at] = mixed


def glu_back(index, keep, unit, norm, grad, weight, others, sums, values, gates, tokens):
    full, channels = keep.shape
    width, columns = weight.shape
    spans = len(others)
    count = full // spans
    block = min(256, channels)
    turns = channels // block

    def whole(j, c):
        return (0, 0)

    def rows_at(j, c):
        return (jnp.where(j < turns, (1 - c[0]) * turns + j, (c[0] - 1) * turns + j), 0)

    wide = pl.BlockSpec((full, channels), whole)
    span_wide = pl.BlockSpec((count, channels), whole)
    span_few = pl.BlockSpec((count, 128), whole)
    few = pl.BlockSpec((8, columns), whole)
    return pl.pallas_call(
        partial(glu_back_kernel, spans),
        grid_spec=pltpu.PrefetchScalarGridSpec(
            num_scalar_prefetch=1,
            grid=(2 * turns,),
            in_specs=[wide, wide, pl.BlockSpec((8, channels), whole), wide]
            + [pl.BlockSpec((block, columns), rows_at)]
            + [pl.BlockSpec((count, channels + 128), whole)] * spans
            + ([span_few] * spans + [span_wide] * (2 * spans))
            + [anywhere] * len(tokens),
            out_specs=[
                wide,
                pl.BlockSpec((full, columns), whole),
                pl.BlockSpec((block, full), lambda j, c: (jnp.maximum(j - turns, 0), 0)),
                pl.BlockSpec((8, 3 * channels), whole),
                few,
            ]
            + [pl.BlockSpec((block, count), lambda j, c: (jnp.minimum(j, turns - 1), 0))] * spans,
            scratch_shapes=[pltpu.VMEM((full, columns), jnp.bfloat16)] * 2,
        ),
        out_shape=[
            jax.ShapeDtypeStruct(shape, jnp.float32)
            for shape in (
                (full, channels),
                (full, columns),
                (channels, full),
                (8, 3 * channels),
                (8, columns),
            )
            + ((channels, count),) * spans
        ],
        compiler_params=pltpu.CompilerParams(vmem_limit_bytes=60 * 1024 * 1024),
        cost_estimate=pl.CostEstimate(
            flops=6 * window * full * width * columns,
            bytes_accessed=4 * (11 * full * channels + width * columns),
            transcendentals=0,
        ),
        name="glu_backward",
    )(
        index,
        keep,
        unit,
        norm,
        grad,
        weight,
        *others,
        *sums,
        *values,
        *gates,
        *tokens,
    )


def first_norm_kernel(inputs_ref, resid_ref, rows_ref, *rest):
    out_ref = rest[-1]
    bands = len(rest) // 2
    channels = inputs_ref.shape[1]
    width = 2.0 * channels
    columns = rows_ref[...].T
    mean, scale, total, along = [columns[:, i : i + 1] for i in range(4)]
    for band in range(bands):
        scaled = rest[band][...].T
        lanes = slice(band * scaled.shape[1], (band + 1) * scaled.shape[1])
        unit = (inputs_ref[:, lanes] - mean) * scale
        out_ref[:, lanes] = resid_ref[:, lanes] + scale * (
            scaled - total / width - unit * (along / width)
        )


def first_norm_back(inputs, resid, rows, backs, tokens):
    count, channels = inputs.shape
    block = min(256, count)
    wide = pl.BlockSpec((block, channels), lambda j: (j, 0))
    bands = [pl.BlockSpec((v.shape[0], block), lambda j: (0, j)) for v in backs]
    tokens = list(tokens) + [backs[0]] * (len(backs) - len(tokens))
    return pl.pallas_call(
        first_norm_kernel,
        grid=(count // block,),
        in_specs=[wide, wide, pl.BlockSpec((8, block), lambda j: (0, j))]
        + bands
        + [anywhere] * len(tokens),
        out_specs=wide,
        out_shape=jax.ShapeDtypeStruct((count, channels), jnp.float32),
        compiler_params=pltpu.CompilerParams(vmem_limit_bytes=32 * 1024 * 1024),
        name="first_norm_backward",
    )(inputs, resid, rows, *backs, *tokens)


def body(
    inputs,
    cotangent,
    norm1_gain,
    norm1_bias,
    log_step,
    decay_log,
    freq,
    out_coef,
    skip,
    glu_weight,
    glu_bias,
    norm2_gain,
    norm2_bias,
    ffn_in,
    ffn_in_bias,
    ffn_out,
    ffn_out_bias,
):
    sequences, rows, channels = inputs.shape
    groups = lax.axis_size("seq")
    seq_index = lax.axis_index("seq")
    chan_index = lax.axis_index("chan")
    dp_index = lax.axis_index("dp")
    width = channels * lax.axis_size("chan")
    count = sequences * rows
    part = channels // groups
    steps = [1 << bit for bit in range(groups.bit_length() - 1)]
    bands = 2
    band = channels // bands
    share = part // bands
    spans = 2
    span = count // spans
    spots = [slice(i * span, (i + 1) * span) for i in range(spans)]

    def to_chan(values):
        return lax.ppermute(values, "chan", swap)

    def to_seq(values, step):
        return lax.ppermute(values, "seq", [(a, a ^ step) for a in range(groups)])

    def spread(values):
        return lax.all_to_all(values, "seq", 0, 0, tiled=True)

    def own_part(values, dim):
        pieces = [
            lax.dynamic_slice_in_dim(values, i * band + seq_index * share, share, dim)
            for i in range(bands)
        ]
        return jnp.concatenate(pieces, axis=dim)

    def in_order(own, other):
        first = chan_index == 0
        return jnp.concatenate(
            [jnp.where(first, own, other), jnp.where(first, other, own)], axis=1
        )

    def halve(values, step, *earlier):
        pairs = values.reshape(-1, 2, *values.shape[1:])
        mine = (seq_index & step) // step
        keep = lax.dynamic_index_in_dim(pairs, mine, 1, keepdims=False)
        send = lax.dynamic_index_in_dim(pairs, 1 - mine, 1, keepdims=False)
        got = to_seq(send, step)
        return keep + (tie(got, *earlier) if earlier else got)

    def finish(values, start, *earlier):
        for step in steps[start:]:
            values = halve(values, step, *earlier)
        return values[0]

    def halves_of(values, step):
        pairs = values.reshape(-1, 2, *values.shape[1:])
        mine = (seq_index & step) // step
        return [lax.dynamic_index_in_dim(pairs, at, 1, keepdims=False) for at in (mine, 1 - mine)]

    own_at = chan_index * channels
    other_at = channels - own_at

    flat = inputs.reshape(count, channels)
    grad_out = cotangent.reshape(count, channels)
    stats = jnp.concatenate([jnp.sum(inputs, axis=2), jnp.sum(inputs * inputs, axis=2)], axis=0)
    stats = lax.psum(stats, "chan")
    mean = stats[:sequences] / width
    scale1 = lax.rsqrt(stats[sequences:] / width - mean * mean + epsilon).reshape(count, 1)
    unit1 = (flat - mean.reshape(count, 1)) * scale1
    grad_out_other = to_chan(tie(grad_out, stats))
    same = chan_index == dp_index
    index = jnp.stack([chan_index, same.astype(jnp.int32), seq_index & 1]).astype(jnp.int32)

    def kept_and_sent(own, other):
        return (jnp.where(same, own, other), jnp.where(same, other, own))

    columns_own = lax.dynamic_slice_in_dim(ffn_out, own_at, channels, 1)
    columns_other = lax.dynamic_slice_in_dim(ffn_out, other_at, channels, 1)
    grad_hidden = contract(grad_out, columns_own, 1, 1)
    grad_hidden_own = grad_hidden
    grad_hidden = grad_hidden + contract(grad_out_other, columns_other, 1, 1)
    norms = jnp.stack([norm2_gain, norm2_bias] + [jnp.zeros((channels,), jnp.float32)] * 6)
    norms = in_order(norms, to_chan(tie(norms, grad_out_other)))
    lines = jnp.dot(norms, ffn_in, precision=highest, preferred_element_type=jnp.float32)
    lines = jnp.stack(
        [ffn_in_bias, lines[0], ffn_in_bias + lines[1]] + [jnp.zeros_like(ffn_in_bias)] * 5
    )

    modes, modes_back = jax.vjp(
        state_modes,
        own_part(log_step, 0),
        own_part(decay_log, 0),
        own_part(freq, 0),
        own_part(out_coef, 1),
    )
    weight_real, weight_imag, scaled_real, scaled_imag = modes
    fine_at = jnp.arange(rows, dtype=jnp.int32).astype(jnp.float32)
    coarse_at = (jnp.arange(groups, dtype=jnp.int32) * rows).astype(jnp.float32)
    fine_real, fine_imag = powers(fine_at, scaled_real, scaled_imag)
    coarse_real, coarse_imag = powers(coarse_at, scaled_real, scaled_imag)
    fine = jnp.concatenate([fine_real, fine_imag], axis=1)
    start_real = weight_real[:, :, None] * coarse_real - weight_imag[:, :, None] * coarse_imag
    start_imag = weight_real[:, :, None] * coarse_imag + weight_imag[:, :, None] * coarse_real
    kernel = 2.0 * jnp.einsum(
        "hnd,hnb->hdb",
        jnp.concatenate([start_real, -start_imag], axis=1),
        fine,
        precision=highest,
        preferred_element_type=jnp.float32,
    )
    table = jnp.stack(
        [own_part(norm1_gain, 0), own_part(norm1_bias, 0), own_part(skip, 0)]
        + [jnp.zeros((part,), jnp.float32)] * 5,
        axis=1,
    )
    table = jnp.broadcast_to(table[:, :, None], (part, 8, rows))
    kernel_turned = jnp.roll(kernel[:, :, ::-1], 1, axis=2)
    kernels_turned = [kernel_turned[i * share : (i + 1) * share] for i in range(bands)]
    kernels = [kernel[i * share : (i + 1) * share] for i in range(bands)]
    tables = [table[i * share : (i + 1) * share] for i in range(bands)]

    unit_parts, unit_turned, slope_parts, mixed, mixed_other = [], [], [], [], []
    for i in range(bands):
        turned = unit1[:, i * band : (i + 1) * band].T.reshape(groups, share, sequences, rows)
        unit_turned.append(turned)
        unit_parts.append(spread(tie(turned, kernel, grad_hidden_own) if i else turned))
    for i in range(bands):
        tokens = (grad_hidden, lines) if i else ()
        mixed_part, slope_part = long_conv(unit_parts[i], kernels[i], tables[i], tokens)
        slope_parts.append(slope_part)
        arrived = spread(mixed_part).reshape(band, count)
        if i:
            arrived = tie(arrived, mixed_other[0])
        mixed.append(arrived)
        mixed_other.append(to_chan(arrived))

    glu_flat = glu_weight.reshape(width, 2 * channels)
    glu_own = lax.dynamic_slice_in_dim(glu_flat, own_at, channels, 0)
    glu_rows_other = lax.dynamic_slice_in_dim(glu_flat, other_at, channels, 0)
    both_held = glu_bias.reshape(1, 2 * channels)
    for i in range(bands):
        both_held = both_held + contract(mixed[i], glu_own[i * band : (i + 1) * band], 0, 0)
    for i in range(bands - 1):
        both_held = both_held + contract(mixed_other[i], glu_rows_other[i * band : (i + 1) * band], 0, 0)
    values, gates, resids, resids_other = [], [], [], []
    for at in spots:
        both = both_held[at] + contract(
            mixed_other[-1][:, at], glu_rows_other[(bands - 1) * band :], 0, 0
        )
        values.append(both[:, :channels])
        gates.append(jax.nn.sigmoid(both[:, channels:]))
        resids.append(flat[at] + values[-1] * gates[-1])
        resids_other.append(to_chan(resids[-1]))

    grad_out_turned = [v.T for v in kept_and_sent(grad_out, tie(grad_out_other, resids[1]))]
    mixed_pair = kept_and_sent(
        jnp.concatenate(mixed, axis=0), tie(jnp.concatenate(mixed_other, axis=0), resids[1])
    )
    held, tokens = (), (*grad_out_turned, *mixed_pair, *kernels_turned)
    row_sums, hidden_sums, sent = [], [], []
    for i in range(spans):
        *held, row_sum, hidden_sum, send = feed_forward(
            index, resids[i], resids_other[i], norms, ffn_in, lines, grad_hidden, held, tokens, i, spans
        )
        tokens = ()
        row_sums.append(row_sum)
        hidden_sums.append(hidden_sum)
        sent.append(send)
    hidden, grad_pre, normed_keep, normed_send, units, kept = held
    arrived = [to_chan(v) for v in sent]

    def to_dp(values):
        return lax.ppermute(values, "dp", swap)

    def ready(keep, others, groups_at):
        half, size = keep.shape[0] // 2, others[0].shape[1]
        total = jnp.concatenate([keep[:half, g * size : (g + 1) * size] + others[g] for g in groups_at], axis=1)
        return total.reshape(groups // 2, -1, total.shape[1])

    def joined(keep, others, got, groups_at):
        half, size = keep.shape[0] // 2, others[0].shape[1]
        stay = others[len(others) // 2 :]
        total = jnp.concatenate([keep[half:, g * size : (g + 1) * size] + stay[g] for g in groups_at], axis=1)
        return total.reshape(got.shape) + got

    out_keep, out_send = weight_grad(
        index, groups, *grad_out_turned, hidden, (sent[1], arrived[0])
    )
    out_other = [to_dp(v) for v in out_send]
    every = range(len(out_other) // 2)
    out_keep = tie(out_keep, arrived[1])
    out_ready = [ready(out_keep, out_other, [g]) for g in every]

    grad_resid, grad_both, mixed_kept, norm_sums, glu_sums, *mixed_sent = glu_back(
        index,
        kept,
        units,
        jnp.broadcast_to(norm2_gain, (8, channels)),
        grad_out,
        glu_flat,
        arrived,
        row_sums,
        values,
        gates,
        out_ready,
    )
    locals_flat = jnp.concatenate(
        [
            jnp.sum(glu_sums, axis=0),
            jnp.sum(norm_sums, axis=0),
            jnp.sum(sum(hidden_sums), axis=0),
        ]
    )
    out_got = [to_seq(v, steps[0]) for v in out_ready]
    out_stay = [tie(v, mixed_sent[1]) for v in out_other]
    out_first = joined(out_keep, out_stay, tie(out_got[0], mixed_sent[1]), [0])
    in_keep, in_send = weight_grad(
        index, groups, normed_keep, normed_send, grad_pre, (mixed_sent[1], out_first)
    )
    in_other = [to_dp(v) for v in in_send]

    few = sequences // spans
    spread_spans = []
    tokens = (in_send[0],)
    for i, at in enumerate(spots):
        total = mixed_kept[:, at] + tie(to_chan(mixed_sent[i]), *tokens)
        moved = total.reshape(bands, groups, share, few, rows).swapaxes(0, 1)
        spread_spans.append(spread(moved))
        if not i:
            out_second = joined(out_keep, out_stay, tie(out_got[1], moved), [1])
            in_keep = tie(in_keep, out_second)
            in_ready = ready(in_keep, in_other, every)
            glu_keep, glu_send = weight_grad(index, groups, *mixed_pair, grad_both, (in_ready,))
            glu_other = [to_dp(v) for v in glu_send]
            tokens = (glu_send[0], spread_spans[0])
    hidden = tie(hidden, out_keep, moved)
    output_send = contract(hidden, columns_other, 1, 0)
    glu_keep = tie(glu_keep, output_send)
    glu_other = [tie(v, output_send) for v in glu_other]
    glu_ready = ready(glu_keep, glu_other, [0])
    in_got = to_seq(in_ready, steps[0])
    out_half = jnp.concatenate([out_first, out_second], axis=2)
    out_more = halve(out_half, steps[1], output_send)
    in_half = joined(in_keep, in_other, tie(in_got, output_send), every)
    glu_got = to_seq(glu_ready, steps[0])
    grad_backs, backs, grad_kernels, conv_sums = [], [], [], []
    for i in range(bands):
        if i:
            before = grad_backs[0]
            out_most = halve(out_more, steps[2], before) if len(steps) > 2 else out_more
            glu_half = joined(glu_keep, glu_other, tie(glu_got, before), [0])
            tokens = (out_most, glu_half)
        else:
            tokens = (glu_ready, in_half, out_more)
        back, grad_kernel, conv_sum = long_conv_back(
            unit_parts[i], slope_parts[i], spread_spans, i, kernels_turned[i], tables[i], tokens
        )
        grad_backs.append(back)
        grad_kernels.append(grad_kernel)
        conv_sums.append(conv_sum)
    backs.append(spread(grad_backs[0]).reshape(band, count))

    back = tie(grad_backs[1], backs[0])
    grad_kernels[1] = tie(grad_kernels[1], back)
    grad_kernel = jnp.concatenate(grad_kernels, axis=0)
    pulled = jnp.einsum(
        "hdb,hnb->hnd",
        jnp.concatenate([grad_kernel, grad_kernel * fine_at], axis=1),
        fine,
        precision=highest,
        preferred_element_type=jnp.float32,
    )
    modes_count = freq.shape[1]
    flat_real, flat_imag = pulled[:, :modes_count, :groups], pulled[:, modes_count:, :groups]
    slant_real = pulled[:, :modes_count, groups:] + coarse_at * flat_real
    slant_imag = pulled[:, modes_count:, groups:] + coarse_at * flat_imag
    zero_real = jnp.sum(coarse_real * flat_real - coarse_imag * flat_imag, axis=2)
    zero_imag = jnp.sum(coarse_real * flat_imag + coarse_imag * flat_real, axis=2)
    one_real = jnp.sum(coarse_real * slant_real - coarse_imag * slant_imag, axis=2)
    one_imag = jnp.sum(coarse_real * slant_imag + coarse_imag * slant_real, axis=2)
    grad_step, grad_decay, grad_freq, grad_coef = modes_back(
        (
            2.0 * zero_real,
            -2.0 * zero_imag,
            2.0 * (weight_real * one_real - weight_imag * one_imag),
            -2.0 * (weight_real * one_imag + weight_imag * one_real),
        )
    )
    sums = jnp.sum(jnp.concatenate(conv_sums, axis=0), axis=2)
    states = jnp.concatenate(
        [grad_decay, grad_freq, grad_coef[0], grad_coef[1], sums[:, :3], grad_step[:, None]], axis=1
    )
    columns = states.shape[1]
    states = jnp.pad(states.reshape(-1), (0, -states.size % (8 * rows))).reshape(-1, rows)
    states_rows = states.shape[0]
    smalls = jnp.concatenate([states, locals_flat.reshape(-1, rows)], axis=0)
    smalls = smalls + to_dp(smalls)
    glu_more = halve(glu_half, steps[1], back)
    in_more = halve(in_half, steps[1], back)
    backs.append(spread(back).reshape(band, count))
    last_step = steps[min(2, len(steps) - 1)]
    last_halves = [halves_of(v, last_step) for v in (in_more, glu_more)]
    smalls = jnp.broadcast_to(smalls, (groups, *smalls.shape))
    hidden = tie(hidden, output_send, back, smalls, *[v[1] for v in last_halves])
    output_keep = contract(hidden, columns_own, 1, 0)
    output = to_chan(output_send) + (
        output_keep + jnp.concatenate(resids, axis=0) + ffn_out_bias
    )
    smalls = spread(tie(smalls, backs[1], output))
    last_got = [to_seq(tie(v[1], backs[1], output), last_step) for v in last_halves]
    turned = tie(jnp.concatenate([v.reshape(band, count) for v in unit_turned], axis=0), backs[0])
    sums = [
        jnp.stack([jnp.sum(v, axis=0), jnp.sum(v * turned[i * band : (i + 1) * band], axis=0)])
        for i, v in enumerate(backs)
    ]
    sums = sum(sums).reshape(-1, rows)
    token_sums = (sums + to_chan(sums)).reshape(2, count)

    states = smalls[:, :states_rows].reshape(groups, -1)[:, : part * columns]
    states = states.reshape(groups, bands, share, columns).swapaxes(0, 1).reshape(channels, columns)
    states = tie(states.T, smalls).T
    locals_flat = jnp.sum(smalls[:, states_rows:], axis=0).reshape(-1)
    norm_rows = jnp.concatenate(
        [mean.reshape(1, count), scale1.reshape(1, count), token_sums, jnp.zeros((4, count), jnp.float32)],
        axis=0,
    )
    grad_inputs = first_norm_back(flat, grad_resid, norm_rows, backs, ())
    grad_ffn_out = finish(out_most, 3).T
    in_last, glu_last = [v[0] + tie(got, states, locals_flat) for v, got in zip(last_halves, last_got)]
    grad_ffn_in = finish(in_last, 3)
    grad_glu = finish(glu_last, 3)
    c = channels
    return (
        output.reshape(sequences, rows, channels),
        grad_inputs.reshape(sequences, rows, channels),
        states[:, 4 * modes_count],
        states[:, 4 * modes_count + 1],
        states[:, 4 * modes_count + 3],
        states[:, :modes_count],
        states[:, modes_count : 2 * modes_count],
        jnp.stack(
            [
                states[:, 2 * modes_count : 3 * modes_count],
                states[:, 3 * modes_count : 4 * modes_count],
            ]
        ),
        states[:, 4 * modes_count + 2],
        grad_glu.reshape(-1, 2, channels),
        locals_flat[: 2 * c].reshape(2, c),
        locals_flat[2 * c : 3 * c],
        locals_flat[3 * c : 4 * c],
        grad_ffn_in,
        locals_flat[5 * c :],
        grad_ffn_out,
        locals_flat[4 * c : 5 * c],
    )


def solution(mesh):
    placed = (
        P("dp", "seq", "chan"),
        P("dp", "seq", "chan"),
        P("chan"),
        P("chan"),
        P("chan"),
        P("chan", None),
        P("chan", None),
        P(None, "chan", None),
        P("chan"),
        P(None, None, "chan"),
        P(None, "chan"),
        P("chan"),
        P("chan"),
        P(None, "chan"),
        P("chan"),
        P("chan", None),
        P("chan"),
    )
    return jax.shard_map(
        body,
        mesh=mesh,
        in_specs=placed,
        out_specs=(
            P("dp", "seq", "chan"),
            P("dp", "seq", "chan"),
            P("chan"),
            P("chan"),
            P("chan"),
            P("chan", None),
            P("chan", None),
            P(None, "chan", None),
            P("chan"),
            P(("dp", "seq"), None, "chan"),
            P(None, "chan"),
            P("chan"),
            P("chan"),
            P(("dp", "seq"), "chan"),
            P("chan"),
            P("chan", ("dp", "seq")),
            P("chan"),
        ),
        check_vma=False,
    )
```

```python
from functools import partial

import jax
import jax.numpy as jnp
from jax import lax
from jax.experimental import pallas as pl
from jax.experimental.pallas import tpu as pltpu
from jax.sharding import PartitionSpec as P

epsilon = 1e-05
high = lax.Precision.HIGH
highest = lax.Precision.HIGHEST
swap = [(0, 1), (1, 0)]
anywhere = pl.BlockSpec(memory_space=pl.ANY)
window = 120


def tie(values, *earlier):
    def kernel(*refs):
        pass

    return pl.pallas_call(
        kernel,
        in_specs=[anywhere] * (1 + len(earlier)),
        out_specs=anywhere,
        out_shape=jax.ShapeDtypeStruct(values.shape, values.dtype),
        input_output_aliases={0: 0},
        name="tie",
    )(values, *earlier)


def split(values):
    first = values.astype(jnp.bfloat16)
    return (first, (values - first.astype(jnp.float32)).astype(jnp.bfloat16))


def dot(left, right):
    return jnp.dot(left, right, preferred_element_type=jnp.float32)


def contract(left, right, left_dim, right_dim):
    return lax.dot_general(
        left,
        right,
        (((left_dim,), (right_dim,)), ((), ())),
        precision=high,
        preferred_element_type=jnp.float32,
    )


def state_modes(log_step, decay_log, freq, out_coef):
    step = jnp.exp(log_step)[:, None]
    real_rate = -jnp.exp(decay_log)
    scaled_real = step * real_rate
    scaled_imag = step * freq
    minus_real = (
        jnp.expm1(scaled_real) * jnp.cos(scaled_imag) - 2.0 * jnp.sin(0.5 * scaled_imag) ** 2
    )
    minus_imag = jnp.exp(scaled_real) * jnp.sin(scaled_imag)
    modulus = real_rate * real_rate + freq * freq
    ratio_real = (minus_real * real_rate + minus_imag * freq) / modulus
    ratio_imag = (minus_imag * real_rate - minus_real * freq) / modulus
    weight_real = out_coef[0] * ratio_real - out_coef[1] * ratio_imag
    weight_imag = out_coef[0] * ratio_imag + out_coef[1] * ratio_real
    return (weight_real, weight_imag, scaled_real, scaled_imag)


def powers(positions, scaled_real, scaled_imag):
    where = positions[None, None, :]
    magnitude = jnp.exp(where * scaled_real[:, :, None])
    angle = where * scaled_imag[:, :, None]
    return (magnitude * jnp.cos(angle), magnitude * jnp.sin(angle))


def split(values):
    first = values.astype(jnp.bfloat16)
    return (first, (values - first.astype(jnp.float32)).astype(jnp.bfloat16))

def dot(left, right):
    return jnp.dot(left, right, preferred_element_type=jnp.float32)

def toeplitz_pair(line_ref, channel, lag, before, keep, turn):
    size, rows = keep.shape
    out = []
    for step in range(2):
        line = line_ref[channel, pl.ds(lag + step, 1), :]
        now = pltpu.roll(jnp.broadcast_to(line, (size, rows)), turn, 1, stride=1, stride_axis=0)
        out.append(jnp.where(keep, now, before))
        before = now
    high, low = split(jnp.concatenate(out, axis=1))
    return (jnp.concatenate([high, high, low, jnp.zeros_like(low)], axis=0), before)


def half_blocks(values, left):
    size = values.shape[1] // 2
    high = values.astype(jnp.bfloat16).astype(jnp.float32)
    low = values - high
    high_turned, low_turned = pltpu.roll(high, size, 1), pltpu.roll(low, size, 1)
    first = jnp.concatenate([jnp.where(left, high, low_turned), high], axis=1)
    second = jnp.concatenate([jnp.where(left, high_turned, low), high_turned], axis=1)
    return jnp.concatenate([first, second], axis=0).astype(jnp.bfloat16)


def conv_kernel(unit_ref, kernel_ref, table_ref, *rest):
    mixed_ref, slope_ref = rest[-2:]
    groups, block, sequences, rows = unit_ref.shape
    count, half = groups * sequences, rows // 2
    keep = lax.broadcasted_iota(jnp.int32, (half, rows), 1) >= lax.broadcasted_iota(
        jnp.int32, (half, rows), 0
    )
    left = lax.broadcasted_iota(jnp.int32, (count, rows), 1) < half

    def one(channel, carry):
        unit = unit_ref[:, channel].reshape(count, rows)
        gain = table_ref[channel, 0:1, :]
        bias = table_ref[channel, 1:2, :]
        skip = table_ref[channel, 2:3, :]
        normed = unit * gain + bias
        signal = half_blocks(normed, left)
        before = jnp.zeros((half, rows), jnp.float32)
        even, odd = [0.0] * groups, [0.0] * groups
        for lag in range(0, groups, 2):
            table, before = toeplitz_pair(kernel_ref, channel, lag, before, keep, 0)
            part = dot(signal, table)
            for step in range(2):
                lanes = slice(step * rows, (step + 1) * rows)
                for group in range(groups - lag - step):
                    at, to = group * sequences, group + lag + step
                    even[to] += part[at : at + sequences, lanes]
                    odd[to] += part[count + at : count + at + sequences, lanes]
        turned = pltpu.roll(jnp.concatenate(odd, axis=0), half, 1)
        late = jnp.concatenate(
            [jnp.zeros((sequences, rows), jnp.float32), turned[: count - sequences]], axis=0
        )
        inner = (
            jnp.concatenate(even, axis=0) + jnp.where(left, late, turned) + skip * normed
        )
        below = 0.5 + 0.5 * lax.erf(inner * 0.7071067811865476)
        density = 0.3989422804014327 * jnp.exp(-0.5 * inner * inner)
        mixed_ref[:, channel] = (inner * below).reshape(groups, sequences, rows)
        slope_ref[:, channel] = (below + inner * density).reshape(groups, sequences, rows)
        return carry

    lax.fori_loop(0, block, one, 0, unroll=block)


def conv_back_kernel(spans, unit_ref, slope_ref, kernel_ref, table_ref, *rest):
    grad_refs = rest[:spans]
    back_ref, lags_ref, sums_ref, cross_ref = rest[-4:]
    groups, block, sequences, rows = unit_ref.shape
    count, half = groups * sequences, rows // 2
    keep = (
        lax.broadcasted_iota(jnp.int32, (half, rows), 1)
        <= lax.broadcasted_iota(jnp.int32, (half, rows), 0) + half
    )
    left = lax.broadcasted_iota(jnp.int32, (count, rows), 1) < half
    line_at = lax.broadcasted_iota(jnp.int32, (8, rows), 1)
    tile_row = lax.broadcasted_iota(jnp.int32, (8, rows), 0)

    def diagonals(channel, carry):
        lines = [None] * groups
        for tile in range(half // 8):
            turned = []
            for lag in range(groups):
                now = cross_ref[
                    channel,
                    lag // 2,
                    8 * tile : 8 * tile + 8,
                    (lag % 2) * rows : (lag % 2 + 1) * rows,
                ]
                turned.append(pltpu.roll(now, rows - 8 * tile, 1) if tile else now)
            turned.append(jnp.zeros((8, rows), jnp.float32))
            for lag in range(groups):
                now = turned[lag]
                if tile:
                    now = jnp.where(line_at < rows - 8 * tile, now, turned[lag + 1])
                lines[lag] = now if lines[lag] is None else lines[lag] + now
        lines.append(jnp.zeros((8, rows), jnp.float32))
        for lag in range(groups):
            line = lines[lag]
            for bit in (1, 2, 4):
                line = jnp.where(tile_row & bit != 0, pltpu.roll(line, rows - bit, 1), line)
            lines[lag] = line
        for lag in range(groups):
            line = jnp.where(line_at + tile_row < rows, lines[lag], lines[lag + 1])
            lags_ref[channel, lag : lag + 1, :] = jnp.sum(line, axis=0, keepdims=True)
        return carry

    def one(channel, carry):
        unit = unit_ref[:, channel].reshape(count, rows)
        gain = table_ref[channel, 0:1, :]
        bias = table_ref[channel, 1:2, :]
        skip = table_ref[channel, 2:3, :]
        normed = unit * gain + bias
        grad = jnp.concatenate([ref[:, 0, channel] for ref in grad_refs], axis=1)
        grad = (grad * slope_ref[:, channel]).reshape(count, rows)
        nothing = jnp.zeros((sequences, rows), jnp.float32)
        signal = half_blocks(grad, left)
        turned = pltpu.roll(grad, half, 1)
        between = jnp.where(
            left, turned, jnp.concatenate([turned[sequences:], nothing], axis=0)
        )
        sides = jnp.concatenate([normed, pltpu.roll(normed, half, 1)], axis=0)
        sides, sides_low = split(sides.T[:half])
        sides = jnp.concatenate([sides, sides_low, sides], axis=1)
        before = jnp.zeros((half, rows), jnp.float32)
        even, odd = [0.0] * groups, [0.0] * groups
        for lag in range(0, groups, 2):
            table, before = toeplitz_pair(kernel_ref, channel, lag, before, keep, half)
            part = dot(signal, table)
            moved = []
            for step in range(2):
                lanes = slice(step * rows, (step + 1) * rows)
                shift = (lag + step) * sequences
                for group in range(groups - lag - step):
                    at = group * sequences + shift
                    even[group] += part[at : at + sequences, lanes]
                    odd[group] += part[count + at : count + at + sequences, lanes]
                pad = [jnp.zeros((shift, rows), jnp.float32)] if shift else []
                moved.append(
                    jnp.concatenate([grad[shift:], *pad, between[shift:], *pad], axis=0)
                )
            right, right_low = split(jnp.concatenate(moved, axis=1))
            cross_ref[channel, lag // 2] = dot(
                sides, jnp.concatenate([right, right, right_low], axis=0)
            )
        turned = pltpu.roll(jnp.concatenate(even, axis=0), half, 1)
        early = jnp.concatenate([turned[sequences:], nothing], axis=0)
        total = jnp.concatenate(odd, axis=0) + jnp.where(left, turned, early) + skip * grad
        back_ref[:, channel] = (total * gain).reshape(groups, sequences, rows)
        sums_ref[channel, 0:1, :] = jnp.sum(total * unit, axis=0, keepdims=True)
        sums_ref[channel, 1:2, :] = jnp.sum(total, axis=0, keepdims=True)
        sums_ref[channel, 2:3, :] = jnp.sum(grad * normed, axis=0, keepdims=True)
        sums_ref[channel, 3:8, :] = jnp.zeros((5, rows), jnp.float32)
        return carry

    lax.fori_loop(0, block, one, 0, unroll=min(4, block))
    lax.fori_loop(0, block, diagonals, 0, unroll=min(2, block))


def channel_blocks(groups, part):
    block = max(1, 64 // groups)
    return block if part % block == 0 else 1


def long_conv(unit, kernel, table, tokens):
    groups, part, sequences, rows = unit.shape
    block = channel_blocks(groups, part)
    wide = pl.BlockSpec((groups, block, sequences, rows), lambda i: (0, i, 0, 0))
    return pl.pallas_call(
        conv_kernel,
        grid=(part // block,),
        in_specs=[
            wide,
            pl.BlockSpec((block, groups, rows), lambda i: (i, 0, 0)),
            pl.BlockSpec((block, 8, rows), lambda i: (i, 0, 0)),
        ]
        + [anywhere] * len(tokens),
        out_specs=[wide, wide],
        out_shape=[jax.ShapeDtypeStruct(unit.shape, jnp.float32)] * 2,
        compiler_params=pltpu.CompilerParams(vmem_limit_bytes=48 * 1024 * 1024),
        cost_estimate=pl.CostEstimate(
            flops=part * groups * groups * sequences * rows * rows * 6 * window,
            bytes_accessed=12 * unit.size,
            transcendentals=2 * unit.size,
        ),
        name="conv_forward",
    )(unit, kernel, table, *tokens)

def long_conv_back(unit, slope, grads, band, kernel, table, tokens):
    groups, part, sequences, rows = unit.shape
    block = channel_blocks(groups, part)
    wide = pl.BlockSpec((groups, block, sequences, rows), lambda i: (0, i, 0, 0))
    lags = pl.BlockSpec((block, groups, rows), lambda i: (i, 0, 0))
    few = pl.BlockSpec((block, 8, rows), lambda i: (i, 0, 0))
    return pl.pallas_call(
        partial(conv_back_kernel, len(grads)),
        grid=(part // block,),
        in_specs=[wide, wide, lags, few]
        + [pl.BlockSpec((groups, 1, block, *v.shape[3:]), lambda i: (0, band, i, 0, 0)) for v in grads]
        + [anywhere] * len(tokens),
        out_specs=[wide, lags, few],
        out_shape=[
            jax.ShapeDtypeStruct(unit.shape, jnp.float32),
            jax.ShapeDtypeStruct(kernel.shape, jnp.float32),
            jax.ShapeDtypeStruct((part, 8, rows), jnp.float32),
        ],
        scratch_shapes=[pltpu.VMEM((block, groups // 2, rows // 2, 2 * rows), jnp.float32)],
        compiler_params=pltpu.CompilerParams(vmem_limit_bytes=48 * 1024 * 1024),
        cost_estimate=pl.CostEstimate(
            flops=part * groups * groups * sequences * rows * rows * 12 * window,
            bytes_accessed=16 * unit.size,
            transcendentals=0,
        ),
        name="conv_backward",
    )(unit, slope, kernel, table, *grads, *tokens)


def turned_dot(left, right):
    return lax.dot_general(
        left, right, (((1,), (1,)), ((), ())), preferred_element_type=jnp.float32
    )


def feed_forward_kernel(
    index_ref, resid_ref, other_ref, norm_ref, weight_ref, line_ref, back_ref, *rest
):
    (
        hidden_ref,
        grad_ref,
        keep_ref,
        send_ref,
        unit_ref,
        kept_ref,
        sums_ref,
        bias_ref,
        sent_ref,
        high_ref,
        low_ref,
        total_ref,
    ) = rest[-12:]
    count, channels = resid_ref.shape
    step = pl.program_id(0)
    own_at = pl.ds(pl.multiple_of(index_ref[0] * channels, channels), channels)
    other_at = pl.ds(pl.multiple_of((1 - index_ref[0]) * channels, channels), channels)

    @pl.when(step == 0)
    def _():
        resid, other = resid_ref[...], other_ref[...]
        width = 2.0 * channels
        mean = (
            jnp.sum(resid, axis=1, keepdims=True) + jnp.sum(other, axis=1, keepdims=True)
        ) / width
        squares = jnp.sum(resid * resid, axis=1, keepdims=True) + jnp.sum(
            other * other, axis=1, keepdims=True
        )
        scale = lax.rsqrt(squares / width - mean * mean + epsilon)
        lane = lax.broadcasted_iota(jnp.int32, (count, 128), 1)
        sums_ref[...] = jnp.where(lane == 2, scale, 0.0)
        total_ref[...] = jnp.zeros(total_ref.shape, jnp.float32)
        unit = (resid - mean) * scale
        unit_ref[...] = unit
        same = index_ref[1] == 1
        for values, at, first in (
            (unit, own_at, same),
            ((other - mean) * scale, other_at, jnp.logical_not(same)),
        ):
            normed = values * norm_ref[0:1, at] + norm_ref[1:2, at]
            high, low = split(normed)
            high_ref[:, at] = high
            low_ref[:, at] = low

            @pl.when(first)
            def _():
                keep_ref[...] = normed.T

            @pl.when(jnp.logical_not(first))
            def _():
                send_ref[...] = normed.T

    weight, weight_low = split(weight_ref[...])
    size = weight.shape[1]
    total = jnp.zeros((8, size), jnp.float32)
    chunk = min(count, 256)
    for start in range(0, count, chunk):
        at = slice(start, start + chunk)
        high, low = high_ref[at], low_ref[at]
        pre = dot(high, weight) + dot(low, weight) + dot(high, weight_low) + line_ref[0:1]
        below = 0.5 + 0.5 * lax.erf(pre * 0.7071067811865476)
        density = 0.3989422804014327 * jnp.exp(-0.5 * pre * pre)
        hidden_ref[at] = pre * below
        grad = back_ref[at] * (below + pre * density)
        grad_ref[at] = grad
        total = total + jnp.sum(grad.reshape(chunk // 8, 8, size), axis=0)
        first = jnp.sum(grad * line_ref[1:2], axis=1, keepdims=True)
        second = jnp.sum(grad * (pre - line_ref[2:3]), axis=1, keepdims=True)
        lane = lax.broadcasted_iota(jnp.int32, (chunk, 128), 1)
        sums_ref[at] += jnp.where(lane == 0, first, jnp.where(lane == 1, second, 0.0))
        high, low = split(grad)
        total_ref[at] += (
            turned_dot(high, weight) + turned_dot(low, weight) + turned_dot(high, weight_low)
        )
    bias_ref[...] = total

    @pl.when(step == pl.num_programs(0) - 1)
    def _():
        kept_ref[...] = total_ref[:, own_at]
        sent_ref[:, :channels] = total_ref[:, other_at]
        sent_ref[:, channels:] = sums_ref[...]


def feed_forward(index, resid, other, norm, weight, lines, back, held, tokens, place, spans):
    count, channels = resid.shape
    width, hidden = weight.shape
    size = min(512, hidden)
    full = spans * count
    held = list(held)

    def whole(j, c):
        return (0, 0)

    wide = pl.BlockSpec((count, size), lambda j, c: (place, j))
    narrow = pl.BlockSpec((count, channels), whole)
    turned = pl.BlockSpec((channels, count), lambda j, c: (0, place))
    spot = pl.BlockSpec((count, channels), lambda j, c: (place, 0))
    return pl.pallas_call(
        feed_forward_kernel,
        grid_spec=pltpu.PrefetchScalarGridSpec(
            num_scalar_prefetch=1,
            grid=(hidden // size,),
            in_specs=[
                narrow,
                narrow,
                pl.BlockSpec((8, width), whole),
                pl.BlockSpec((width, size), lambda j, c: (0, j)),
                pl.BlockSpec((8, size), lambda j, c: (0, j)),
                wide,
            ]
            + [anywhere] * (len(held) + len(tokens)),
            out_specs=[
                wide,
                wide,
                turned,
                turned,
                spot,
                spot,
                pl.BlockSpec((count, 128), whole),
                pl.BlockSpec((8, size), lambda j, c: (0, j)),
                pl.BlockSpec((count, channels + 128), whole),
            ],
            scratch_shapes=[
                pltpu.VMEM((count, width), jnp.bfloat16),
                pltpu.VMEM((count, width), jnp.bfloat16),
                pltpu.VMEM((count, width), jnp.float32),
            ],
        ),
        out_shape=[
            jax.ShapeDtypeStruct(shape, jnp.float32)
            for shape in (
                (full, hidden),
                (full, hidden),
                (channels, full),
                (channels, full),
                (full, channels),
                (full, channels),
                (count, 128),
                (8, hidden),
                (count, channels + 128),
            )
        ],
        input_output_aliases={7 + i: i for i in range(len(held))},
        compiler_params=pltpu.CompilerParams(vmem_limit_bytes=56 * 1024 * 1024),
        cost_estimate=pl.CostEstimate(
            flops=count * width * hidden * 12 * window,
            bytes_accessed=4 * (width * hidden + 3 * count * hidden + 8 * count * channels),
            transcendentals=2 * count * hidden,
        ),
        name="feed_forward",
    )(index, resid, other, norm, weight, lines, back, *held, *tokens)


def weight_kernel(rows, turns, index_ref, keep_ref, send_ref, right_ref, *rest):
    high_ref, low_ref = rest[-2:]
    kept_ref, *sent_refs = rest[-3 - turns : -2]
    parts_of = max(1, turns // 2)
    size = keep_ref.shape[0]
    turn = pl.program_id(0)

    @pl.when(turn == 0)
    def _():
        for at, ref in ((0, send_ref), (size, keep_ref)):
            high, low = split(ref[...])
            high_ref[at : at + size] = high
            low_ref[at : at + size] = low

    right, right_low = split(right_ref[...])
    chunk = min(size, 256)

    def parts(at, place):
        for start in range(0, size, chunk):
            rows_at = slice(at + start, at + start + chunk)
            left, left_low = high_ref[rows_at], low_ref[rows_at]
            part = dot(left, right) + dot(left_low, right) + dot(left, right_low)
            for first in range(0, chunk, rows):
                block = (start + first) // rows
                place(block, part[first : first + rows])

    def keep(block, values):
        stays = (block % 2 == index_ref[2]).astype(jnp.int32)
        to = pl.multiple_of(stays * (size // 2) + block // 2 * rows, rows)
        kept_ref[pl.ds(to, rows)] = values

    parts(size, keep)
    for piece in range(turns):
        group, lane = piece // 2, piece % 2 * right.shape[1]

        def send(block, values):
            at = (pl.ds(block // 2 * rows, rows), pl.ds(lane, values.shape[1]))
            goes = block % 2 != index_ref[2]

            @pl.when(goes)
            def _():
                sent_refs[group][at] = values

            @pl.when(jnp.logical_not(goes))
            def _():
                sent_refs[parts_of + group][at] = values

        @pl.when(turn == piece)
        def _():
            parts(0, send)


def weight_grad(index, groups, keep, send, right, tokens):
    size, depth = keep.shape
    columns = right.shape[1]
    block = min(512, columns)
    turns = columns // block
    whole = pl.BlockSpec((size, depth), lambda j, c: (0, 0))
    kept, *sent = pl.pallas_call(
        partial(weight_kernel, size // groups, turns),
        grid_spec=pltpu.PrefetchScalarGridSpec(
            num_scalar_prefetch=1,
            grid=(turns,),
            in_specs=[whole, whole, pl.BlockSpec((depth, block), lambda j, c: (0, j))]
            + [anywhere] * len(tokens),
            out_specs=[pl.BlockSpec((size, block), lambda j, c: (0, j))]
            + [pl.BlockSpec((size // 2, 2 * block), lambda j, c: (0, 0))] * turns,
            scratch_shapes=[pltpu.VMEM((2 * size, depth), jnp.bfloat16)] * 2,
        ),
        out_shape=[jax.ShapeDtypeStruct((size, columns), jnp.float32)]
        + [jax.ShapeDtypeStruct((size // 2, 2 * block), jnp.float32)] * turns,
        compiler_params=pltpu.CompilerParams(vmem_limit_bytes=56 * 1024 * 1024),
        cost_estimate=pl.CostEstimate(
            flops=12 * window * size * depth * columns,
            bytes_accessed=4 * (2 * size * depth + depth * columns + 2 * size * columns),
            transcendentals=0,
        ),
        name="weight_gradient",
    )(index, keep, send, right, *tokens)
    return (kept, sent)


def glu_back_kernel(spans, index_ref, keep_ref, unit_ref, norm_ref, grad_ref, weight_ref, *rest):
    by_span = [rest[i * spans : (i + 1) * spans] for i in range(4)]
    out = rest[-(7 + spans) :]
    resid_ref, both_ref, kept_ref, gain_ref, bias_ref = out[:5]
    sent_refs = out[5 : 5 + spans]
    high_ref, low_ref = out[5 + spans :]
    full, channels = keep_ref.shape
    count = full // spans
    width = 2.0 * channels

    @pl.when(pl.program_id(0) == 0)
    def _():
        chunk = min(count, 128)
        gains = jnp.zeros((8, channels), jnp.float32)
        biases, value_sums, gate_sums, grad_sums = gains, gains, gains, gains

        def fold(values):
            return jnp.sum(values.reshape(chunk // 8, 8, channels), axis=0)

        for start in range(0, full, chunk):
            at = slice(start, start + chunk)
            span, local = start // count, slice(start % count, start % count + chunk)
            other, own_sums, value, gate = [refs[span][local] for refs in by_span]
            grad_normed = keep_ref[at] + other[:, :channels]
            sums = own_sums + other[:, channels:]
            total, along, scale = sums[:, 0:1], sums[:, 1:2], own_sums[:, 2:3]
            unit = unit_ref[at]
            grad_resid = grad_ref[at] + scale * (
                grad_normed * norm_ref[0:1] - total / width - unit * (along / width)
            )
            resid_ref[at] = grad_resid
            grad_value = grad_resid * gate
            grad_gate = grad_value * value * (1.0 - gate)
            gains = gains + fold(grad_normed * unit)
            biases = biases + fold(grad_normed)
            value_sums = value_sums + fold(grad_value)
            gate_sums = gate_sums + fold(grad_gate)
            grad_sums = grad_sums + fold(grad_ref[at])
            for first, values in ((0, grad_value), (channels, grad_gate)):
                lanes = slice(first, first + channels)
                both_ref[at, lanes] = values
                high, low = split(values)
                high_ref[at, lanes] = high
                low_ref[at, lanes] = low
        gain_ref[:, :channels] = gains
        gain_ref[:, channels : 2 * channels] = biases
        gain_ref[:, 2 * channels :] = grad_sums
        bias_ref[:, :channels] = value_sums
        bias_ref[:, channels:] = gate_sums

    weight, weight_low = split(weight_ref[...])
    sending = pl.program_id(0) < pl.num_programs(0) // 2
    for span in range(spans):
        at = slice(span * count, (span + 1) * count)
        high = high_ref[at]
        mixed = (
            turned_dot(weight, high) + turned_dot(weight, low_ref[at]) + turned_dot(weight_low, high)
        )

        @pl.when(sending)
        def _():
            sent_refs[span][...] = mixed

        @pl.when(jnp.logical_not(sending))
        def _():
            kept_ref[:, at] = mixed


def glu_back(index, keep, unit, norm, grad, weight, others, sums, values, gates, tokens):
    full, channels = keep.shape
    width, columns = weight.shape
    spans = len(others)
    count = full // spans
    block = min(256, channels)
    turns = channels // block

    def whole(j, c):
        return (0, 0)

    def rows_at(j, c):
        return (jnp.where(j < turns, (1 - c[0]) * turns + j, (c[0] - 1) * turns + j), 0)

    wide = pl.BlockSpec((full, channels), whole)
    span_wide = pl.BlockSpec((count, channels), whole)
    span_few = pl.BlockSpec((count, 128), whole)
    few = pl.BlockSpec((8, columns), whole)
    return pl.pallas_call(
        partial(glu_back_kernel, spans),
        grid_spec=pltpu.PrefetchScalarGridSpec(
            num_scalar_prefetch=1,
            grid=(2 * turns,),
            in_specs=[wide, wide, pl.BlockSpec((8, channels), whole), wide]
            + [pl.BlockSpec((block, columns), rows_at)]
            + [pl.BlockSpec((count, channels + 128), whole)] * spans
            + ([span_few] * spans + [span_wide] * (2 * spans))
            + [anywhere] * len(tokens),
            out_specs=[
                wide,
                pl.BlockSpec((full, columns), whole),
                pl.BlockSpec((block, full), lambda j, c: (jnp.maximum(j - turns, 0), 0)),
                pl.BlockSpec((8, 3 * channels), whole),
                few,
            ]
            + [pl.BlockSpec((block, count), lambda j, c: (jnp.minimum(j, turns - 1), 0))] * spans,
            scratch_shapes=[pltpu.VMEM((full, columns), jnp.bfloat16)] * 2,
        ),
        out_shape=[
            jax.ShapeDtypeStruct(shape, jnp.float32)
            for shape in (
                (full, channels),
                (full, columns),
                (channels, full),
                (8, 3 * channels),
                (8, columns),
            )
            + ((channels, count),) * spans
        ],
        compiler_params=pltpu.CompilerParams(vmem_limit_bytes=60 * 1024 * 1024),
        cost_estimate=pl.CostEstimate(
            flops=6 * window * full * width * columns,
            bytes_accessed=4 * (11 * full * channels + width * columns),
            transcendentals=0,
        ),
        name="glu_backward",
    )(
        index,
        keep,
        unit,
        norm,
        grad,
        weight,
        *others,
        *sums,
        *values,
        *gates,
        *tokens,
    )


def first_norm_kernel(inputs_ref, resid_ref, rows_ref, *rest):
    out_ref = rest[-1]
    bands = len(rest) // 2
    channels = inputs_ref.shape[1]
    width = 2.0 * channels
    columns = rows_ref[...].T
    mean, scale, total, along = [columns[:, i : i + 1] for i in range(4)]
    for band in range(bands):
        scaled = rest[band][...].T
        lanes = slice(band * scaled.shape[1], (band + 1) * scaled.shape[1])
        unit = (inputs_ref[:, lanes] - mean) * scale
        out_ref[:, lanes] = resid_ref[:, lanes] + scale * (
            scaled - total / width - unit * (along / width)
        )


def first_norm_back(inputs, resid, rows, backs, tokens):
    count, channels = inputs.shape
    block = min(256, count)
    wide = pl.BlockSpec((block, channels), lambda j: (j, 0))
    bands = [pl.BlockSpec((v.shape[0], block), lambda j: (0, j)) for v in backs]
    tokens = list(tokens) + [backs[0]] * (len(backs) - len(tokens))
    return pl.pallas_call(
        first_norm_kernel,
        grid=(count // block,),
        in_specs=[wide, wide, pl.BlockSpec((8, block), lambda j: (0, j))]
        + bands
        + [anywhere] * len(tokens),
        out_specs=wide,
        out_shape=jax.ShapeDtypeStruct((count, channels), jnp.float32),
        compiler_params=pltpu.CompilerParams(vmem_limit_bytes=32 * 1024 * 1024),
        name="first_norm_backward",
    )(inputs, resid, rows, *backs, *tokens)


def body(
    inputs,
    cotangent,
    norm1_gain,
    norm1_bias,
    log_step,
    decay_log,
    freq,
    out_coef,
    skip,
    glu_weight,
    glu_bias,
    norm2_gain,
    norm2_bias,
    ffn_in,
    ffn_in_bias,
    ffn_out,
    ffn_out_bias,
):
    sequences, rows, channels = inputs.shape
    groups = lax.axis_size("seq")
    seq_index = lax.axis_index("seq")
    chan_index = lax.axis_index("chan")
    dp_index = lax.axis_index("dp")
    width = channels * lax.axis_size("chan")
    count = sequences * rows
    part = channels // groups
    steps = [1 << bit for bit in range(groups.bit_length() - 1)]
    bands = 2
    band = channels // bands
    share = part // bands
    spans = 2
    span = count // spans
    spots = [slice(i * span, (i + 1) * span) for i in range(spans)]

    def to_chan(values):
        return lax.ppermute(values, "chan", swap)

    def to_seq(values, step):
        return lax.ppermute(values, "seq", [(a, a ^ step) for a in range(groups)])

    def spread(values):
        return lax.all_to_all(values, "seq", 0, 0, tiled=True)

    def own_part(values, dim):
        pieces = [
            lax.dynamic_slice_in_dim(values, i * band + seq_index * share, share, dim)
            for i in range(bands)
        ]
        return jnp.concatenate(pieces, axis=dim)

    def in_order(own, other):
        first = chan_index == 0
        return jnp.concatenate(
            [jnp.where(first, own, other), jnp.where(first, other, own)], axis=1
        )

    def halve(values, step, *earlier):
        pairs = values.reshape(-1, 2, *values.shape[1:])
        mine = (seq_index & step) // step
        keep = lax.dynamic_index_in_dim(pairs, mine, 1, keepdims=False)
        send = lax.dynamic_index_in_dim(pairs, 1 - mine, 1, keepdims=False)
        got = to_seq(send, step)
        return keep + (tie(got, *earlier) if earlier else got)

    def finish(values, start, *earlier):
        for step in steps[start:]:
            values = halve(values, step, *earlier)
        return values[0]

    def halves_of(values, step):
        pairs = values.reshape(-1, 2, *values.shape[1:])
        mine = (seq_index & step) // step
        return [lax.dynamic_index_in_dim(pairs, at, 1, keepdims=False) for at in (mine, 1 - mine)]

    own_at = chan_index * channels
    other_at = channels - own_at

    flat = inputs.reshape(count, channels)
    grad_out = cotangent.reshape(count, channels)
    stats = jnp.concatenate([jnp.sum(inputs, axis=2), jnp.sum(inputs * inputs, axis=2)], axis=0)
    stats = lax.psum(stats, "chan")
    mean = stats[:sequences] / width
    scale1 = lax.rsqrt(stats[sequences:] / width - mean * mean + epsilon).reshape(count, 1)
    unit1 = (flat - mean.reshape(count, 1)) * scale1
    grad_out_other = to_chan(tie(grad_out, stats))
    same = chan_index == dp_index
    index = jnp.stack([chan_index, same.astype(jnp.int32), seq_index & 1]).astype(jnp.int32)

    def kept_and_sent(own, other):
        return (jnp.where(same, own, other), jnp.where(same, other, own))

    columns_own = lax.dynamic_slice_in_dim(ffn_out, own_at, channels, 1)
    columns_other = lax.dynamic_slice_in_dim(ffn_out, other_at, channels, 1)
    grad_hidden = contract(grad_out, columns_own, 1, 1)
    grad_hidden_own = grad_hidden
    grad_hidden = grad_hidden + contract(grad_out_other, columns_other, 1, 1)
    norms = jnp.stack([norm2_gain, norm2_bias] + [jnp.zeros((channels,), jnp.float32)] * 6)
    norms = in_order(norms, to_chan(tie(norms, grad_out_other)))
    lines = jnp.dot(norms, ffn_in, precision=highest, preferred_element_type=jnp.float32)
    lines = jnp.stack(
        [ffn_in_bias, lines[0], ffn_in_bias + lines[1]] + [jnp.zeros_like(ffn_in_bias)] * 5
    )

    modes, modes_back = jax.vjp(
        state_modes,
        own_part(log_step, 0),
        own_part(decay_log, 0),
        own_part(freq, 0),
        own_part(out_coef, 1),
    )
    weight_real, weight_imag, scaled_real, scaled_imag = modes
    fine_at = jnp.arange(rows, dtype=jnp.int32).astype(jnp.float32)
    coarse_at = (jnp.arange(groups, dtype=jnp.int32) * rows).astype(jnp.float32)
    fine_real, fine_imag = powers(fine_at, scaled_real, scaled_imag)
    coarse_real, coarse_imag = powers(coarse_at, scaled_real, scaled_imag)
    fine = jnp.concatenate([fine_real, fine_imag], axis=1)
    start_real = weight_real[:, :, None] * coarse_real - weight_imag[:, :, None] * coarse_imag
    start_imag = weight_real[:, :, None] * coarse_imag + weight_imag[:, :, None] * coarse_real
    kernel = 2.0 * jnp.einsum(
        "hnd,hnb->hdb",
        jnp.concatenate([start_real, -start_imag], axis=1),
        fine,
        precision=highest,
        preferred_element_type=jnp.float32,
    )
    table = jnp.stack(
        [own_part(norm1_gain, 0), own_part(norm1_bias, 0), own_part(skip, 0)]
        + [jnp.zeros((part,), jnp.float32)] * 5,
        axis=1,
    )
    table = jnp.broadcast_to(table[:, :, None], (part, 8, rows))
    kernel_turned = jnp.roll(kernel[:, :, ::-1], 1, axis=2)
    kernels_turned = [kernel_turned[i * share : (i + 1) * share] for i in range(bands)]
    kernels = [kernel[i * share : (i + 1) * share] for i in range(bands)]
    tables = [table[i * share : (i + 1) * share] for i in range(bands)]

    unit_parts, unit_turned, slope_parts, mixed, mixed_other = [], [], [], [], []
    for i in range(bands):
        turned = unit1[:, i * band : (i + 1) * band].T.reshape(groups, share, sequences, rows)
        unit_turned.append(turned)
        unit_parts.append(spread(tie(turned, kernel, grad_hidden_own) if i else turned))
    for i in range(bands):
        tokens = (grad_hidden, lines) if i else ()
        mixed_part, slope_part = long_conv(unit_parts[i], kernels[i], tables[i], tokens)
        slope_parts.append(slope_part)
        arrived = spread(mixed_part).reshape(band, count)
        if i:
            arrived = tie(arrived, mixed_other[0])
        mixed.append(arrived)
        mixed_other.append(to_chan(arrived))

    glu_flat = glu_weight.reshape(width, 2 * channels)
    glu_own = lax.dynamic_slice_in_dim(glu_flat, own_at, channels, 0)
    glu_rows_other = lax.dynamic_slice_in_dim(glu_flat, other_at, channels, 0)
    both_held = glu_bias.reshape(1, 2 * channels)
    for i in range(bands):
        both_held = both_held + contract(mixed[i], glu_own[i * band : (i + 1) * band], 0, 0)
    for i in range(bands - 1):
        both_held = both_held + contract(mixed_other[i], glu_rows_other[i * band : (i + 1) * band], 0, 0)
    values, gates, resids, resids_other = [], [], [], []
    for at in spots:
        both = both_held[at] + contract(
            mixed_other[-1][:, at], glu_rows_other[(bands - 1) * band :], 0, 0
        )
        values.append(both[:, :channels])
        gates.append(jax.nn.sigmoid(both[:, channels:]))
        resids.append(flat[at] + values[-1] * gates[-1])
        resids_other.append(to_chan(resids[-1]))

    grad_out_turned = [v.T for v in kept_and_sent(grad_out, tie(grad_out_other, resids[1]))]
    mixed_pair = kept_and_sent(
        jnp.concatenate(mixed, axis=0), tie(jnp.concatenate(mixed_other, axis=0), resids[1])
    )
    held, tokens = (), (*grad_out_turned, *mixed_pair, *kernels_turned)
    row_sums, hidden_sums, sent = [], [], []
    for i in range(spans):
        *held, row_sum, hidden_sum, send = feed_forward(
            index, resids[i], resids_other[i], norms, ffn_in, lines, grad_hidden, held, tokens, i, spans
        )
        tokens = ()
        row_sums.append(row_sum)
        hidden_sums.append(hidden_sum)
        sent.append(send)
    hidden, grad_pre, normed_keep, normed_send, units, kept = held
    arrived = [to_chan(v) for v in sent]

    def to_dp(values):
        return lax.ppermute(values, "dp", swap)

    def ready(keep, others, groups_at):
        half, size = keep.shape[0] // 2, others[0].shape[1]
        total = jnp.concatenate([keep[:half, g * size : (g + 1) * size] + others[g] for g in groups_at], axis=1)
        return total.reshape(groups // 2, -1, total.shape[1])

    def joined(keep, others, got, groups_at):
        half, size = keep.shape[0] // 2, others[0].shape[1]
        stay = others[len(others) // 2 :]
        total = jnp.concatenate([keep[half:, g * size : (g + 1) * size] + stay[g] for g in groups_at], axis=1)
        return total.reshape(got.shape) + got

    out_keep, out_send = weight_grad(
        index, groups, *grad_out_turned, hidden, (sent[1], arrived[0])
    )
    out_other = [to_dp(v) for v in out_send]
    every = range(len(out_other) // 2)
    out_keep = tie(out_keep, arrived[1])
    out_ready = [ready(out_keep, out_other, [g]) for g in every]

    grad_resid, grad_both, mixed_kept, norm_sums, glu_sums, *mixed_sent = glu_back(
        index,
        kept,
        units,
        jnp.broadcast_to(norm2_gain, (8, channels)),
        grad_out,
        glu_flat,
        arrived,
        row_sums,
        values,
        gates,
        out_ready,
    )
    locals_flat = jnp.concatenate(
        [
            jnp.sum(glu_sums, axis=0),
            jnp.sum(norm_sums, axis=0),
            jnp.sum(sum(hidden_sums), axis=0),
        ]
    )
    out_got = [to_seq(v, steps[0]) for v in out_ready]
    out_stay = [tie(v, mixed_sent[1]) for v in out_other]
    out_first = joined(out_keep, out_stay, tie(out_got[0], mixed_sent[1]), [0])
    in_keep, in_send = weight_grad(
        index, groups, normed_keep, normed_send, grad_pre, (mixed_sent[1], out_first)
    )
    in_other = [to_dp(v) for v in in_send]

    few = sequences // spans
    spread_spans = []
    tokens = (in_send[0],)
    for i, at in enumerate(spots):
        total = mixed_kept[:, at] + tie(to_chan(mixed_sent[i]), *tokens)
        moved = total.reshape(bands, groups, share, few, rows).swapaxes(0, 1)
        spread_spans.append(spread(moved))
        if not i:
            out_second = joined(out_keep, out_stay, tie(out_got[1], moved), [1])
            in_keep = tie(in_keep, out_second)
            in_ready = ready(in_keep, in_other, every)
            glu_keep, glu_send = weight_grad(index, groups, *mixed_pair, grad_both, (in_ready,))
            glu_other = [to_dp(v) for v in glu_send]
            tokens = (glu_send[0], spread_spans[0])
    hidden = tie(hidden, out_keep, moved)
    output_send = contract(hidden, columns_other, 1, 0)
    glu_keep = tie(glu_keep, output_send)
    glu_other = [tie(v, output_send) for v in glu_other]
    glu_ready = ready(glu_keep, glu_other, [0])
    in_got = to_seq(in_ready, steps[0])
    out_half = jnp.concatenate([out_first, out_second], axis=2)
    out_more = halve(out_half, steps[1], output_send)
    in_half = joined(in_keep, in_other, tie(in_got, output_send), every)
    glu_got = to_seq(glu_ready, steps[0])
    grad_backs, backs, grad_kernels, conv_sums = [], [], [], []
    for i in range(bands):
        if i:
            before = grad_backs[0]
            out_most = halve(out_more, steps[2], before) if len(steps) > 2 else out_more
            glu_half = joined(glu_keep, glu_other, tie(glu_got, before), [0])
            tokens = (out_most, glu_half)
        else:
            tokens = (glu_ready, in_half, out_more)
        back, grad_kernel, conv_sum = long_conv_back(
            unit_parts[i], slope_parts[i], spread_spans, i, kernels_turned[i], tables[i], tokens
        )
        grad_backs.append(back)
        grad_kernels.append(grad_kernel)
        conv_sums.append(conv_sum)
    backs.append(spread(grad_backs[0]).reshape(band, count))

    back = tie(grad_backs[1], backs[0])
    grad_kernels[1] = tie(grad_kernels[1], back)
    grad_kernel = jnp.concatenate(grad_kernels, axis=0)
    pulled = jnp.einsum(
        "hdb,hnb->hnd",
        jnp.concatenate([grad_kernel, grad_kernel * fine_at], axis=1),
        fine,
        precision=highest,
        preferred_element_type=jnp.float32,
    )
    modes_count = freq.shape[1]
    flat_real, flat_imag = pulled[:, :modes_count, :groups], pulled[:, modes_count:, :groups]
    slant_real = pulled[:, :modes_count, groups:] + coarse_at * flat_real
    slant_imag = pulled[:, modes_count:, groups:] + coarse_at * flat_imag
    zero_real = jnp.sum(coarse_real * flat_real - coarse_imag * flat_imag, axis=2)
    zero_imag = jnp.sum(coarse_real * flat_imag + coarse_imag * flat_real, axis=2)
    one_real = jnp.sum(coarse_real * slant_real - coarse_imag * slant_imag, axis=2)
    one_imag = jnp.sum(coarse_real * slant_imag + coarse_imag * slant_real, axis=2)
    grad_step, grad_decay, grad_freq, grad_coef = modes_back(
        (
            2.0 * zero_real,
            -2.0 * zero_imag,
            2.0 * (weight_real * one_real - weight_imag * one_imag),
            -2.0 * (weight_real * one_imag + weight_imag * one_real),
        )
    )
    sums = jnp.sum(jnp.concatenate(conv_sums, axis=0), axis=2)
    states = jnp.concatenate(
        [grad_decay, grad_freq, grad_coef[0], grad_coef[1], sums[:, :3], grad_step[:, None]], axis=1
    )
    columns = states.shape[1]
    states = jnp.pad(states.reshape(-1), (0, -states.size % (8 * rows))).reshape(-1, rows)
    states_rows = states.shape[0]
    smalls = jnp.concatenate([states, locals_flat.reshape(-1, rows)], axis=0)
    smalls = smalls + to_dp(smalls)
    glu_more = halve(glu_half, steps[1], back)
    in_more = halve(in_half, steps[1], back)
    backs.append(spread(back).reshape(band, count))
    last_step = steps[min(2, len(steps) - 1)]
    last_halves = [halves_of(v, last_step) for v in (in_more, glu_more)]
    smalls = jnp.broadcast_to(smalls, (groups, *smalls.shape))
    hidden = tie(hidden, output_send, back, smalls, *[v[1] for v in last_halves])
    output_keep = contract(hidden, columns_own, 1, 0)
    output = to_chan(output_send) + (
        output_keep + jnp.concatenate(resids, axis=0) + ffn_out_bias
    )
    smalls = spread(tie(smalls, backs[1], output))
    last_got = [to_seq(tie(v[1], backs[1], output), last_step) for v in last_halves]
    turned = tie(jnp.concatenate([v.reshape(band, count) for v in unit_turned], axis=0), backs[0])
    sums = [
        jnp.stack([jnp.sum(v, axis=0), jnp.sum(v * turned[i * band : (i + 1) * band], axis=0)])
        for i, v in enumerate(backs)
    ]
    sums = sum(sums).reshape(-1, rows)
    token_sums = (sums + to_chan(sums)).reshape(2, count)

    states = smalls[:, :states_rows].reshape(groups, -1)[:, : part * columns]
    states = states.reshape(groups, bands, share, columns).swapaxes(0, 1).reshape(channels, columns)
    states = tie(states.T, smalls).T
    locals_flat = jnp.sum(smalls[:, states_rows:], axis=0).reshape(-1)
    norm_rows = jnp.concatenate(
        [mean.reshape(1, count), scale1.reshape(1, count), token_sums, jnp.zeros((4, count), jnp.float32)],
        axis=0,
    )
    grad_inputs = first_norm_back(flat, grad_resid, norm_rows, backs, ())
    grad_ffn_out = finish(out_most, 3).T
    in_last, glu_last = [v[0] + tie(got, states, locals_flat) for v, got in zip(last_halves, last_got)]
    grad_ffn_in = finish(in_last, 3)
    grad_glu = finish(glu_last, 3)
    c = channels
    return (
        output.reshape(sequences, rows, channels),
        grad_inputs.reshape(sequences, rows, channels),
        states[:, 4 * modes_count],
        states[:, 4 * modes_count + 1],
        states[:, 4 * modes_count + 3],
        states[:, :modes_count],
        states[:, modes_count : 2 * modes_count],
        jnp.stack(
            [
                states[:, 2 * modes_count : 3 * modes_count],
                states[:, 3 * modes_count : 4 * modes_count],
            ]
        ),
        states[:, 4 * modes_count + 2],
        grad_glu.reshape(-1, 2, channels),
        locals_flat[: 2 * c].reshape(2, c),
        locals_flat[2 * c : 3 * c],
        locals_flat[3 * c : 4 * c],
        grad_ffn_in,
        locals_flat[5 * c :],
        grad_ffn_out,
        locals_flat[4 * c : 5 * c],
    )


def solution(mesh):
    placed = (
        P("dp", "seq", "chan"),
        P("dp", "seq", "chan"),
        P("chan"),
        P("chan"),
        P("chan"),
        P("chan", None),
        P("chan", None),
        P(None, "chan", None),
        P("chan"),
        P(None, None, "chan"),
        P(None, "chan"),
        P("chan"),
        P("chan"),
        P(None, "chan"),
        P("chan"),
        P("chan", None),
        P("chan"),
    )
    return jax.shard_map(
        body,
        mesh=mesh,
        in_specs=placed,
        out_specs=(
            P("dp", "seq", "chan"),
            P("dp", "seq", "chan"),
            P("chan"),
            P("chan"),
            P("chan"),
            P("chan", None),
            P("chan", None),
            P(None, "chan", None),
            P("chan"),
            P(("dp", "seq"), None, "chan"),
            P(None, "chan"),
            P("chan"),
            P("chan"),
            P(("dp", "seq"), "chan"),
            P("chan"),
            P("chan", ("dp", "seq")),
            P("chan"),
        ),
        check_vma=False,
    )
```

```python
from functools import partial

import jax
import jax.numpy as jnp
from jax import lax
from jax.experimental import pallas as pl
from jax.experimental.pallas import tpu as pltpu
from jax.sharding import PartitionSpec as P

epsilon = 1e-05
high = lax.Precision.HIGH
highest = lax.Precision.HIGHEST
swap = [(0, 1), (1, 0)]
anywhere = pl.BlockSpec(memory_space=pl.ANY)
window = 120


def tie(values, *earlier):
    def kernel(*refs):
        pass

    return pl.pallas_call(
        kernel,
        in_specs=[anywhere] * (1 + len(earlier)),
        out_specs=anywhere,
        out_shape=jax.ShapeDtypeStruct(values.shape, values.dtype),
        input_output_aliases={0: 0},
        name="tie",
    )(values, *earlier)


def split(values):
    first = values.astype(jnp.bfloat16)
    return (first, (values - first.astype(jnp.float32)).astype(jnp.bfloat16))


def dot(left, right):
    return jnp.dot(left, right, preferred_element_type=jnp.float32)


def contract(left, right, left_dim, right_dim):
    return lax.dot_general(
        left,
        right,
        (((left_dim,), (right_dim,)), ((), ())),
        precision=high,
        preferred_element_type=jnp.float32,
    )


def state_modes(log_step, decay_log, freq, out_coef):
    step = jnp.exp(log_step)[:, None]
    real_rate = -jnp.exp(decay_log)
    scaled_real = step * real_rate
    scaled_imag = step * freq
    minus_real = (
        jnp.expm1(scaled_real) * jnp.cos(scaled_imag) - 2.0 * jnp.sin(0.5 * scaled_imag) ** 2
    )
    minus_imag = jnp.exp(scaled_real) * jnp.sin(scaled_imag)
    modulus = real_rate * real_rate + freq * freq
    ratio_real = (minus_real * real_rate + minus_imag * freq) / modulus
    ratio_imag = (minus_imag * real_rate - minus_real * freq) / modulus
    weight_real = out_coef[0] * ratio_real - out_coef[1] * ratio_imag
    weight_imag = out_coef[0] * ratio_imag + out_coef[1] * ratio_real
    return (weight_real, weight_imag, scaled_real, scaled_imag)


def powers(positions, scaled_real, scaled_imag):
    where = positions[None, None, :]
    magnitude = jnp.exp(where * scaled_real[:, :, None])
    angle = where * scaled_imag[:, :, None]
    return (magnitude * jnp.cos(angle), magnitude * jnp.sin(angle))


def split(values):
    first = values.astype(jnp.bfloat16)
    return (first, (values - first.astype(jnp.float32)).astype(jnp.bfloat16))

def dot(left, right):
    return jnp.dot(left, right, preferred_element_type=jnp.float32)

def toeplitz_pair(line_ref, channel, lag, before, keep, turn):
    size, rows = keep.shape
    out = []
    for step in range(2):
        line = line_ref[channel, pl.ds(lag + step, 1), :]
        now = pltpu.roll(jnp.broadcast_to(line, (size, rows)), turn, 1, stride=1, stride_axis=0)
        out.append(jnp.where(keep, now, before))
        before = now
    high, low = split(jnp.concatenate(out, axis=1))
    return (jnp.concatenate([high, high, low, jnp.zeros_like(low)], axis=0), before)


def half_blocks(values, left):
    size = values.shape[1] // 2
    high = values.astype(jnp.bfloat16).astype(jnp.float32)
    low = values - high
    high_turned, low_turned = pltpu.roll(high, size, 1), pltpu.roll(low, size, 1)
    first = jnp.concatenate([jnp.where(left, high, low_turned), high], axis=1)
    second = jnp.concatenate([jnp.where(left, high_turned, low), high_turned], axis=1)
    return jnp.concatenate([first, second], axis=0).astype(jnp.bfloat16)


def conv_kernel(unit_ref, kernel_ref, table_ref, *rest):
    mixed_ref, slope_ref = rest[-2:]
    groups, block, sequences, rows = unit_ref.shape
    count, half = groups * sequences, rows // 2
    keep = lax.broadcasted_iota(jnp.int32, (half, rows), 1) >= lax.broadcasted_iota(
        jnp.int32, (half, rows), 0
    )
    left = lax.broadcasted_iota(jnp.int32, (count, rows), 1) < half

    def one(channel, carry):
        unit = unit_ref[:, channel].reshape(count, rows)
        gain = table_ref[channel, 0:1, :]
        bias = table_ref[channel, 1:2, :]
        skip = table_ref[channel, 2:3, :]
        normed = unit * gain + bias
        signal = half_blocks(normed, left)
        before = jnp.zeros((half, rows), jnp.float32)
        even, odd = [0.0] * groups, [0.0] * groups
        for lag in range(0, groups, 2):
            table, before = toeplitz_pair(kernel_ref, channel, lag, before, keep, 0)
            part = dot(signal, table)
            for step in range(2):
                lanes = slice(step * rows, (step + 1) * rows)
                for group in range(groups - lag - step):
                    at, to = group * sequences, group + lag + step
                    even[to] += part[at : at + sequences, lanes]
                    odd[to] += part[count + at : count + at + sequences, lanes]
        turned = pltpu.roll(jnp.concatenate(odd, axis=0), half, 1)
        late = jnp.concatenate(
            [jnp.zeros((sequences, rows), jnp.float32), turned[: count - sequences]], axis=0
        )
        inner = (
            jnp.concatenate(even, axis=0) + jnp.where(left, late, turned) + skip * normed
        )
        below = 0.5 + 0.5 * lax.erf(inner * 0.7071067811865476)
        density = 0.3989422804014327 * jnp.exp(-0.5 * inner * inner)
        mixed_ref[:, channel] = (inner * below).reshape(groups, sequences, rows)
        slope_ref[:, channel] = (below + inner * density).reshape(groups, sequences, rows)
        return carry

    lax.fori_loop(0, block, one, 0, unroll=block)


def conv_back_kernel(spans, unit_ref, slope_ref, kernel_ref, table_ref, *rest):
    grad_refs = rest[:spans]
    back_ref, lags_ref, sums_ref, cross_ref = rest[-4:]
    groups, block, sequences, rows = unit_ref.shape
    count, half = groups * sequences, rows // 2
    keep = (
        lax.broadcasted_iota(jnp.int32, (half, rows), 1)
        <= lax.broadcasted_iota(jnp.int32, (half, rows), 0) + half
    )
    left = lax.broadcasted_iota(jnp.int32, (count, rows), 1) < half
    line_at = lax.broadcasted_iota(jnp.int32, (8, rows), 1)
    tile_row = lax.broadcasted_iota(jnp.int32, (8, rows), 0)

    def diagonals(channel, carry):
        lines = [None] * groups
        for tile in range(half // 8):
            turned = []
            for lag in range(groups):
                now = cross_ref[
                    channel,
                    lag // 2,
                    8 * tile : 8 * tile + 8,
                    (lag % 2) * rows : (lag % 2 + 1) * rows,
                ]
                turned.append(pltpu.roll(now, rows - 8 * tile, 1) if tile else now)
            turned.append(jnp.zeros((8, rows), jnp.float32))
            for lag in range(groups):
                now = turned[lag]
                if tile:
                    now = jnp.where(line_at < rows - 8 * tile, now, turned[lag + 1])
                lines[lag] = now if lines[lag] is None else lines[lag] + now
        lines.append(jnp.zeros((8, rows), jnp.float32))
        for lag in range(groups):
            line = lines[lag]
            for bit in (1, 2, 4):
                line = jnp.where(tile_row & bit != 0, pltpu.roll(line, rows - bit, 1), line)
            lines[lag] = line
        for lag in range(groups):
            line = jnp.where(line_at + tile_row < rows, lines[lag], lines[lag + 1])
            lags_ref[channel, lag : lag + 1, :] = jnp.sum(line, axis=0, keepdims=True)
        return carry

    def one(channel, carry):
        unit = unit_ref[:, channel].reshape(count, rows)
        gain = table_ref[channel, 0:1, :]
        bias = table_ref[channel, 1:2, :]
        skip = table_ref[channel, 2:3, :]
        normed = unit * gain + bias
        grad = jnp.concatenate([ref[:, 0, channel] for ref in grad_refs], axis=1)
        grad = (grad * slope_ref[:, channel]).reshape(count, rows)
        nothing = jnp.zeros((sequences, rows), jnp.float32)
        signal = half_blocks(grad, left)
        turned = pltpu.roll(grad, half, 1)
        between = jnp.where(
            left, turned, jnp.concatenate([turned[sequences:], nothing], axis=0)
        )
        sides = jnp.concatenate([normed, pltpu.roll(normed, half, 1)], axis=0)
        sides, sides_low = split(sides.T[:half])
        sides = jnp.concatenate([sides, sides_low, sides], axis=1)
        before = jnp.zeros((half, rows), jnp.float32)
        even, odd = [0.0] * groups, [0.0] * groups
        for lag in range(0, groups, 2):
            table, before = toeplitz_pair(kernel_ref, channel, lag, before, keep, half)
            part = dot(signal, table)
            moved = []
            for step in range(2):
                lanes = slice(step * rows, (step + 1) * rows)
                shift = (lag + step) * sequences
                for group in range(groups - lag - step):
                    at = group * sequences + shift
                    even[group] += part[at : at + sequences, lanes]
                    odd[group] += part[count + at : count + at + sequences, lanes]
                pad = [jnp.zeros((shift, rows), jnp.float32)] if shift else []
                moved.append(
                    jnp.concatenate([grad[shift:], *pad, between[shift:], *pad], axis=0)
                )
            right, right_low = split(jnp.concatenate(moved, axis=1))
            cross_ref[channel, lag // 2] = dot(
                sides, jnp.concatenate([right, right, right_low], axis=0)
            )
        turned = pltpu.roll(jnp.concatenate(even, axis=0), half, 1)
        early = jnp.concatenate([turned[sequences:], nothing], axis=0)
        total = jnp.concatenate(odd, axis=0) + jnp.where(left, turned, early) + skip * grad
        back_ref[:, channel] = (total * gain).reshape(groups, sequences, rows)
        sums_ref[channel, 0:1, :] = jnp.sum(total * unit, axis=0, keepdims=True)
        sums_ref[channel, 1:2, :] = jnp.sum(total, axis=0, keepdims=True)
        sums_ref[channel, 2:3, :] = jnp.sum(grad * normed, axis=0, keepdims=True)
        sums_ref[channel, 3:8, :] = jnp.zeros((5, rows), jnp.float32)
        return carry

    lax.fori_loop(0, block, one, 0, unroll=min(4, block))
    lax.fori_loop(0, block, diagonals, 0, unroll=min(2, block))


def channel_blocks(groups, part):
    block = max(1, 64 // groups)
    return block if part % block == 0 else 1


def long_conv(unit, kernel, table, tokens):
    groups, part, sequences, rows = unit.shape
    block = channel_blocks(groups, part)
    wide = pl.BlockSpec((groups, block, sequences, rows), lambda i: (0, i, 0, 0))
    return pl.pallas_call(
        conv_kernel,
        grid=(part // block,),
        in_specs=[
            wide,
            pl.BlockSpec((block, groups, rows), lambda i: (i, 0, 0)),
            pl.BlockSpec((block, 8, rows), lambda i: (i, 0, 0)),
        ]
        + [anywhere] * len(tokens),
        out_specs=[wide, wide],
        out_shape=[jax.ShapeDtypeStruct(unit.shape, jnp.float32)] * 2,
        compiler_params=pltpu.CompilerParams(vmem_limit_bytes=48 * 1024 * 1024),
        cost_estimate=pl.CostEstimate(
            flops=part * groups * groups * sequences * rows * rows * 6 * window,
            bytes_accessed=12 * unit.size,
            transcendentals=2 * unit.size,
        ),
        name="conv_forward",
    )(unit, kernel, table, *tokens)

def long_conv_back(unit, slope, grads, band, kernel, table, tokens):
    groups, part, sequences, rows = unit.shape
    block = channel_blocks(groups, part)
    wide = pl.BlockSpec((groups, block, sequences, rows), lambda i: (0, i, 0, 0))
    lags = pl.BlockSpec((block, groups, rows), lambda i: (i, 0, 0))
    few = pl.BlockSpec((block, 8, rows), lambda i: (i, 0, 0))
    return pl.pallas_call(
        partial(conv_back_kernel, len(grads)),
        grid=(part // block,),
        in_specs=[wide, wide, lags, few]
        + [pl.BlockSpec((groups, 1, block, *v.shape[3:]), lambda i: (0, band, i, 0, 0)) for v in grads]
        + [anywhere] * len(tokens),
        out_specs=[wide, lags, few],
        out_shape=[
            jax.ShapeDtypeStruct(unit.shape, jnp.float32),
            jax.ShapeDtypeStruct(kernel.shape, jnp.float32),
            jax.ShapeDtypeStruct((part, 8, rows), jnp.float32),
        ],
        scratch_shapes=[pltpu.VMEM((block, groups // 2, rows // 2, 2 * rows), jnp.float32)],
        compiler_params=pltpu.CompilerParams(vmem_limit_bytes=48 * 1024 * 1024),
        cost_estimate=pl.CostEstimate(
            flops=part * groups * groups * sequences * rows * rows * 12 * window,
            bytes_accessed=16 * unit.size,
            transcendentals=0,
        ),
        name="conv_backward",
    )(unit, slope, kernel, table, *grads, *tokens)


def turned_dot(left, right):
    return lax.dot_general(
        left, right, (((1,), (1,)), ((), ())), preferred_element_type=jnp.float32
    )


def feed_forward_kernel(
    index_ref, resid_ref, other_ref, norm_ref, weight_ref, line_ref, back_ref, *rest
):
    (
        hidden_ref,
        grad_ref,
        keep_ref,
        send_ref,
        unit_ref,
        kept_ref,
        sums_ref,
        bias_ref,
        sent_ref,
        high_ref,
        low_ref,
        total_ref,
    ) = rest[-12:]
    count, channels = resid_ref.shape
    step = pl.program_id(0)
    own_at = pl.ds(pl.multiple_of(index_ref[0] * channels, channels), channels)
    other_at = pl.ds(pl.multiple_of((1 - index_ref[0]) * channels, channels), channels)

    @pl.when(step == 0)
    def _():
        resid, other = resid_ref[...], other_ref[...]
        width = 2.0 * channels
        mean = (
            jnp.sum(resid, axis=1, keepdims=True) + jnp.sum(other, axis=1, keepdims=True)
        ) / width
        squares = jnp.sum(resid * resid, axis=1, keepdims=True) + jnp.sum(
            other * other, axis=1, keepdims=True
        )
        scale = lax.rsqrt(squares / width - mean * mean + epsilon)
        lane = lax.broadcasted_iota(jnp.int32, (count, 128), 1)
        sums_ref[...] = jnp.where(lane == 2, scale, 0.0)
        total_ref[...] = jnp.zeros(total_ref.shape, jnp.float32)
        unit = (resid - mean) * scale
        unit_ref[...] = unit
        same = index_ref[1] == 1
        for values, at, first in (
            (unit, own_at, same),
            ((other - mean) * scale, other_at, jnp.logical_not(same)),
        ):
            normed = values * norm_ref[0:1, at] + norm_ref[1:2, at]
            high, low = split(normed)
            high_ref[:, at] = high
            low_ref[:, at] = low

            @pl.when(first)
            def _():
                keep_ref[...] = normed.T

            @pl.when(jnp.logical_not(first))
            def _():
                send_ref[...] = normed.T

    weight, weight_low = split(weight_ref[...])
    size = weight.shape[1]
    total = jnp.zeros((8, size), jnp.float32)
    chunk = min(count, 512)
    for start in range(0, count, chunk):
        at = slice(start, start + chunk)
        high, low = high_ref[at], low_ref[at]
        pre = dot(high, weight) + dot(low, weight) + dot(high, weight_low) + line_ref[0:1]
        below = 0.5 + 0.5 * lax.erf(pre * 0.7071067811865476)
        density = 0.3989422804014327 * jnp.exp(-0.5 * pre * pre)
        hidden_ref[at] = pre * below
        grad = back_ref[at] * (below + pre * density)
        grad_ref[at] = grad
        total = total + jnp.sum(grad.reshape(chunk // 8, 8, size), axis=0)
        first = jnp.sum(grad * line_ref[1:2], axis=1, keepdims=True)
        second = jnp.sum(grad * (pre - line_ref[2:3]), axis=1, keepdims=True)
        lane = lax.broadcasted_iota(jnp.int32, (chunk, 128), 1)
        sums_ref[at] += jnp.where(lane == 0, first, jnp.where(lane == 1, second, 0.0))
        high, low = split(grad)
        total_ref[at] += (
            turned_dot(high, weight) + turned_dot(low, weight) + turned_dot(high, weight_low)
        )
    bias_ref[...] = total

    @pl.when(step == pl.num_programs(0) - 1)
    def _():
        kept_ref[...] = total_ref[:, own_at]
        sent_ref[:, :channels] = total_ref[:, other_at]
        sent_ref[:, channels:] = sums_ref[...]


def feed_forward(index, resid, other, norm, weight, lines, back, held, tokens, place, spans):
    count, channels = resid.shape
    width, hidden = weight.shape
    size = min(512, hidden)
    full = spans * count
    held = list(held)

    def whole(j, c):
        return (0, 0)

    wide = pl.BlockSpec((count, size), lambda j, c: (place, j))
    narrow = pl.BlockSpec((count, channels), whole)
    turned = pl.BlockSpec((channels, count), lambda j, c: (0, place))
    spot = pl.BlockSpec((count, channels), lambda j, c: (place, 0))
    return pl.pallas_call(
        feed_forward_kernel,
        grid_spec=pltpu.PrefetchScalarGridSpec(
            num_scalar_prefetch=1,
            grid=(hidden // size,),
            in_specs=[
                narrow,
                narrow,
                pl.BlockSpec((8, width), whole),
                pl.BlockSpec((width, size), lambda j, c: (0, j)),
                pl.BlockSpec((8, size), lambda j, c: (0, j)),
                wide,
            ]
            + [anywhere] * (len(held) + len(tokens)),
            out_specs=[
                wide,
                wide,
                turned,
                turned,
                spot,
                spot,
                pl.BlockSpec((count, 128), whole),
                pl.BlockSpec((8, size), lambda j, c: (0, j)),
                pl.BlockSpec((count, channels + 128), whole),
            ],
            scratch_shapes=[
                pltpu.VMEM((count, width), jnp.bfloat16),
                pltpu.VMEM((count, width), jnp.bfloat16),
                pltpu.VMEM((count, width), jnp.float32),
            ],
        ),
        out_shape=[
            jax.ShapeDtypeStruct(shape, jnp.float32)
            for shape in (
                (full, hidden),
                (full, hidden),
                (channels, full),
                (channels, full),
                (full, channels),
                (full, channels),
                (count, 128),
                (8, hidden),
                (count, channels + 128),
            )
        ],
        input_output_aliases={7 + i: i for i in range(len(held))},
        compiler_params=pltpu.CompilerParams(vmem_limit_bytes=56 * 1024 * 1024),
        cost_estimate=pl.CostEstimate(
            flops=count * width * hidden * 12 * window,
            bytes_accessed=4 * (width * hidden + 3 * count * hidden + 8 * count * channels),
            transcendentals=2 * count * hidden,
        ),
        name="feed_forward",
    )(index, resid, other, norm, weight, lines, back, *held, *tokens)


def weight_kernel(rows, turns, index_ref, keep_ref, send_ref, right_ref, *rest):
    high_ref, low_ref = rest[-2:]
    kept_ref, *sent_refs = rest[-3 - turns : -2]
    parts_of = max(1, turns // 2)
    size = keep_ref.shape[0]
    turn = pl.program_id(0)

    @pl.when(turn == 0)
    def _():
        for at, ref in ((0, send_ref), (size, keep_ref)):
            high, low = split(ref[...])
            high_ref[at : at + size] = high
            low_ref[at : at + size] = low

    right, right_low = split(right_ref[...])
    chunk = min(size, 256)

    def parts(at, place):
        for start in range(0, size, chunk):
            rows_at = slice(at + start, at + start + chunk)
            left, left_low = high_ref[rows_at], low_ref[rows_at]
            part = dot(left, right) + dot(left_low, right) + dot(left, right_low)
            for first in range(0, chunk, rows):
                block = (start + first) // rows
                place(block, part[first : first + rows])

    def keep(block, values):
        stays = (block % 2 == index_ref[2]).astype(jnp.int32)
        to = pl.multiple_of(stays * (size // 2) + block // 2 * rows, rows)
        kept_ref[pl.ds(to, rows)] = values

    parts(size, keep)
    for piece in range(turns):
        group, lane = piece // 2, piece % 2 * right.shape[1]

        def send(block, values):
            at = (pl.ds(block // 2 * rows, rows), pl.ds(lane, values.shape[1]))
            goes = block % 2 != index_ref[2]

            @pl.when(goes)
            def _():
                sent_refs[group][at] = values

            @pl.when(jnp.logical_not(goes))
            def _():
                sent_refs[parts_of + group][at] = values

        @pl.when(turn == piece)
        def _():
            parts(0, send)


def weight_grad(index, groups, keep, send, right, tokens):
    size, depth = keep.shape
    columns = right.shape[1]
    block = min(512, columns)
    turns = columns // block
    whole = pl.BlockSpec((size, depth), lambda j, c: (0, 0))
    kept, *sent = pl.pallas_call(
        partial(weight_kernel, size // groups, turns),
        grid_spec=pltpu.PrefetchScalarGridSpec(
            num_scalar_prefetch=1,
            grid=(turns,),
            in_specs=[whole, whole, pl.BlockSpec((depth, block), lambda j, c: (0, j))]
            + [anywhere] * len(tokens),
            out_specs=[pl.BlockSpec((size, block), lambda j, c: (0, j))]
            + [pl.BlockSpec((size // 2, 2 * block), lambda j, c: (0, 0))] * turns,
            scratch_shapes=[pltpu.VMEM((2 * size, depth), jnp.bfloat16)] * 2,
        ),
        out_shape=[jax.ShapeDtypeStruct((size, columns), jnp.float32)]
        + [jax.ShapeDtypeStruct((size // 2, 2 * block), jnp.float32)] * turns,
        compiler_params=pltpu.CompilerParams(vmem_limit_bytes=56 * 1024 * 1024),
        cost_estimate=pl.CostEstimate(
            flops=12 * window * size * depth * columns,
            bytes_accessed=4 * (2 * size * depth + depth * columns + 2 * size * columns),
            transcendentals=0,
        ),
        name="weight_gradient",
    )(index, keep, send, right, *tokens)
    return (kept, sent)


def glu_back_kernel(spans, index_ref, keep_ref, unit_ref, norm_ref, grad_ref, weight_ref, *rest):
    by_span = [rest[i * spans : (i + 1) * spans] for i in range(4)]
    out = rest[-(7 + spans) :]
    resid_ref, both_ref, kept_ref, gain_ref, bias_ref = out[:5]
    sent_refs = out[5 : 5 + spans]
    high_ref, low_ref = out[5 + spans :]
    full, channels = keep_ref.shape
    count = full // spans
    width = 2.0 * channels

    @pl.when(pl.program_id(0) == 0)
    def _():
        chunk = min(count, 128)
        gains = jnp.zeros((8, channels), jnp.float32)
        biases, value_sums, gate_sums, grad_sums = gains, gains, gains, gains

        def fold(values):
            return jnp.sum(values.reshape(chunk // 8, 8, channels), axis=0)

        for start in range(0, full, chunk):
            at = slice(start, start + chunk)
            span, local = start // count, slice(start % count, start % count + chunk)
            other, own_sums, value, gate = [refs[span][local] for refs in by_span]
            grad_normed = keep_ref[at] + other[:, :channels]
            sums = own_sums + other[:, channels:]
            total, along, scale = sums[:, 0:1], sums[:, 1:2], own_sums[:, 2:3]
            unit = unit_ref[at]
            grad_resid = grad_ref[at] + scale * (
                grad_normed * norm_ref[0:1] - total / width - unit * (along / width)
            )
            resid_ref[at] = grad_resid
            grad_value = grad_resid * gate
            grad_gate = grad_value * value * (1.0 - gate)
            gains = gains + fold(grad_normed * unit)
            biases = biases + fold(grad_normed)
            value_sums = value_sums + fold(grad_value)
            gate_sums = gate_sums + fold(grad_gate)
            grad_sums = grad_sums + fold(grad_ref[at])
            for first, values in ((0, grad_value), (channels, grad_gate)):
                lanes = slice(first, first + channels)
                both_ref[at, lanes] = values
                high, low = split(values)
                high_ref[at, lanes] = high
                low_ref[at, lanes] = low
        gain_ref[:, :channels] = gains
        gain_ref[:, channels : 2 * channels] = biases
        gain_ref[:, 2 * channels :] = grad_sums
        bias_ref[:, :channels] = value_sums
        bias_ref[:, channels:] = gate_sums

    weight, weight_low = split(weight_ref[...])
    sending = pl.program_id(0) < pl.num_programs(0) // 2
    for span in range(spans):
        at = slice(span * count, (span + 1) * count)
        high = high_ref[at]
        mixed = (
            turned_dot(weight, high) + turned_dot(weight, low_ref[at]) + turned_dot(weight_low, high)
        )

        @pl.when(sending)
        def _():
            sent_refs[span][...] = mixed

        @pl.when(jnp.logical_not(sending))
        def _():
            kept_ref[:, at] = mixed


def glu_back(index, keep, unit, norm, grad, weight, others, sums, values, gates, tokens):
    full, channels = keep.shape
    width, columns = weight.shape
    spans = len(others)
    count = full // spans
    block = min(256, channels)
    turns = channels // block

    def whole(j, c):
        return (0, 0)

    def rows_at(j, c):
        return (jnp.where(j < turns, (1 - c[0]) * turns + j, (c[0] - 1) * turns + j), 0)

    wide = pl.BlockSpec((full, channels), whole)
    span_wide = pl.BlockSpec((count, channels), whole)
    span_few = pl.BlockSpec((count, 128), whole)
    few = pl.BlockSpec((8, columns), whole)
    return pl.pallas_call(
        partial(glu_back_kernel, spans),
        grid_spec=pltpu.PrefetchScalarGridSpec(
            num_scalar_prefetch=1,
            grid=(2 * turns,),
            in_specs=[wide, wide, pl.BlockSpec((8, channels), whole), wide]
            + [pl.BlockSpec((block, columns), rows_at)]
            + [pl.BlockSpec((count, channels + 128), whole)] * spans
            + ([span_few] * spans + [span_wide] * (2 * spans))
            + [anywhere] * len(tokens),
            out_specs=[
                wide,
                pl.BlockSpec((full, columns), whole),
                pl.BlockSpec((block, full), lambda j, c: (jnp.maximum(j - turns, 0), 0)),
                pl.BlockSpec((8, 3 * channels), whole),
                few,
            ]
            + [pl.BlockSpec((block, count), lambda j, c: (jnp.minimum(j, turns - 1), 0))] * spans,
            scratch_shapes=[pltpu.VMEM((full, columns), jnp.bfloat16)] * 2,
        ),
        out_shape=[
            jax.ShapeDtypeStruct(shape, jnp.float32)
            for shape in (
                (full, channels),
                (full, columns),
                (channels, full),
                (8, 3 * channels),
                (8, columns),
            )
            + ((channels, count),) * spans
        ],
        compiler_params=pltpu.CompilerParams(vmem_limit_bytes=60 * 1024 * 1024),
        cost_estimate=pl.CostEstimate(
            flops=6 * window * full * width * columns,
            bytes_accessed=4 * (11 * full * channels + width * columns),
            transcendentals=0,
        ),
        name="glu_backward",
    )(
        index,
        keep,
        unit,
        norm,
        grad,
        weight,
        *others,
        *sums,
        *values,
        *gates,
        *tokens,
    )


def first_norm_kernel(inputs_ref, resid_ref, rows_ref, *rest):
    out_ref = rest[-1]
    bands = len(rest) // 2
    channels = inputs_ref.shape[1]
    width = 2.0 * channels
    columns = rows_ref[...].T
    mean, scale, total, along = [columns[:, i : i + 1] for i in range(4)]
    for band in range(bands):
        scaled = rest[band][...].T
        lanes = slice(band * scaled.shape[1], (band + 1) * scaled.shape[1])
        unit = (inputs_ref[:, lanes] - mean) * scale
        out_ref[:, lanes] = resid_ref[:, lanes] + scale * (
            scaled - total / width - unit * (along / width)
        )


def first_norm_back(inputs, resid, rows, backs, tokens):
    count, channels = inputs.shape
    block = min(256, count)
    wide = pl.BlockSpec((block, channels), lambda j: (j, 0))
    bands = [pl.BlockSpec((v.shape[0], block), lambda j: (0, j)) for v in backs]
    tokens = list(tokens) + [backs[0]] * (len(backs) - len(tokens))
    return pl.pallas_call(
        first_norm_kernel,
        grid=(count // block,),
        in_specs=[wide, wide, pl.BlockSpec((8, block), lambda j: (0, j))]
        + bands
        + [anywhere] * len(tokens),
        out_specs=wide,
        out_shape=jax.ShapeDtypeStruct((count, channels), jnp.float32),
        compiler_params=pltpu.CompilerParams(vmem_limit_bytes=32 * 1024 * 1024),
        name="first_norm_backward",
    )(inputs, resid, rows, *backs, *tokens)


def body(
    inputs,
    cotangent,
    norm1_gain,
    norm1_bias,
    log_step,
    decay_log,
    freq,
    out_coef,
    skip,
    glu_weight,
    glu_bias,
    norm2_gain,
    norm2_bias,
    ffn_in,
    ffn_in_bias,
    ffn_out,
    ffn_out_bias,
):
    sequences, rows, channels = inputs.shape
    groups = lax.axis_size("seq")
    seq_index = lax.axis_index("seq")
    chan_index = lax.axis_index("chan")
    dp_index = lax.axis_index("dp")
    width = channels * lax.axis_size("chan")
    count = sequences * rows
    part = channels // groups
    steps = [1 << bit for bit in range(groups.bit_length() - 1)]
    bands = 2
    band = channels // bands
    share = part // bands
    spans = 2
    span = count // spans
    spots = [slice(i * span, (i + 1) * span) for i in range(spans)]

    def to_chan(values):
        return lax.ppermute(values, "chan", swap)

    def to_seq(values, step):
        return lax.ppermute(values, "seq", [(a, a ^ step) for a in range(groups)])

    def spread(values):
        return lax.all_to_all(values, "seq", 0, 0, tiled=True)

    def own_part(values, dim):
        pieces = [
            lax.dynamic_slice_in_dim(values, i * band + seq_index * share, share, dim)
            for i in range(bands)
        ]
        return jnp.concatenate(pieces, axis=dim)

    def in_order(own, other):
        first = chan_index == 0
        return jnp.concatenate(
            [jnp.where(first, own, other), jnp.where(first, other, own)], axis=1
        )

    def halve(values, step, *earlier):
        pairs = values.reshape(-1, 2, *values.shape[1:])
        mine = (seq_index & step) // step
        keep = lax.dynamic_index_in_dim(pairs, mine, 1, keepdims=False)
        send = lax.dynamic_index_in_dim(pairs, 1 - mine, 1, keepdims=False)
        got = to_seq(send, step)
        return keep + (tie(got, *earlier) if earlier else got)

    def finish(values, start, *earlier):
        for step in steps[start:]:
            values = halve(values, step, *earlier)
        return values[0]

    def halves_of(values, step):
        pairs = values.reshape(-1, 2, *values.shape[1:])
        mine = (seq_index & step) // step
        return [lax.dynamic_index_in_dim(pairs, at, 1, keepdims=False) for at in (mine, 1 - mine)]

    own_at = chan_index * channels
    other_at = channels - own_at

    flat = inputs.reshape(count, channels)
    grad_out = cotangent.reshape(count, channels)
    stats = jnp.concatenate([jnp.sum(inputs, axis=2), jnp.sum(inputs * inputs, axis=2)], axis=0)
    stats = lax.psum(stats, "chan")
    mean = stats[:sequences] / width
    scale1 = lax.rsqrt(stats[sequences:] / width - mean * mean + epsilon).reshape(count, 1)
    unit1 = (flat - mean.reshape(count, 1)) * scale1
    grad_out_other = to_chan(tie(grad_out, stats))
    same = chan_index == dp_index
    index = jnp.stack([chan_index, same.astype(jnp.int32), seq_index & 1]).astype(jnp.int32)

    def kept_and_sent(own, other):
        return (jnp.where(same, own, other), jnp.where(same, other, own))

    columns_own = lax.dynamic_slice_in_dim(ffn_out, own_at, channels, 1)
    columns_other = lax.dynamic_slice_in_dim(ffn_out, other_at, channels, 1)
    grad_hidden = contract(grad_out, columns_own, 1, 1)
    grad_hidden_own = grad_hidden
    grad_hidden = grad_hidden + contract(grad_out_other, columns_other, 1, 1)
    norms = jnp.stack([norm2_gain, norm2_bias] + [jnp.zeros((channels,), jnp.float32)] * 6)
    norms = in_order(norms, to_chan(tie(norms, grad_out_other)))
    lines = jnp.dot(norms, ffn_in, precision=highest, preferred_element_type=jnp.float32)
    lines = jnp.stack(
        [ffn_in_bias, lines[0], ffn_in_bias + lines[1]] + [jnp.zeros_like(ffn_in_bias)] * 5
    )

    modes, modes_back = jax.vjp(
        state_modes,
        own_part(log_step, 0),
        own_part(decay_log, 0),
        own_part(freq, 0),
        own_part(out_coef, 1),
    )
    weight_real, weight_imag, scaled_real, scaled_imag = modes
    fine_at = jnp.arange(rows, dtype=jnp.int32).astype(jnp.float32)
    coarse_at = (jnp.arange(groups, dtype=jnp.int32) * rows).astype(jnp.float32)
    fine_real, fine_imag = powers(fine_at, scaled_real, scaled_imag)
    coarse_real, coarse_imag = powers(coarse_at, scaled_real, scaled_imag)
    fine = jnp.concatenate([fine_real, fine_imag], axis=1)
    start_real = weight_real[:, :, None] * coarse_real - weight_imag[:, :, None] * coarse_imag
    start_imag = weight_real[:, :, None] * coarse_imag + weight_imag[:, :, None] * coarse_real
    kernel = 2.0 * jnp.einsum(
        "hnd,hnb->hdb",
        jnp.concatenate([start_real, -start_imag], axis=1),
        fine,
        precision=highest,
        preferred_element_type=jnp.float32,
    )
    table = jnp.stack(
        [own_part(norm1_gain, 0), own_part(norm1_bias, 0), own_part(skip, 0)]
        + [jnp.zeros((part,), jnp.float32)] * 5,
        axis=1,
    )
    table = jnp.broadcast_to(table[:, :, None], (part, 8, rows))
    kernel_turned = jnp.roll(kernel[:, :, ::-1], 1, axis=2)
    kernels_turned = [kernel_turned[i * share : (i + 1) * share] for i in range(bands)]
    kernels = [kernel[i * share : (i + 1) * share] for i in range(bands)]
    tables = [table[i * share : (i + 1) * share] for i in range(bands)]

    unit_parts, unit_turned, slope_parts, mixed, mixed_other = [], [], [], [], []
    for i in range(bands):
        turned = unit1[:, i * band : (i + 1) * band].T.reshape(groups, share, sequences, rows)
        unit_turned.append(turned)
        unit_parts.append(spread(tie(turned, kernel, grad_hidden_own) if i else turned))
    for i in range(bands):
        tokens = (grad_hidden, lines) if i else ()
        mixed_part, slope_part = long_conv(unit_parts[i], kernels[i], tables[i], tokens)
        slope_parts.append(slope_part)
        arrived = spread(mixed_part).reshape(band, count)
        if i:
            arrived = tie(arrived, mixed_other[0])
        mixed.append(arrived)
        mixed_other.append(to_chan(arrived))

    glu_flat = glu_weight.reshape(width, 2 * channels)
    glu_own = lax.dynamic_slice_in_dim(glu_flat, own_at, channels, 0)
    glu_rows_other = lax.dynamic_slice_in_dim(glu_flat, other_at, channels, 0)
    both_held = glu_bias.reshape(1, 2 * channels)
    for i in range(bands):
        both_held = both_held + contract(mixed[i], glu_own[i * band : (i + 1) * band], 0, 0)
    for i in range(bands - 1):
        both_held = both_held + contract(mixed_other[i], glu_rows_other[i * band : (i + 1) * band], 0, 0)
    values, gates, resids, resids_other = [], [], [], []
    for at in spots:
        both = both_held[at] + contract(
            mixed_other[-1][:, at], glu_rows_other[(bands - 1) * band :], 0, 0
        )
        values.append(both[:, :channels])
        gates.append(jax.nn.sigmoid(both[:, channels:]))
        resids.append(flat[at] + values[-1] * gates[-1])
        resids_other.append(to_chan(resids[-1]))

    grad_out_turned = [v.T for v in kept_and_sent(grad_out, tie(grad_out_other, resids[1]))]
    mixed_pair = kept_and_sent(
        jnp.concatenate(mixed, axis=0), tie(jnp.concatenate(mixed_other, axis=0), resids[1])
    )
    held, tokens = (), (*grad_out_turned, *mixed_pair, *kernels_turned)
    row_sums, hidden_sums, sent = [], [], []
    for i in range(spans):
        *held, row_sum, hidden_sum, send = feed_forward(
            index, resids[i], resids_other[i], norms, ffn_in, lines, grad_hidden, held, tokens, i, spans
        )
        tokens = ()
        row_sums.append(row_sum)
        hidden_sums.append(hidden_sum)
        sent.append(send)
    hidden, grad_pre, normed_keep, normed_send, units, kept = held
    arrived = [to_chan(v) for v in sent]

    def to_dp(values):
        return lax.ppermute(values, "dp", swap)

    def ready(keep, others, groups_at):
        half, size = keep.shape[0] // 2, others[0].shape[1]
        total = jnp.concatenate([keep[:half, g * size : (g + 1) * size] + others[g] for g in groups_at], axis=1)
        return total.reshape(groups // 2, -1, total.shape[1])

    def joined(keep, others, got, groups_at):
        half, size = keep.shape[0] // 2, others[0].shape[1]
        stay = others[len(others) // 2 :]
        total = jnp.concatenate([keep[half:, g * size : (g + 1) * size] + stay[g] for g in groups_at], axis=1)
        return total.reshape(got.shape) + got

    out_keep, out_send = weight_grad(
        index, groups, *grad_out_turned, hidden, (sent[1], arrived[0])
    )
    out_other = [to_dp(v) for v in out_send]
    every = range(len(out_other) // 2)
    out_keep = tie(out_keep, arrived[1])
    out_ready = [ready(out_keep, out_other, [g]) for g in every]

    grad_resid, grad_both, mixed_kept, norm_sums, glu_sums, *mixed_sent = glu_back(
        index,
        kept,
        units,
        jnp.broadcast_to(norm2_gain, (8, channels)),
        grad_out,
        glu_flat,
        arrived,
        row_sums,
        values,
        gates,
        out_ready,
    )
    locals_flat = jnp.concatenate(
        [
            jnp.sum(glu_sums, axis=0),
            jnp.sum(norm_sums, axis=0),
            jnp.sum(sum(hidden_sums), axis=0),
        ]
    )
    out_got = [to_seq(v, steps[0]) for v in out_ready]
    out_stay = [tie(v, mixed_sent[1]) for v in out_other]
    out_first = joined(out_keep, out_stay, tie(out_got[0], mixed_sent[1]), [0])
    in_keep, in_send = weight_grad(
        index, groups, normed_keep, normed_send, grad_pre, (mixed_sent[1], out_first)
    )
    in_other = [to_dp(v) for v in in_send]

    few = sequences // spans
    spread_spans = []
    tokens = (in_send[0],)
    for i, at in enumerate(spots):
        total = mixed_kept[:, at] + tie(to_chan(mixed_sent[i]), *tokens)
        moved = total.reshape(bands, groups, share, few, rows).swapaxes(0, 1)
        spread_spans.append(spread(moved))
        if not i:
            out_second = joined(out_keep, out_stay, tie(out_got[1], moved), [1])
            in_keep = tie(in_keep, out_second)
            in_ready = ready(in_keep, in_other, every)
            glu_keep, glu_send = weight_grad(index, groups, *mixed_pair, grad_both, (in_ready,))
            glu_other = [to_dp(v) for v in glu_send]
            tokens = (glu_send[0], spread_spans[0])
    hidden = tie(hidden, out_keep, moved)
    output_send = contract(hidden, columns_other, 1, 0)
    glu_keep = tie(glu_keep, output_send)
    glu_other = [tie(v, output_send) for v in glu_other]
    glu_ready = ready(glu_keep, glu_other, [0])
    in_got = to_seq(in_ready, steps[0])
    out_half = jnp.concatenate([out_first, out_second], axis=2)
    out_more = halve(out_half, steps[1], output_send)
    in_stay = [tie(v, output_send) for v in in_other]
    in_half = joined(in_keep, in_stay, tie(in_got, output_send), every)
    glu_got = to_seq(glu_ready, steps[0])
    grad_backs, backs, grad_kernels, conv_sums = [], [], [], []
    for i in range(bands):
        if i:
            before = grad_backs[0]
            out_most = halve(out_more, steps[2], before) if len(steps) > 2 else out_more
            glu_half = joined(glu_keep, glu_other, tie(glu_got, before), [0])
            tokens = (out_most, glu_half)
        else:
            tokens = (glu_ready, in_half, out_more)
        back, grad_kernel, conv_sum = long_conv_back(
            unit_parts[i], slope_parts[i], spread_spans, i, kernels_turned[i], tables[i], tokens
        )
        grad_backs.append(back)
        grad_kernels.append(grad_kernel)
        conv_sums.append(conv_sum)
    backs.append(spread(grad_backs[0]).reshape(band, count))

    back = tie(grad_backs[1], backs[0])
    grad_kernels[1] = tie(grad_kernels[1], back)
    grad_kernel = jnp.concatenate(grad_kernels, axis=0)
    pulled = jnp.einsum(
        "hdb,hnb->hnd",
        jnp.concatenate([grad_kernel, grad_kernel * fine_at], axis=1),
        fine,
        precision=highest,
        preferred_element_type=jnp.float32,
    )
    modes_count = freq.shape[1]
    flat_real, flat_imag = pulled[:, :modes_count, :groups], pulled[:, modes_count:, :groups]
    slant_real = pulled[:, :modes_count, groups:] + coarse_at * flat_real
    slant_imag = pulled[:, modes_count:, groups:] + coarse_at * flat_imag
    zero_real = jnp.sum(coarse_real * flat_real - coarse_imag * flat_imag, axis=2)
    zero_imag = jnp.sum(coarse_real * flat_imag + coarse_imag * flat_real, axis=2)
    one_real = jnp.sum(coarse_real * slant_real - coarse_imag * slant_imag, axis=2)
    one_imag = jnp.sum(coarse_real * slant_imag + coarse_imag * slant_real, axis=2)
    grad_step, grad_decay, grad_freq, grad_coef = modes_back(
        (
            2.0 * zero_real,
            -2.0 * zero_imag,
            2.0 * (weight_real * one_real - weight_imag * one_imag),
            -2.0 * (weight_real * one_imag + weight_imag * one_real),
        )
    )
    sums = jnp.sum(jnp.concatenate(conv_sums, axis=0), axis=2)
    states = jnp.concatenate(
        [grad_decay, grad_freq, grad_coef[0], grad_coef[1], sums[:, :3], grad_step[:, None]], axis=1
    )
    columns = states.shape[1]
    states = jnp.pad(states.reshape(-1), (0, -states.size % (8 * rows))).reshape(-1, rows)
    states_rows = states.shape[0]
    smalls = jnp.concatenate([states, locals_flat.reshape(-1, rows)], axis=0)
    smalls = smalls + to_dp(smalls)
    glu_more = halve(glu_half, steps[1], back)
    in_more = halve(in_half, steps[1], back)
    backs.append(spread(back).reshape(band, count))
    last_step = steps[min(2, len(steps) - 1)]
    last_halves = [halves_of(v, last_step) for v in (in_more, glu_more)]
    smalls = jnp.broadcast_to(smalls, (groups, *smalls.shape))
    hidden = tie(hidden, output_send, back, smalls, *[v[1] for v in last_halves])
    output_keep = contract(hidden, columns_own, 1, 0)
    output = to_chan(output_send) + (
        output_keep + jnp.concatenate(resids, axis=0) + ffn_out_bias
    )
    smalls = spread(tie(smalls, backs[1], output))
    last_got = [to_seq(tie(v[1], backs[1], output), last_step) for v in last_halves]
    turned = tie(jnp.concatenate([v.reshape(band, count) for v in unit_turned], axis=0), backs[0])
    sums = [
        jnp.stack([jnp.sum(v, axis=0), jnp.sum(v * turned[i * band : (i + 1) * band], axis=0)])
        for i, v in enumerate(backs)
    ]
    sums = sum(sums).reshape(-1, rows)
    token_sums = (sums + to_chan(sums)).reshape(2, count)

    states = smalls[:, :states_rows].reshape(groups, -1)[:, : part * columns]
    states = states.reshape(groups, bands, share, columns).swapaxes(0, 1).reshape(channels, columns)
    states = tie(states.T, smalls).T
    locals_flat = jnp.sum(smalls[:, states_rows:], axis=0).reshape(-1)
    norm_rows = jnp.concatenate(
        [mean.reshape(1, count), scale1.reshape(1, count), token_sums, jnp.zeros((4, count), jnp.float32)],
        axis=0,
    )
    grad_inputs = first_norm_back(flat, grad_resid, norm_rows, backs, ())
    grad_ffn_out = finish(out_most, 3).T
    in_last, glu_last = [v[0] + tie(got, states, locals_flat) for v, got in zip(last_halves, last_got)]
    grad_ffn_in = finish(in_last, 3)
    grad_glu = finish(glu_last, 3)
    c = channels
    return (
        output.reshape(sequences, rows, channels),
        grad_inputs.reshape(sequences, rows, channels),
        states[:, 4 * modes_count],
        states[:, 4 * modes_count + 1],
        states[:, 4 * modes_count + 3],
        states[:, :modes_count],
        states[:, modes_count : 2 * modes_count],
        jnp.stack(
            [
                states[:, 2 * modes_count : 3 * modes_count],
                states[:, 3 * modes_count : 4 * modes_count],
            ]
        ),
        states[:, 4 * modes_count + 2],
        grad_glu.reshape(-1, 2, channels),
        locals_flat[: 2 * c].reshape(2, c),
        locals_flat[2 * c : 3 * c],
        locals_flat[3 * c : 4 * c],
        grad_ffn_in,
        locals_flat[5 * c :],
        grad_ffn_out,
        locals_flat[4 * c : 5 * c],
    )


def solution(mesh):
    placed = (
        P("dp", "seq", "chan"),
        P("dp", "seq", "chan"),
        P("chan"),
        P("chan"),
        P("chan"),
        P("chan", None),
        P("chan", None),
        P(None, "chan", None),
        P("chan"),
        P(None, None, "chan"),
        P(None, "chan"),
        P("chan"),
        P("chan"),
        P(None, "chan"),
        P("chan"),
        P("chan", None),
        P("chan"),
    )
    return jax.shard_map(
        body,
        mesh=mesh,
        in_specs=placed,
        out_specs=(
            P("dp", "seq", "chan"),
            P("dp", "seq", "chan"),
            P("chan"),
            P("chan"),
            P("chan"),
            P("chan", None),
            P("chan", None),
            P(None, "chan", None),
            P("chan"),
            P(("dp", "seq"), None, "chan"),
            P(None, "chan"),
            P("chan"),
            P("chan"),
            P(("dp", "seq"), "chan"),
            P("chan"),
            P("chan", ("dp", "seq")),
            P("chan"),
        ),
        check_vma=False,
    )
```
